128 devices in a mesh: ctx: 32 (over x, z, core), exp: 4 (over y).
Axes of the slice: x: 4, y: 4, z: 4, core: 2. Of those that a mesh axis runs over, the one named last changes fastest.
Arguments:
- tokens: bfloat16 [65536, 1280], P('ctx'), may hold values from -40 to 40
- slot_weight: bfloat16 [1280, 256], replicated, may hold values from -0.5 to 0.5
- w_in: bfloat16 [128, 1280, 2560], P(('ctx', 'exp')), may hold values from -0.15625 to 0.15625
- w_out: bfloat16 [128, 2560, 1280], P(('ctx', 'exp')), may hold values from -0.125 to 0.125
- cotangent: bfloat16 [65536, 1280], P(('ctx', 'exp')), may hold values from -24 to 24
Outputs:
- mixed_out: bfloat16 [65536, 1280], P(('ctx', 'exp'))
- token_grad: bfloat16 [65536, 1280], P(('ctx', 'exp'))
The draws below stay inside these ranges and needn't reach their ends.
All inputs are finite; a program needn't handle non-finite values.
Results may differ from the reference program's by a relative error of at most 0.034.
Values may be sent and summed in bfloat16 or wider, within the bound.
No kernel may reach another device: no remote copies, remote signals or barrier semaphores. Data moves between devices by JAX's collectives and lax.ppermute only.
A program may use at most 128 MiB of HBM per device.

```python
import jax
import jax.numpy as jnp
from jax import lax

D = 1280
F = 2560
TOK_DEV = 2048
TOKENS = 65536
EXPERTS = 128
SLOTS = 256
N_CTX = 32


def shared_slots(key):
    normal_draw = jax.random.normal(jax.random.fold_in(key, 7), (D, SLOTS), jnp.float32)
    return jnp.clip(normal_draw * (6.0 / D) ** 0.5, -0.5, 0.5)


def draw_slot_weight(key, part):
    columns = shared_slots(key)
    return columns.astype(jnp.bfloat16)


def draw_tokens(key, part):
    key = jax.random.fold_in(key, 2)
    jitter_key = jax.random.fold_in(key, 0)
    return jnp.clip(jax.random.normal(jitter_key, (TOKENS, D), jnp.float32), -6.0, 6.0).astype(jnp.bfloat16)


def block_levels(own_key, extent, shards, low, high):
    factor_of, own = 1.0, jax.random.fold_in(own_key, 6)
    for axis_at, blocks in shards:
        heights = jnp.exp(jax.random.uniform(jax.random.fold_in(own, axis_at), (blocks,), jnp.float32, low / len(shards), high / len(shards)))
        factor_of = factor_of * jnp.repeat(heights, extent[axis_at] // blocks).reshape([-1 if axis == axis_at else 1 for axis in range(len(extent))])
    return factor_of


def normal_values(own_key, shape, scale, bound, cuts=(), dtype=jnp.bfloat16):
    array = scale * jax.random.normal(own_key, shape, jnp.float32)
    if cuts:
        array = array * block_levels(own_key, shape, cuts, -0.22, 0.18)
    return jnp.clip(array, -bound, bound).astype(dtype)


def setup_inputs(seed: int = 0) -> dict:
    arg_keys = jax.random.split(jax.random.key(seed), 6)
    return {
        "tokens": draw_tokens(jax.random.fold_in(arg_keys[5], 71), 0),
        "slot_weight": draw_slot_weight(jax.random.fold_in(arg_keys[5], 71), 0),
        "w_in": normal_values(arg_keys[2], (EXPERTS, D, F), D ** -0.5, 0.15625, ((0, 128),)),
        "w_out": normal_values(arg_keys[3], (EXPERTS, F, D), F ** -0.5, 0.125, ((0, 128),)),
        "cotangent": normal_values(arg_keys[4], (TOKENS, D), 4.0, 24.0, ((0, 128),)),
    }


def inner_rows(left_rows, right_rows):
    return lax.dot_general(left_rows, right_rows, (((1,), (1,)), ((), ())), preferred_element_type=jnp.float32)

def inner_cols(left_rows, right_rows):
    return lax.dot_general(left_rows, right_rows, (((0,), (0,)), ((), ())), preferred_element_type=jnp.float32)

def reference(tokens, slot_weight, w_in, w_out, cotangent):
    logits = jnp.dot(tokens, slot_weight, preferred_element_type=jnp.float32)
    blocks = logits.reshape(N_CTX, TOK_DEV, SLOTS)
    block_max = lax.optimization_barrier(jnp.max(blocks, axis=1))
    highest = lax.optimization_barrier(jnp.max(block_max, axis=0))
    shifted = jnp.exp(blocks - block_max[:, None, :])
    block_sum = lax.optimization_barrier(jnp.sum(shifted, axis=1))
    rescale = jnp.exp(block_max - highest[None, :])
    totals = lax.optimization_barrier(jnp.sum(rescale * block_sum, axis=0))
    token_blocks = tokens.reshape(N_CTX, TOK_DEV, D)

    def one_block(inputs):
        weights, rows = inputs
        return inner_cols(weights.astype(jnp.bfloat16), rows)
    partial_value = lax.map(one_block, (shifted, token_blocks))
    slot_exact = lax.optimization_barrier(jnp.sum(partial_value * rescale[:, :, None], axis=0)) / totals[:, None]
    slot_low = slot_exact.astype(jnp.bfloat16).reshape(EXPERTS, 2, D)

    def expert_forward(inputs):
        slot_rows, first, second = inputs
        preact = jnp.dot(slot_rows, first, preferred_element_type=jnp.float32)
        hidden = jax.nn.gelu(preact).astype(jnp.bfloat16)
        return (preact, jnp.dot(hidden, second, preferred_element_type=jnp.float32).astype(jnp.bfloat16))
    preact, slot_out = lax.map(expert_forward, (slot_low, w_in, w_out))
    slot_out = slot_out.reshape(SLOTS, D)
    combine = jax.nn.softmax(logits, axis=1)
    combine_low = combine.astype(jnp.bfloat16)
    mixed_out = jnp.dot(combine_low, slot_out, preferred_element_type=jnp.float32).astype(jnp.bfloat16)
    comb_grad = inner_rows(cotangent, slot_out)
    logit_comb = combine * (comb_grad - lax.optimization_barrier(jnp.sum(combine * comb_grad, axis=1, keepdims=True)))
    out_grad = inner_cols(combine_low, cotangent).astype(jnp.bfloat16).reshape(EXPERTS, 2, D)

    def expert_backward(inputs):
        grad_rows, preact_rows, first, second = inputs
        hid_grad = inner_rows(grad_rows, second)
        pullback = jax.vjp(jax.nn.gelu, preact_rows)[1]
        pre_grad = pullback(hid_grad)[0].astype(jnp.bfloat16)
        return inner_rows(pre_grad, first)
    in_grad = lax.map(expert_backward, (out_grad, preact, w_in, w_out)).reshape(SLOTS, D)
    slot_product = lax.optimization_barrier(jnp.sum(slot_exact * in_grad, axis=1))
    in_low = in_grad.astype(jnp.bfloat16)
    dispatch = jnp.exp(logits - highest[None, :]) / totals[None, :]
    dispatch_low = dispatch.astype(jnp.bfloat16)
    logit_disp = (dispatch * (inner_rows(tokens, in_low) - slot_product[None, :])).astype(jnp.bfloat16)
    token_grad = inner_rows(logit_disp, slot_weight) + jnp.dot(dispatch_low, in_low, preferred_element_type=jnp.float32)
    token_grad = token_grad + inner_rows(logit_comb.astype(jnp.bfloat16), slot_weight)
    return (mixed_out, token_grad.astype(jnp.bfloat16))
```

```python
import functools

import jax
import jax.numpy as jnp
from jax import lax
from jax.experimental import pallas as pl
from jax.experimental.pallas import tpu as pltpu
from jax.sharding import Mesh
from jax.sharding import PartitionSpec as P

LOW = jnp.bfloat16
WIDE = jnp.float32
EXTRA = 128
LIMIT = 40 * 1024 * 1024


def product(left, right, left_dim, right_dim):
    return lax.dot_general(
        left, right, (((left_dim,), (right_dim,)), ((), ())), preferred_element_type=WIDE
    )


def split3(value):
    high = value.astype(LOW).astype(WIDE)
    rest = value - high
    mid = rest.astype(LOW).astype(WIDE)
    return [high, mid, rest - mid]


def place(pieces, shape, axis):
    index = lax.broadcasted_iota(jnp.int32, shape, axis)
    total = jnp.zeros(shape, WIDE)
    for at, piece in enumerate(pieces):
        total = jnp.where(index == at, piece, total)
    return total


def lanes(block, first):
    index = lax.broadcasted_iota(jnp.int32, block.shape, 1)
    inside = (index >= first) & (index < first + 3)
    return jnp.sum(jnp.where(inside, block, 0.0), axis=1, keepdims=True)


def opening_kernel(at_ref, tok_ref, weight_ref, cot_ref, comb_ref, logit_ref, order_ref, *outs):
    slots = weight_ref.shape[1]
    half = slots // 2
    width = tok_ref.shape[1]
    core = at_ref[1]
    to = lax.broadcasted_iota(jnp.int32, (slots, slots), 1)
    source = lax.broadcasted_iota(jnp.int32, (slots, slots), 0)
    other = to // half
    within = to % half
    wanted = (within // 8) * 16 + jnp.where(other == 0, core, 1 - core) * 8 + within % 8
    order = (source == wanted).astype(WIDE).astype(LOW)
    weight = product(weight_ref[...], order, 1, 0).astype(LOW)
    order_ref[...] = weight
    rows = tok_ref[...]
    logits = product(rows, weight, 1, 0)
    logit_ref[...] = logits
    col_max = jnp.max(logits, axis=0, keepdims=True)
    shifted = jnp.exp(logits - col_max)
    col_sum = jnp.sum(shifted, axis=0, keepdims=True)
    slot_part = product(shifted.astype(LOW), rows, 0, 0)
    raised = jnp.exp(logits - jnp.max(logits, axis=1, keepdims=True))
    combine = raised / jnp.sum(raised, axis=1, keepdims=True)
    comb_ref[...] = combine
    grad_part = product(combine.astype(LOW), cot_ref[...], 0, 0)
    pieces = place(split3(col_max) + split3(col_sum), (EXTRA, slots), 0).T
    for at, out in enumerate(outs):
        part = slice(at * half, (at + 1) * half)
        out[:, :width] = slot_part[part].astype(LOW)
        out[:, width : 2 * width] = grad_part[part].astype(LOW)
        out[:, 2 * width :] = pieces[part].astype(LOW)


def opening(at, tokens, slot_weight, cotangent):
    rows, width = cotangent.shape
    slots = slot_weight.shape[1]
    wide = 2 * width + EXTRA
    whole = lambda shape: pl.BlockSpec(shape, lambda i, at: (0, 0))
    return pl.pallas_call(
        opening_kernel,
        grid_spec=pltpu.PrefetchScalarGridSpec(
            num_scalar_prefetch=1,
            grid=(1,),
            in_specs=[
                pl.BlockSpec((rows, width), lambda i, at: (at[0], 0)),
                whole((width, slots)),
                whole((rows, width)),
            ],
            out_specs=[
                whole((rows, slots)),
                whole((rows, slots)),
                whole((width, slots)),
                whole((slots // 2, wide)),
                whole((slots // 2, wide)),
            ],
        ),
        out_shape=[
            jax.ShapeDtypeStruct((rows, slots), WIDE),
            jax.ShapeDtypeStruct((rows, slots), WIDE),
            jax.ShapeDtypeStruct((width, slots), LOW),
            jax.ShapeDtypeStruct((slots // 2, wide), LOW),
            jax.ShapeDtypeStruct((slots // 2, wide), LOW),
        ],
        compiler_params=pltpu.CompilerParams(vmem_limit_bytes=LIMIT),
        name="opening",
    )(at, tokens, slot_weight, cotangent)


def merge_kernel(kept_ref, taken_ref, out_ref):
    width = (out_ref.shape[1] - EXTRA) // 2
    kept, taken = kept_ref[:, 2 * width :].astype(WIDE), taken_ref[:, 2 * width :].astype(WIDE)
    kept_max, taken_max = lanes(kept, 0), lanes(taken, 0)
    top = jnp.maximum(kept_max, taken_max)
    kept_scale, taken_scale = jnp.exp(kept_max - top), jnp.exp(taken_max - top)
    total = kept_scale * lanes(kept, 3) + taken_scale * lanes(taken, 3)
    out_ref[:, :width] = (
        kept_scale * kept_ref[:, :width].astype(WIDE)
        + taken_scale * taken_ref[:, :width].astype(WIDE)
    ).astype(LOW)
    out_ref[:, width : 2 * width] = (
        kept_ref[:, width : 2 * width].astype(WIDE) + taken_ref[:, width : 2 * width].astype(WIDE)
    ).astype(LOW)
    out_ref[:, 2 * width :] = place(split3(top) + split3(total), kept.shape, 1).astype(LOW)


def merge(kept, taken):
    return pl.pallas_call(
        merge_kernel,
        out_shape=jax.ShapeDtypeStruct(kept.shape, LOW),
        compiler_params=pltpu.CompilerParams(vmem_limit_bytes=LIMIT),
        name="merge",
    )(kept, taken)


PARTS = 4


def expert_kernel(got_ref, in_hbm, out_hbm, told_ref, w_in, w_out, in_sem, out_sem):
    width, hidden = w_in.shape
    in_rows, out_rows = width // PARTS, hidden // PARTS

    in_copies = [
        pltpu.make_async_copy(
            in_hbm.at[0, pl.ds(at * in_rows, in_rows)],
            w_in.at[pl.ds(at * in_rows, in_rows)],
            in_sem.at[at],
        )
        for at in range(PARTS)
    ]
    out_copies = [
        pltpu.make_async_copy(
            out_hbm.at[0, pl.ds(at * out_rows, out_rows)],
            w_out.at[pl.ds(at * out_rows, out_rows)],
            out_sem.at[at],
        )
        for at in range(PARTS)
    ]
    for copy in in_copies + out_copies:
        copy.start()
    pieces = got_ref[:, 2 * width :].astype(WIDE)
    count = pieces.shape[0]
    block_max, block_sum = lanes(pieces, 0), lanes(pieces, 3)
    odd = lax.broadcasted_iota(jnp.int32, (count, 1), 0) % 2 == 1
    lowest = jnp.full((count, 1), -jnp.inf, WIDE)
    top = [
        jnp.max(jnp.where(odd, lowest, block_max), axis=0, keepdims=True),
        jnp.max(jnp.where(odd, block_max, lowest), axis=0, keepdims=True),
    ]
    scale = jnp.exp(block_max - jnp.where(odd, top[1], top[0]))
    scaled_sum = scale * block_sum
    totals = [
        jnp.sum(jnp.where(odd, 0.0, scaled_sum), axis=0, keepdims=True),
        jnp.sum(jnp.where(odd, scaled_sum, 0.0), axis=0, keepdims=True),
    ]
    scaled = scale * got_ref[:, :width].astype(WIDE)
    exact = [
        jnp.sum(jnp.where(odd, 0.0, scaled), axis=0, keepdims=True) / totals[0],
        jnp.sum(jnp.where(odd, scaled, 0.0), axis=0, keepdims=True) / totals[1],
    ]
    sent = got_ref[:, width : 2 * width].astype(WIDE)
    grads = [
        jnp.sum(jnp.where(odd, 0.0, sent), axis=0, keepdims=True),
        jnp.sum(jnp.where(odd, sent, 0.0), axis=0, keepdims=True),
    ]
    exact = place(exact, (8, width), 0)
    out_grad = place(grads, (8, width), 0).astype(LOW)
    slot_low = exact.astype(LOW)
    preact = jnp.zeros((8, hidden), WIDE)
    for at in range(PARTS):
        in_copies[at].wait()
        part = slice(at * in_rows, (at + 1) * in_rows)
        preact += product(slot_low[:, part], w_in[part, :], 1, 0)
    rate = 0.7978845608028654
    square = preact * preact
    curve = jnp.tanh(rate * (preact + 0.044715 * square * preact))
    low_hidden = (0.5 * preact * (1.0 + curve)).astype(LOW)
    slope = 0.5 * (1.0 + curve) + 0.5 * preact * (1.0 - curve * curve) * rate * (
        1.0 + 3.0 * 0.044715 * square
    )
    slot_out = jnp.zeros((8, width), WIDE)
    in_grad = jnp.zeros((8, width), WIDE)
    for at in range(PARTS):
        out_copies[at].wait()
        part = slice(at * out_rows, (at + 1) * out_rows)
        slot_out += product(low_hidden[:, part], w_out[part, :], 1, 0)
        pre_grad = (slope[:, part] * product(out_grad, w_out[part, :], 1, 1)).astype(LOW)
        in_grad += product(pre_grad, w_in[:, part], 1, 1)
    told_ref[:, :width] = slot_out.astype(LOW)
    told_ref[:, width : 2 * width] = in_grad.astype(LOW)
    slot_product = jnp.sum(exact * in_grad, axis=1, keepdims=True)
    top = place(top, (8, 1), 0)
    totals = place(totals, (8, 1), 0)
    told_ref[:, 2 * width :] = place(
        split3(slot_product) + split3(top) + split3(totals), (8, EXTRA), 1
    ).astype(LOW)


def expert(got, w_in, w_out):
    width, hidden = w_in.shape[1:]
    return pl.pallas_call(
        expert_kernel,
        in_specs=[
            pl.BlockSpec(memory_space=pltpu.VMEM),
            pl.BlockSpec(memory_space=pl.ANY),
            pl.BlockSpec(memory_space=pl.ANY),
        ],
        out_specs=pl.BlockSpec(memory_space=pltpu.VMEM),
        out_shape=jax.ShapeDtypeStruct((8, 2 * width + EXTRA), LOW),
        scratch_shapes=[
            pltpu.VMEM((width, hidden), LOW),
            pltpu.VMEM((hidden, width), LOW),
            pltpu.SemaphoreType.DMA((PARTS,)),
            pltpu.SemaphoreType.DMA((PARTS,)),
        ],
        compiler_params=pltpu.CompilerParams(vmem_limit_bytes=LIMIT),
        name="expert",
    )(got, w_in, w_out)


def closing_kernel(
    at_ref, tok_ref, cot_ref, comb_ref, logit_ref, weight_ref, mine_ref, pair_ref,
    mixed_ref, grad_ref, all_out, in_low, rows_ref,
):
    width = tok_ref.shape[1]
    half = mine_ref.shape[0]

    @pl.when(pl.program_id(0) == 0)
    def _():
        for at, ref in enumerate((mine_ref, pair_ref)):
            part = slice(at * half, (at + 1) * half)
            all_out[part, :] = ref[:, :width]
            in_low[part, :] = ref[:, width : 2 * width]
            pieces = ref[:, 2 * width :].astype(WIDE).T
            for row in range(3):
                rows_ref[row : row + 1, part] = jnp.sum(
                    pieces[3 * row : 3 * row + 3], axis=0, keepdims=True
                )

    slot_product, highest, totals = rows_ref[0:1], rows_ref[1:2], rows_ref[2:3]
    combine = comb_ref[...]
    mixed_ref[...] = product(combine.astype(LOW), all_out[...], 1, 0).astype(LOW)
    comb_grad = product(cot_ref[...], all_out[...], 1, 1)
    logit_grad = combine * (comb_grad - jnp.sum(combine * comb_grad, axis=1, keepdims=True))
    dispatch = jnp.exp(logit_ref[...] - highest) / totals
    logit_grad += dispatch * (product(tok_ref[...], in_low[...], 1, 1) - slot_product)
    token_grad = product(logit_grad.astype(LOW), weight_ref[...], 1, 1)
    token_grad += product(dispatch.astype(LOW), in_low[...], 1, 0)
    grad_ref[...] = token_grad.astype(LOW)


def closing(at, tokens, cotangent, combine, logits, weight, mine, pair):
    rows, width = cotangent.shape
    slots = weight.shape[1]
    steps = 2
    block = rows // steps
    whole = lambda shape: pl.BlockSpec(shape, lambda i, at: (0, 0))
    tall = lambda cols: pl.BlockSpec((block, cols), lambda i, at: (i, 0))
    return pl.pallas_call(
        closing_kernel,
        grid_spec=pltpu.PrefetchScalarGridSpec(
            num_scalar_prefetch=1,
            grid=(steps,),
            in_specs=[
                pl.BlockSpec((block, width), lambda i, at: (at[0] * steps + i, 0)),
                tall(width),
                tall(slots),
                tall(slots),
                whole(weight.shape),
                whole(mine.shape),
                whole(pair.shape),
            ],
            out_specs=[tall(width), tall(width)],
            scratch_shapes=[
                pltpu.VMEM((slots, width), LOW),
                pltpu.VMEM((slots, width), LOW),
                pltpu.VMEM((8, slots), WIDE),
            ],
        ),
        out_shape=[jax.ShapeDtypeStruct((rows, width), LOW)] * 2,
        compiler_params=pltpu.CompilerParams(vmem_limit_bytes=LIMIT),
        name="closing",
    )(at, tokens, cotangent, combine, logits, weight, mine, pair)


def shards(tokens, slot_weight, w_in, w_out, cotangent):
    chips, cores, exp_count = lax.axis_size("chip"), lax.axis_size("core"), lax.axis_size("exp")
    peers = chips * exp_count
    swap = [(0, 1), (1, 0)]
    at = jnp.stack([lax.axis_index("exp"), lax.axis_index("core")]).astype(jnp.int32)
    slots = slot_weight.shape[1]
    half = slots // cores
    combine, logits, weight, kept, given = opening(at, tokens, slot_weight, cotangent)
    merged = merge(kept, lax.ppermute(given, "core", swap))
    sent = merged.reshape(peers, half // peers, -1)
    got = lax.all_to_all(sent, ("chip", "exp"), split_axis=0, concat_axis=0, tiled=True)
    told = expert(got.reshape(half, -1), w_in, w_out)[: half // peers]
    told = jnp.broadcast_to(told[None], (peers,) + told.shape)
    told = lax.all_to_all(told, ("chip", "exp"), split_axis=0, concat_axis=0, tiled=True)
    told = told.reshape(half, -1)
    pair = lax.ppermute(told, "core", swap)
    mixed_out, token_grad = closing(at, tokens, cotangent, combine, logits, weight, told, pair)
    return (mixed_out, token_grad)


def solution(mesh):
    ctx, exp = mesh.devices.shape
    finer = Mesh(mesh.devices.reshape(ctx // 2, 2, exp), ("chip", "core", "exp"))
    rows = P(("chip", "core", "exp"), None)
    experts = P(("chip", "core", "exp"), None, None)
    return jax.shard_map(
        shards,
        mesh=finer,
        in_specs=(P(("chip", "core"), None), P(), experts, experts, rows),
        out_specs=(rows, rows),
        check_vma=False,
    )
```

```python
import functools

import jax
import jax.numpy as jnp
from jax import lax
from jax.experimental import pallas as pl
from jax.experimental.pallas import tpu as pltpu
from jax.sharding import Mesh
from jax.sharding import PartitionSpec as P

LOW = jnp.bfloat16
WIDE = jnp.float32
EXTRA = 128
LIMIT = 20 * 1024 * 1024


def product(left, right, left_dim, right_dim):
    return lax.dot_general(
        left, right, (((left_dim,), (right_dim,)), ((), ())), preferred_element_type=WIDE
    )


def split3(value):
    high = value.astype(LOW).astype(WIDE)
    rest = value - high
    mid = rest.astype(LOW).astype(WIDE)
    return [high, mid, rest - mid]


def place(pieces, shape, axis):
    index = lax.broadcasted_iota(jnp.int32, shape, axis)
    total = jnp.zeros(shape, WIDE)
    for at, piece in enumerate(pieces):
        total = jnp.where(index == at, piece, total)
    return total


def lanes(block, first):
    index = lax.broadcasted_iota(jnp.int32, block.shape, 1)
    inside = (index >= first) & (index < first + 3)
    return jnp.sum(jnp.where(inside, block, 0.0), axis=1, keepdims=True)


IN_SMEM = pl.BlockSpec(memory_space=pltpu.SMEM)
IN_VMEM = pl.BlockSpec(memory_space=pltpu.VMEM)
IN_HBM = pl.BlockSpec(memory_space=pltpu.HBM)


def stay(array):
    return pltpu.with_memory_space_constraint(array, pltpu.HBM)


def call(kernel, name, args, specs, out_specs, out_shape, scratch=()):
    return pl.pallas_call(
        kernel,
        in_specs=specs,
        out_specs=out_specs,
        out_shape=out_shape,
        scratch_shapes=scratch,
        compiler_params=pltpu.CompilerParams(vmem_limit_bytes=LIMIT),
        name=name,
    )(*args)


def ordering(core, slots):
    to = lax.broadcasted_iota(jnp.int32, (slots, slots), 1)
    source = lax.broadcasted_iota(jnp.int32, (slots, slots), 0)
    half = slots // 2
    within = to % half
    other = jnp.where(to // half == 0, core, 1 - core)
    wanted = (within // 8) * 16 + other * 8 + within % 8
    return (source == wanted).astype(WIDE).astype(LOW)


def opening_kernel(
    at_ref, tok_hbm, weight_hbm, cot_hbm,
    kept_ref, given_ref, comb_ref, logit_ref, order_ref, rows_ref, cot_ref,
    weight_ref, sems,
):
    slots = weight_ref.shape[1]
    half = slots // 2
    count, width = rows_ref.shape
    start = pl.multiple_of(at_ref[0] * count, count)
    loads = [
        pltpu.make_async_copy(source, target, sems.at[at])
        for at, (source, target) in enumerate(
            (
                (weight_hbm, weight_ref),
                (tok_hbm.at[pl.ds(start, count)], rows_ref),
                (cot_hbm, cot_ref),
            )
        )
    ]
    for copy in loads:
        copy.start()
    order = ordering(at_ref[1], slots)
    loads[0].wait()
    weight = product(weight_ref[...], order, 1, 0).astype(LOW)
    order_ref[...] = weight
    loads[1].wait()
    rows = rows_ref[...]
    logits = product(rows, weight, 1, 0)
    logit_ref[...] = logits
    col_max = jnp.max(logits, axis=0, keepdims=True)
    shifted = jnp.exp(logits - col_max)
    col_sum = jnp.sum(shifted, axis=0, keepdims=True)
    slot_part = product(shifted.astype(LOW), rows, 0, 0)
    raised = jnp.exp(logits - jnp.max(logits, axis=1, keepdims=True))
    combine = raised / jnp.sum(raised, axis=1, keepdims=True)
    comb_ref[...] = combine
    loads[2].wait()
    grad_part = product(combine.astype(LOW), cot_ref[...], 0, 0)
    pieces = place(split3(col_max) + split3(col_sum), (EXTRA, slots), 0).T
    for at, out in enumerate((kept_ref, given_ref)):
        part = slice(at * half, (at + 1) * half)
        out[:, :width] = slot_part[part].astype(LOW)
        out[:, width : 2 * width] = grad_part[part].astype(LOW)
        out[:, 2 * width :] = pieces[part].astype(LOW)


def opening(at, tokens, slot_weight, cotangent):
    rows, width = cotangent.shape
    slots = slot_weight.shape[1]
    shapes = [((slots // 2, 2 * width + EXTRA), LOW)] * 2
    shapes += [((rows, slots), WIDE)] * 2 + [((width, slots), LOW)] + [((rows, width), LOW)] * 2
    return call(
        opening_kernel,
        "opening",
        (at, stay(tokens), stay(slot_weight), stay(cotangent)),
        [IN_SMEM] + [IN_HBM] * 3,
        [IN_VMEM] * len(shapes),
        [jax.ShapeDtypeStruct(*shape) for shape in shapes],
        [pltpu.VMEM((width, slots), LOW), pltpu.SemaphoreType.DMA((3,))],
    )


def merge_kernel(kept_ref, taken_ref, out_ref):
    width = (out_ref.shape[2] - EXTRA) // 2
    kept, taken = kept_ref[:, 2 * width :].astype(WIDE), taken_ref[:, 2 * width :].astype(WIDE)
    kept_max, taken_max = lanes(kept, 0), lanes(taken, 0)
    top = jnp.maximum(kept_max, taken_max)
    kept_scale, taken_scale = jnp.exp(kept_max - top), jnp.exp(taken_max - top)
    total = kept_scale * lanes(kept, 3) + taken_scale * lanes(taken, 3)
    slots = kept_scale * kept_ref[:, :width].astype(WIDE) + taken_scale * taken_ref[
        :, :width
    ].astype(WIDE)
    grads = kept_ref[:, width : 2 * width].astype(WIDE) + taken_ref[
        :, width : 2 * width
    ].astype(WIDE)
    pieces = place(split3(top) + split3(total), kept.shape, 1)
    peers, own = out_ref.shape[:2]
    out_ref[:, :, :width] = slots.astype(LOW).reshape(peers, own, width)
    out_ref[:, :, width : 2 * width] = grads.astype(LOW).reshape(peers, own, width)
    out_ref[:, :, 2 * width :] = pieces.astype(LOW).reshape(peers, own, EXTRA)


def merge(kept, taken, peers):
    shape = jax.ShapeDtypeStruct((peers, kept.shape[0] // peers, kept.shape[1]), LOW)
    return call(merge_kernel, "merge", (kept, taken), [IN_VMEM] * 2, IN_VMEM, shape)


def expert_kernel(got_ref, in_ref, out_ref, told_ref):
    w_in, w_out = in_ref[0], out_ref[0]
    peers, own, wide = got_ref.shape
    count, width = peers * own, w_in.shape[0]
    got = got_ref[...].reshape(count, wide)
    pieces = got[:, 2 * width :].astype(WIDE)
    block_max, block_sum = lanes(pieces, 0), lanes(pieces, 3)
    odd = lax.broadcasted_iota(jnp.int32, (count, 1), 0) % 2 == 1
    lowest = jnp.full((count, 1), -jnp.inf, WIDE)
    top = [
        jnp.max(jnp.where(odd, lowest, block_max), axis=0, keepdims=True),
        jnp.max(jnp.where(odd, block_max, lowest), axis=0, keepdims=True),
    ]
    scale = jnp.exp(block_max - jnp.where(odd, top[1], top[0]))
    scaled_sum = scale * block_sum
    totals = [
        jnp.sum(jnp.where(odd, 0.0, scaled_sum), axis=0, keepdims=True),
        jnp.sum(jnp.where(odd, scaled_sum, 0.0), axis=0, keepdims=True),
    ]
    scaled = scale * got[:, :width].astype(WIDE)
    exact = [
        jnp.sum(jnp.where(odd, 0.0, scaled), axis=0, keepdims=True) / totals[0],
        jnp.sum(jnp.where(odd, scaled, 0.0), axis=0, keepdims=True) / totals[1],
    ]
    sent = got[:, width : 2 * width].astype(WIDE)
    grads = [
        jnp.sum(jnp.where(odd, 0.0, sent), axis=0, keepdims=True),
        jnp.sum(jnp.where(odd, sent, 0.0), axis=0, keepdims=True),
    ]
    exact = place(exact, (8, width), 0)
    out_grad = place(grads, (8, width), 0).astype(LOW)
    slot_low = exact.astype(LOW)
    preact = product(slot_low, w_in, 1, 0)
    hid_grad = product(out_grad, w_out, 1, 1)
    rate = 0.7978845608028654
    square = preact * preact
    curve = jnp.tanh(rate * (preact + 0.044715 * square * preact))
    low_hidden = (0.5 * preact * (1.0 + curve)).astype(LOW)
    slope = 0.5 * (1.0 + curve) + 0.5 * preact * (1.0 - curve * curve) * rate * (
        1.0 + 3.0 * 0.044715 * square
    )
    pre_grad = (slope * hid_grad).astype(LOW)
    slot_out = product(low_hidden, w_out, 1, 0)
    in_grad = product(pre_grad, w_in, 1, 1)
    slot_product = jnp.sum(exact * in_grad, axis=1, keepdims=True)
    top = place(top, (8, 1), 0)
    totals = place(totals, (8, 1), 0)
    scalars = place(split3(slot_product) + split3(top) + split3(totals), (8, EXTRA), 1)
    spread = lambda block: jnp.broadcast_to(
        block[:own].astype(LOW)[None], (peers, own, block.shape[1])
    )
    told_ref[:, :, :width] = spread(slot_out)
    told_ref[:, :, width : 2 * width] = spread(in_grad)
    told_ref[:, :, 2 * width :] = spread(scalars)


def expert(got, w_in, w_out):
    shape = jax.ShapeDtypeStruct(got.shape, LOW)
    return call(expert_kernel, "expert", (got, w_in, w_out), [IN_VMEM] * 3, IN_VMEM, shape)


STEPS = 2


def closing_kernel(
    mine_ref, pair_ref, tok_ref, cot_ref, comb_ref, logit_ref, order_ref,
    mixed_hbm, grad_hbm,
    all_out, in_low, rows_ref, mixed_ref, grad_ref, out_sems,
):
    count, width = cot_ref.shape
    half = mine_ref.shape[0] * mine_ref.shape[1]
    block = count // STEPS
    for at, ref in enumerate((mine_ref, pair_ref)):
        part = slice(at * half, (at + 1) * half)
        all_out[part, :] = ref[:, :, :width].reshape(half, width)
        in_low[part, :] = ref[:, :, width : 2 * width].reshape(half, width)
        pieces = ref[:, :, 2 * width :].reshape(half, EXTRA).astype(WIDE).T
        for row in range(3):
            rows_ref[row : row + 1, part] = jnp.sum(
                pieces[3 * row : 3 * row + 3], axis=0, keepdims=True
            )
    slot_product, highest, totals = rows_ref[0:1], rows_ref[1:2], rows_ref[2:3]
    stores = []
    for step in range(STEPS):
        part = pl.ds(step * block, block)
        stores.append(
            pltpu.make_async_copy(mixed_ref.at[part], mixed_hbm.at[part], out_sems.at[0, step])
        )
        stores.append(
            pltpu.make_async_copy(grad_ref.at[part], grad_hbm.at[part], out_sems.at[1, step])
        )
        combine = comb_ref[part]
        mixed_ref[part, :] = product(combine.astype(LOW), all_out[...], 1, 0).astype(LOW)
        stores[-2].start()
        comb_grad = product(cot_ref[part], all_out[...], 1, 1)
        logit_grad = combine * (comb_grad - jnp.sum(combine * comb_grad, axis=1, keepdims=True))
        dispatch = jnp.exp(logit_ref[part] - highest) / totals
        logit_grad += dispatch * (product(tok_ref[part], in_low[...], 1, 1) - slot_product)
        token_grad = product(logit_grad.astype(LOW), order_ref[...], 1, 1)
        token_grad += product(dispatch.astype(LOW), in_low[...], 1, 0)
        grad_ref[part, :] = token_grad.astype(LOW)
        stores[-1].start()
    for copy in stores:
        copy.wait()


def closing(mine, pair, tokens, cotangent, combine, logits, weight):
    rows, width = cotangent.shape
    slots = weight.shape[1]
    return call(
        closing_kernel,
        "closing",
        (mine, pair, tokens, cotangent, combine, logits, weight),
        [IN_VMEM] * 7,
        [IN_HBM] * 2,
        [jax.ShapeDtypeStruct((rows, width), LOW)] * 2,
        [
            pltpu.VMEM((slots, width), LOW),
            pltpu.VMEM((slots, width), LOW),
            pltpu.VMEM((8, slots), WIDE),
            pltpu.VMEM((rows, width), LOW),
            pltpu.VMEM((rows, width), LOW),
            pltpu.SemaphoreType.DMA((2, STEPS)),
        ],
    )


def shards(tokens, slot_weight, w_in, w_out, cotangent):
    torus = ("x", "z", "exp")
    swap = [(0, 1), (1, 0)]
    at = jnp.stack([lax.axis_index("exp"), lax.axis_index("core")]).astype(jnp.int32)
    peers = lax.axis_size(torus)
    kept, given, combine, logits, weight, rows, cot = opening(at, tokens, slot_weight, cotangent)
    sent = merge(kept, lax.ppermute(given, "core", swap), peers)
    got = lax.all_to_all(sent, torus, split_axis=0, concat_axis=0, tiled=True)
    told = expert(got, w_in, w_out)
    told = lax.all_to_all(told, torus, split_axis=0, concat_axis=0, tiled=True)
    pair = lax.ppermute(told, "core", swap)
    return tuple(closing(told, pair, rows, cot, combine, logits, weight))


def solution(mesh):
    exp = mesh.devices.shape[1]
    finer = Mesh(mesh.devices.reshape(4, 4, 2, exp), ("x", "z", "core", "exp"))
    every = ("x", "z", "core", "exp")
    rows = P(every, None)
    experts = P(every, None, None)
    return jax.shard_map(
        shards,
        mesh=finer,
        in_specs=(P(("x", "z", "core"), None), P(), experts, experts, rows),
        out_specs=(rows, rows),
        check_vma=False,
    )
```

```python
import functools

import jax
import jax.numpy as jnp
from jax import lax
from jax.experimental import pallas as pl
from jax.experimental.pallas import tpu as pltpu
from jax.sharding import Mesh
from jax.sharding import PartitionSpec as P

LOW = jnp.bfloat16
WIDE = jnp.float32
EXTRA = 128
LIMIT = 20 * 1024 * 1024


def product(left, right, left_dim, right_dim):
    return lax.dot_general(
        left, right, (((left_dim,), (right_dim,)), ((), ())), preferred_element_type=WIDE
    )


def split3(value):
    high = value.astype(LOW).astype(WIDE)
    rest = value - high
    mid = rest.astype(LOW).astype(WIDE)
    return [high, mid, rest - mid]


def place(pieces, shape, axis):
    index = lax.broadcasted_iota(jnp.int32, shape, axis)
    total = jnp.zeros(shape, WIDE)
    for at, piece in enumerate(pieces):
        total = jnp.where(index == at, piece, total)
    return total


def lanes(block, first):
    index = lax.broadcasted_iota(jnp.int32, block.shape, 1)
    inside = (index >= first) & (index < first + 3)
    return jnp.sum(jnp.where(inside, block, 0.0), axis=1, keepdims=True)


IN_SMEM = pl.BlockSpec(memory_space=pltpu.SMEM)
IN_VMEM = pl.BlockSpec(memory_space=pltpu.VMEM)
IN_HBM = pl.BlockSpec(memory_space=pltpu.HBM)


def stay(array):
    return pltpu.with_memory_space_constraint(array, pltpu.HBM)


SPAN = pl.CostEstimate(flops=9_000_000_000, bytes_accessed=20_000_000, transcendentals=0)


def call(kernel, name, args, specs, out_specs, out_shape, scratch=(), cost=None):
    return pl.pallas_call(
        kernel,
        in_specs=specs,
        out_specs=out_specs,
        out_shape=out_shape,
        scratch_shapes=scratch,
        compiler_params=pltpu.CompilerParams(vmem_limit_bytes=LIMIT),
        cost_estimate=cost,
        name=name,
    )(*args)


def ordering(core, slots):
    to = lax.broadcasted_iota(jnp.int32, (slots, 1), 0)
    source = lax.broadcasted_iota(jnp.int32, (slots, slots), 1)
    half = slots // 2
    within = to % half
    other = jnp.where(to // half == 0, core, 1 - core)
    wanted = (within // 8) * 16 + other * 8 + within % 8
    return (source == wanted).astype(WIDE).astype(LOW)


def opening_kernel(
    at_ref, tok_hbm, weight_hbm, cot_hbm, kept_ref, given_ref, order_ref, rows_ref, cot_ref,
    weight_ref, sems,
):
    slots = weight_ref.shape[1]
    half = slots // 2
    count, width = rows_ref.shape
    start = pl.multiple_of(at_ref[0] * count, count)
    loads = [
        pltpu.make_async_copy(source, target, sems.at[at])
        for at, (source, target) in enumerate(
            (
                (weight_hbm, weight_ref),
                (tok_hbm.at[pl.ds(start, count)], rows_ref),
                (cot_hbm, cot_ref),
            )
        )
    ]
    for copy in loads:
        copy.start()
    order = ordering(at_ref[1], slots)
    loads[0].wait()
    weight = product(order, weight_ref[...], 1, 1).astype(LOW)
    order_ref[...] = weight
    loads[1].wait()
    rows = rows_ref[...]
    logits = product(weight, rows, 1, 1)
    slot_max = jnp.max(logits, axis=1, keepdims=True)
    shifted = jnp.exp(logits - slot_max)
    slot_sum = jnp.sum(shifted, axis=1, keepdims=True)
    slot_part = product(shifted.astype(LOW), rows, 1, 0)
    raised = jnp.exp(logits - jnp.max(logits, axis=0, keepdims=True))
    combine = raised * (1.0 / jnp.sum(raised, axis=0, keepdims=True))
    loads[2].wait()
    grad_part = product(combine.astype(LOW), cot_ref[...], 1, 0)
    pieces = place(split3(slot_max) + split3(slot_sum), (slots, EXTRA), 1)
    for at, out in enumerate((kept_ref, given_ref)):
        part = slice(at * half, (at + 1) * half)
        out[:, :width] = slot_part[part].astype(LOW)
        out[:, width : 2 * width] = grad_part[part].astype(LOW)
        out[:, 2 * width :] = pieces[part].astype(LOW)


def opening(at, tokens, slot_weight, cotangent):
    rows, width = cotangent.shape
    slots = slot_weight.shape[1]
    shapes = [(slots // 2, 2 * width + EXTRA)] * 2 + [(slots, width)] + [(rows, width)] * 2
    return call(
        opening_kernel,
        "opening",
        (at, stay(tokens), stay(slot_weight), stay(cotangent)),
        [IN_SMEM] + [IN_HBM] * 3,
        [IN_VMEM] * len(shapes),
        [jax.ShapeDtypeStruct(shape, LOW) for shape in shapes],
        [pltpu.VMEM((width, slots), LOW), pltpu.SemaphoreType.DMA((3,))],
    )


def combine_kernel(rows_ref, order_ref, logit_ref, comb_ref):
    logits = product(rows_ref[...], order_ref[...], 1, 1)
    logit_ref[...] = logits
    raised = jnp.exp(logits - jnp.max(logits, axis=1, keepdims=True))
    comb_ref[...] = raised * (1.0 / jnp.sum(raised, axis=1, keepdims=True))


def combining(rows, order):
    shape = jax.ShapeDtypeStruct((rows.shape[0], order.shape[0]), WIDE)
    cost = pl.CostEstimate(flops=1_000_000_000, bytes_accessed=4_000_000, transcendentals=131_072)
    return call(
        combine_kernel, "combining", (rows, order), [IN_VMEM] * 2, [IN_VMEM] * 2, [shape] * 2, (), cost
    )


def merge_kernel(kept_ref, taken_ref, out_ref):
    width = (out_ref.shape[2] - EXTRA) // 2
    kept, taken = kept_ref[:, 2 * width :].astype(WIDE), taken_ref[:, 2 * width :].astype(WIDE)
    kept_max, taken_max = lanes(kept, 0), lanes(taken, 0)
    top = jnp.maximum(kept_max, taken_max)
    kept_scale, taken_scale = jnp.exp(kept_max - top), jnp.exp(taken_max - top)
    total = kept_scale * lanes(kept, 3) + taken_scale * lanes(taken, 3)
    slots = kept_scale * kept_ref[:, :width].astype(WIDE) + taken_scale * taken_ref[
        :, :width
    ].astype(WIDE)
    grads = kept_ref[:, width : 2 * width].astype(WIDE) + taken_ref[
        :, width : 2 * width
    ].astype(WIDE)
    pieces = place(split3(top) + split3(total), kept.shape, 1)
    peers, own = out_ref.shape[:2]
    out_ref[:, :, :width] = slots.astype(LOW).reshape(peers, own, width)
    out_ref[:, :, width : 2 * width] = grads.astype(LOW).reshape(peers, own, width)
    out_ref[:, :, 2 * width :] = pieces.astype(LOW).reshape(peers, own, EXTRA)


def merge(kept, taken, peers):
    shape = jax.ShapeDtypeStruct((peers, kept.shape[0] // peers, kept.shape[1]), LOW)
    return call(merge_kernel, "merge", (kept, taken), [IN_VMEM] * 2, IN_VMEM, shape, (), SPAN)


def expert_kernel(got_ref, in_ref, out_ref, told_ref):
    w_in, w_out = in_ref[0], out_ref[0]
    peers, own, wide = got_ref.shape
    count, width = peers * own, w_in.shape[0]
    got = got_ref[...].reshape(count, wide)
    pieces = got[:, 2 * width :].astype(WIDE)
    block_max, block_sum = lanes(pieces, 0), lanes(pieces, 3)
    odd = lax.broadcasted_iota(jnp.int32, (count, 1), 0) % 2 == 1
    lowest = jnp.full((count, 1), -jnp.inf, WIDE)
    top = [
        jnp.max(jnp.where(odd, lowest, block_max), axis=0, keepdims=True),
        jnp.max(jnp.where(odd, block_max, lowest), axis=0, keepdims=True),
    ]
    scale = jnp.exp(block_max - jnp.where(odd, top[1], top[0]))
    scaled_sum = scale * block_sum
    totals = [
        jnp.sum(jnp.where(odd, 0.0, scaled_sum), axis=0, keepdims=True),
        jnp.sum(jnp.where(odd, scaled_sum, 0.0), axis=0, keepdims=True),
    ]
    scaled = scale * got[:, :width].astype(WIDE)
    exact = [
        jnp.sum(jnp.where(odd, 0.0, scaled), axis=0, keepdims=True) / totals[0],
        jnp.sum(jnp.where(odd, scaled, 0.0), axis=0, keepdims=True) / totals[1],
    ]
    sent = got[:, width : 2 * width].astype(WIDE)
    grads = [
        jnp.sum(jnp.where(odd, 0.0, sent), axis=0, keepdims=True),
        jnp.sum(jnp.where(odd, sent, 0.0), axis=0, keepdims=True),
    ]
    exact = place(exact, (8, width), 0)
    out_grad = place(grads, (8, width), 0).astype(LOW)
    slot_low = exact.astype(LOW)
    preact = product(slot_low, w_in, 1, 0)
    hid_grad = product(out_grad, w_out, 1, 1)
    rate = 0.7978845608028654
    square = preact * preact
    curve = jnp.tanh(rate * (preact + 0.044715 * square * preact))
    low_hidden = (0.5 * preact * (1.0 + curve)).astype(LOW)
    slope = 0.5 * (1.0 + curve) + 0.5 * preact * (1.0 - curve * curve) * rate * (
        1.0 + 3.0 * 0.044715 * square
    )
    pre_grad = (slope * hid_grad).astype(LOW)
    slot_out = product(low_hidden, w_out, 1, 0)
    in_grad = product(pre_grad, w_in, 1, 1)
    slot_product = jnp.sum(exact * in_grad, axis=1, keepdims=True)
    top = place(top, (8, 1), 0)
    totals = place(totals, (8, 1), 0)
    scalars = place(split3(slot_product) + split3(top) + split3(totals), (8, EXTRA), 1)
    spread = lambda block: jnp.broadcast_to(
        block[:own].astype(LOW)[None], (peers, own, block.shape[1])
    )
    told_ref[:, :, :width] = spread(slot_out)
    told_ref[:, :, width : 2 * width] = spread(in_grad)
    told_ref[:, :, 2 * width :] = spread(scalars)


def expert(got, w_in, w_out):
    shape = jax.ShapeDtypeStruct(got.shape, LOW)
    return call(expert_kernel, "expert", (got, w_in, w_out), [IN_VMEM] * 3, IN_VMEM, shape)


COLUMNS = (slice(0, 768), slice(768, 1280))


def closing_kernel(
    mine_ref, pair_ref, tok_ref, cot_ref, comb_ref, logit_ref, order_ref,
    mixed_hbm, grad_hbm,
    all_out, in_low, rows_ref, mixed_ref, grad_ref, sems,
):
    width = cot_ref.shape[1]
    half = mine_ref.shape[0] * mine_ref.shape[1]
    stores = []

    def store(source, target, columns):
        at = len(stores)
        where = (slice(None), pl.ds(columns.start, columns.stop - columns.start))
        stores.append(pltpu.make_async_copy(source.at[where], target.at[where], sems.at[at]))
        stores[at].start()

    for at, ref in enumerate((mine_ref, pair_ref)):
        part = slice(at * half, (at + 1) * half)
        all_out[part, :] = ref[:, :, :width].reshape(half, width)
        in_low[part, :] = ref[:, :, width : 2 * width].reshape(half, width)
        pieces = ref[:, :, 2 * width :].reshape(half, EXTRA).astype(WIDE).T
        for row in range(3):
            rows_ref[row : row + 1, part] = jnp.sum(
                pieces[3 * row : 3 * row + 3], axis=0, keepdims=True
            )
    slot_product, highest, totals = rows_ref[0:1], rows_ref[1:2], rows_ref[2:3]
    combine = comb_ref[...]
    combine_low = combine.astype(LOW)
    for columns in COLUMNS:
        mixed_ref[:, columns] = product(combine_low, all_out[:, columns], 1, 0).astype(LOW)
        store(mixed_ref, mixed_hbm, columns)
    comb_grad = product(cot_ref[...], all_out[...], 1, 1)
    logit_grad = combine * (comb_grad - jnp.sum(combine * comb_grad, axis=1, keepdims=True))
    dispatch = jnp.exp(logit_ref[...] - highest) * (1.0 / totals)
    logit_grad += dispatch * (product(tok_ref[...], in_low[...], 1, 1) - slot_product)
    logit_low, dispatch_low = logit_grad.astype(LOW), dispatch.astype(LOW)
    for columns in COLUMNS:
        token_grad = product(logit_low, order_ref[:, columns], 1, 0)
        token_grad += product(dispatch_low, in_low[:, columns], 1, 0)
        grad_ref[:, columns] = token_grad.astype(LOW)
        store(grad_ref, grad_hbm, columns)
    for copy in stores:
        copy.wait()


def closing(mine, pair, tokens, cotangent, combine, logits, weight):
    rows, width = cotangent.shape
    slots = weight.shape[0]
    return call(
        closing_kernel,
        "closing",
        (mine, pair, tokens, cotangent, combine, logits, weight),
        [IN_VMEM] * 7,
        [IN_HBM] * 2,
        [jax.ShapeDtypeStruct((rows, width), LOW)] * 2,
        [
            pltpu.VMEM((slots, width), LOW),
            pltpu.VMEM((slots, width), LOW),
            pltpu.VMEM((8, slots), WIDE),
            pltpu.VMEM((rows, width), LOW),
            pltpu.VMEM((rows, width), LOW),
            pltpu.SemaphoreType.DMA((2 * len(COLUMNS),)),
        ],
    )


def shards(tokens, slot_weight, w_in, w_out, cotangent):
    torus = ("x", "z", "exp")
    swap = [(0, 1), (1, 0)]
    at = jnp.stack([lax.axis_index("exp"), lax.axis_index("core")]).astype(jnp.int32)
    peers = lax.axis_size(torus)
    kept, given, weight, rows, cot = opening(at, tokens, slot_weight, cotangent)
    logits, combine = combining(rows, weight)
    sent = merge(kept, lax.ppermute(given, "core", swap), peers)
    got = lax.all_to_all(sent, torus, split_axis=0, concat_axis=0, tiled=True)
    told = expert(got, w_in, w_out)
    told = lax.all_to_all(told, torus, split_axis=0, concat_axis=0, tiled=True)
    pair = lax.ppermute(told, "core", swap)
    return tuple(closing(told, pair, rows, cot, combine, logits, weight))


def solution(mesh):
    exp = mesh.devices.shape[1]
    finer = Mesh(mesh.devices.reshape(4, 4, 2, exp), ("x", "z", "core", "exp"))
    every = ("x", "z", "core", "exp")
    rows = P(every, None)
    experts = P(every, None, None)
    return jax.shard_map(
        shards,
        mesh=finer,
        in_specs=(P(("x", "z", "core"), None), P(), experts, experts, rows),
        out_specs=(rows, rows),
        check_vma=False,
    )
```

```python
import functools

import jax
import jax.numpy as jnp
from jax import lax
from jax.experimental import pallas as pl
from jax.experimental.pallas import tpu as pltpu
from jax.sharding import Mesh
from jax.sharding import PartitionSpec as P

LOW = jnp.bfloat16
WIDE = jnp.float32
EXTRA = 128
LIMIT = 20 * 1024 * 1024


def product(left, right, left_dim, right_dim):
    return lax.dot_general(
        left, right, (((left_dim,), (right_dim,)), ((), ())), preferred_element_type=WIDE
    )


def split3(value):
    high = value.astype(LOW).astype(WIDE)
    rest = value - high
    mid = rest.astype(LOW).astype(WIDE)
    return [high, mid, rest - mid]


def place(pieces, shape, axis):
    index = lax.broadcasted_iota(jnp.int32, shape, axis)
    total = jnp.zeros(shape, WIDE)
    for at, piece in enumerate(pieces):
        total = jnp.where(index == at, piece, total)
    return total


def lanes(block, first):
    index = lax.broadcasted_iota(jnp.int32, block.shape, 1)
    inside = (index >= first) & (index < first + 3)
    return jnp.sum(jnp.where(inside, block, 0.0), axis=1, keepdims=True)


IN_SMEM = pl.BlockSpec(memory_space=pltpu.SMEM)
IN_VMEM = pl.BlockSpec(memory_space=pltpu.VMEM)
IN_HBM = pl.BlockSpec(memory_space=pltpu.HBM)


def stay(array):
    return pltpu.with_memory_space_constraint(array, pltpu.HBM)


SPAN = pl.CostEstimate(flops=9_000_000_000, bytes_accessed=20_000_000, transcendentals=0)


def call(kernel, name, args, specs, out_specs, out_shape, scratch=(), cost=None):
    return pl.pallas_call(
        kernel,
        in_specs=specs,
        out_specs=out_specs,
        out_shape=out_shape,
        scratch_shapes=scratch,
        compiler_params=pltpu.CompilerParams(vmem_limit_bytes=LIMIT),
        cost_estimate=cost,
        name=name,
    )(*args)


def ordering(core, slots):
    to = lax.broadcasted_iota(jnp.int32, (slots, 1), 0)
    source = lax.broadcasted_iota(jnp.int32, (slots, slots), 1)
    half = slots // 2
    within = to % half
    other = jnp.where(to // half == 0, core, 1 - core)
    wanted = (within // 8) * 16 + other * 8 + within % 8
    return (source == wanted).astype(WIDE).astype(LOW)


def halves(value, outs, columns):
    half = outs[0].shape[0]
    for at, out in enumerate(outs):
        out[:, columns] = value[at * half : (at + 1) * half].astype(LOW)


def opening_kernel(
    at_ref, tok_hbm, weight_hbm, cot_hbm,
    kept_ref, given_ref, logit_ref, order_ref, rows_ref, cot_ref,
    weight_ref, sems,
):
    slots = weight_ref.shape[1]
    count, width = rows_ref.shape
    start = pl.multiple_of(at_ref[0] * count, count)
    loads = [
        pltpu.make_async_copy(source, target, sems.at[at])
        for at, (source, target) in enumerate(
            (
                (weight_hbm, weight_ref),
                (tok_hbm.at[pl.ds(start, count)], rows_ref),
                (cot_hbm, cot_ref),
            )
        )
    ]
    loads[0].start()
    loads[1].start()
    order = ordering(at_ref[1], slots)
    loads[0].wait()
    weight = product(order, weight_ref[...], 1, 1).astype(LOW)
    order_ref[...] = weight
    loads[1].wait()
    loads[2].start()
    rows = rows_ref[...]
    logits = product(weight, rows, 1, 1)
    logit_ref[...] = logits
    slot_max = jnp.max(logits, axis=1, keepdims=True)
    shifted = jnp.exp(logits - slot_max)
    slot_sum = jnp.sum(shifted, axis=1, keepdims=True)
    outs = (kept_ref, given_ref)
    halves(product(shifted.astype(LOW), rows, 1, 0), outs, slice(0, width))
    pieces = place(split3(slot_max) + split3(slot_sum), (slots, EXTRA), 1)
    halves(pieces, outs, slice(width, width + EXTRA))
    loads[2].wait()


def opening(at, tokens, slot_weight, cotangent):
    rows, width = cotangent.shape
    slots = slot_weight.shape[1]
    shapes = [((slots // 2, width + EXTRA), LOW)] * 2 + [((slots, rows), WIDE)]
    shapes += [((slots, width), LOW)] + [((rows, width), LOW)] * 2
    return call(
        opening_kernel,
        "opening",
        (at, stay(tokens), stay(slot_weight), stay(cotangent)),
        [IN_SMEM] + [IN_HBM] * 3,
        [IN_VMEM] * len(shapes),
        [jax.ShapeDtypeStruct(*shape) for shape in shapes],
        [pltpu.VMEM((width, slots), LOW), pltpu.SemaphoreType.DMA((3,))],
    )


def grads_kernel(logit_ref, cot_ref, kept_ref, given_ref):
    logits = logit_ref[...]
    raised = jnp.exp(logits - jnp.max(logits, axis=0, keepdims=True))
    combine = raised * (1.0 / jnp.sum(raised, axis=0, keepdims=True))
    grad_part = product(combine.astype(LOW), cot_ref[...], 1, 0)
    halves(grad_part, (kept_ref, given_ref), slice(0, grad_part.shape[1]))


SIDE = pl.CostEstimate(flops=1_000_000_000, bytes_accessed=4_000_000, transcendentals=131_072)


def grads_of(logits, cotangent):
    shape = jax.ShapeDtypeStruct((logits.shape[0] // 2, cotangent.shape[1]), LOW)
    args = (logits, cotangent)
    return call(grads_kernel, "grads", args, [IN_VMEM] * 2, [IN_VMEM] * 2, [shape] * 2, (), SIDE)


def combine_kernel(rows_ref, order_ref, logit_ref, comb_ref):
    logits = product(rows_ref[...], order_ref[...], 1, 1)
    logit_ref[...] = logits
    raised = jnp.exp(logits - jnp.max(logits, axis=1, keepdims=True))
    comb_ref[...] = raised * (1.0 / jnp.sum(raised, axis=1, keepdims=True))


def combining(rows, order):
    shape = jax.ShapeDtypeStruct((rows.shape[0], order.shape[0]), WIDE)
    args = (rows, order)
    return call(
        combine_kernel, "combining", args, [IN_VMEM] * 2, [IN_VMEM] * 2, [shape] * 2, (), SIDE
    )


def merge_kernel(kept_ref, taken_ref, kept_grad_ref, taken_grad_ref, out_ref):
    width = kept_grad_ref.shape[1]
    kept, taken = kept_ref[:, width:].astype(WIDE), taken_ref[:, width:].astype(WIDE)
    kept_max, taken_max = lanes(kept, 0), lanes(taken, 0)
    top = jnp.maximum(kept_max, taken_max)
    kept_scale, taken_scale = jnp.exp(kept_max - top), jnp.exp(taken_max - top)
    total = kept_scale * lanes(kept, 3) + taken_scale * lanes(taken, 3)
    slots = kept_scale * kept_ref[:, :width].astype(WIDE) + taken_scale * taken_ref[
        :, :width
    ].astype(WIDE)
    grads = kept_grad_ref[...].astype(WIDE) + taken_grad_ref[...].astype(WIDE)
    pieces = place(split3(top) + split3(total), kept.shape, 1)
    peers, own = out_ref.shape[:2]
    out_ref[:, :, :width] = slots.astype(LOW).reshape(peers, own, width)
    out_ref[:, :, width : 2 * width] = grads.astype(LOW).reshape(peers, own, width)
    out_ref[:, :, 2 * width :] = pieces.astype(LOW).reshape(peers, own, EXTRA)


def merge(kept, taken, kept_grad, taken_grad, peers):
    wide = kept.shape[1] + kept_grad.shape[1]
    shape = jax.ShapeDtypeStruct((peers, kept.shape[0] // peers, wide), LOW)
    args = (kept, taken, kept_grad, taken_grad)
    return call(merge_kernel, "merge", args, [IN_VMEM] * 4, IN_VMEM, shape, (), SPAN)


def expert_kernel(got_ref, in_ref, out_ref, told_ref):
    w_in, w_out = in_ref[0], out_ref[0]
    peers, own, wide = got_ref.shape
    count, width = peers * own, w_in.shape[0]
    got = got_ref[...].reshape(count, wide)
    pieces = got[:, 2 * width :].astype(WIDE)
    block_max, block_sum = lanes(pieces, 0), lanes(pieces, 3)
    odd = lax.broadcasted_iota(jnp.int32, (count, 1), 0) % 2 == 1
    lowest = jnp.full((count, 1), -jnp.inf, WIDE)
    top = [
        jnp.max(jnp.where(odd, lowest, block_max), axis=0, keepdims=True),
        jnp.max(jnp.where(odd, block_max, lowest), axis=0, keepdims=True),
    ]
    scale = jnp.exp(block_max - jnp.where(odd, top[1], top[0]))
    scaled_sum = scale * block_sum
    totals = [
        jnp.sum(jnp.where(odd, 0.0, scaled_sum), axis=0, keepdims=True),
        jnp.sum(jnp.where(odd, scaled_sum, 0.0), axis=0, keepdims=True),
    ]
    high = scale.astype(LOW).astype(WIDE)
    rest, ones = scale - high, jnp.ones_like(scale)
    columns = []
    for column in (high, rest, ones):
        columns += [jnp.where(odd, 0.0, column), jnp.where(odd, column, 0.0)]
    picks = place(columns, (count, EXTRA), 1).T[:8].astype(LOW)
    sums = product(picks, got[:, : 2 * width], 1, 0)
    sums_of = lambda row, part: sums[row : row + 1, part]
    front, back = slice(0, width), slice(width, 2 * width)
    exact = [(sums_of(row, front) + sums_of(row + 2, front)) / totals[row] for row in range(2)]
    exact = place(exact, (8, width), 0)
    out_grad = place([sums_of(4, back), sums_of(5, back)], (8, width), 0).astype(LOW)
    slot_low = exact.astype(LOW)
    preact = product(slot_low, w_in, 1, 0)
    hid_grad = product(out_grad, w_out, 1, 1)
    rate = 0.7978845608028654
    square = preact * preact
    curve = jnp.tanh(rate * (preact + 0.044715 * square * preact))
    low_hidden = (0.5 * preact * (1.0 + curve)).astype(LOW)
    slope = 0.5 * (1.0 + curve) + 0.5 * preact * (1.0 - curve * curve) * rate * (
        1.0 + 3.0 * 0.044715 * square
    )
    pre_grad = (slope * hid_grad).astype(LOW)
    slot_out = product(low_hidden, w_out, 1, 0)
    in_grad = product(pre_grad, w_in, 1, 1)
    slot_product = jnp.sum(exact * in_grad, axis=1, keepdims=True)
    top = place(top, (8, 1), 0)
    totals = place(totals, (8, 1), 0)
    scalars = place(split3(slot_product) + split3(top) + split3(totals), (8, EXTRA), 1)
    spread = lambda block: jnp.broadcast_to(
        block[:own].astype(LOW)[None], (peers, own, block.shape[1])
    )
    told_ref[:, :, :width] = spread(slot_out)
    told_ref[:, :, width : 2 * width] = spread(in_grad)
    told_ref[:, :, 2 * width :] = spread(scalars)


def expert(got, w_in, w_out):
    shape = jax.ShapeDtypeStruct(got.shape, LOW)
    return call(expert_kernel, "expert", (got, w_in, w_out), [IN_VMEM] * 3, IN_VMEM, shape)


STEPS = 2


def closing_kernel(
    mine_ref, pair_ref, tok_ref, cot_ref, comb_ref, logit_ref, order_ref,
    mixed_hbm, grad_hbm,
    all_out, in_low, rows_ref, mixed_ref, grad_ref, out_sems,
):
    count, width = cot_ref.shape
    half = mine_ref.shape[0] * mine_ref.shape[1]
    block = count // STEPS
    for at, ref in enumerate((mine_ref, pair_ref)):
        part = slice(at * half, (at + 1) * half)
        all_out[part, :] = ref[:, :, :width].reshape(half, width)
        in_low[part, :] = ref[:, :, width : 2 * width].reshape(half, width)
        pieces = ref[:, :, 2 * width :].reshape(half, EXTRA).astype(WIDE).T
        for row in range(3):
            rows_ref[row : row + 1, part] = jnp.sum(
                pieces[3 * row : 3 * row + 3], axis=0, keepdims=True
            )
    slot_product, highest, scale = rows_ref[0:1], rows_ref[1:2], 1.0 / rows_ref[2:3]
    stores = []
    for step in range(STEPS):
        part = pl.ds(step * block, block)
        stores.append(
            pltpu.make_async_copy(mixed_ref.at[part], mixed_hbm.at[part], out_sems.at[0, step])
        )
        stores.append(
            pltpu.make_async_copy(grad_ref.at[part], grad_hbm.at[part], out_sems.at[1, step])
        )
        combine = comb_ref[part]
        mixed_ref[part, :] = product(combine.astype(LOW), all_out[...], 1, 0).astype(LOW)
        stores[-2].start()
        comb_grad = product(cot_ref[part], all_out[...], 1, 1)
        logit_grad = combine * (comb_grad - jnp.sum(combine * comb_grad, axis=1, keepdims=True))
        dispatch = jnp.exp(logit_ref[part] - highest) * scale
        logit_grad += dispatch * (product(tok_ref[part], in_low[...], 1, 1) - slot_product)
        token_grad = product(logit_grad.astype(LOW), order_ref[...], 1, 0)
        token_grad += product(dispatch.astype(LOW), in_low[...], 1, 0)
        grad_ref[part, :] = token_grad.astype(LOW)
        stores[-1].start()
    for copy in stores:
        copy.wait()


def closing(mine, pair, tokens, cotangent, combine, logits, weight):
    rows, width = cotangent.shape
    slots = weight.shape[0]
    return call(
        closing_kernel,
        "closing",
        (mine, pair, tokens, cotangent, combine, logits, weight),
        [IN_VMEM] * 7,
        [IN_HBM] * 2,
        [jax.ShapeDtypeStruct((rows, width), LOW)] * 2,
        [
            pltpu.VMEM((slots, width), LOW),
            pltpu.VMEM((slots, width), LOW),
            pltpu.VMEM((8, slots), WIDE),
            pltpu.VMEM((rows, width), LOW),
            pltpu.VMEM((rows, width), LOW),
            pltpu.SemaphoreType.DMA((2, STEPS)),
        ],
    )


def shards(tokens, slot_weight, w_in, w_out, cotangent):
    torus = ("x", "z", "exp")
    swap = [(0, 1), (1, 0)]
    at = jnp.stack([lax.axis_index("exp"), lax.axis_index("core")]).astype(jnp.int32)
    peers = lax.axis_size(torus)
    kept, given, columns, weight, rows, cot = opening(at, tokens, slot_weight, cotangent)
    taken = lax.ppermute(given, "core", swap)
    kept_grad, given_grad = grads_of(columns, cot)
    taken_grad = lax.ppermute(given_grad, "core", swap)
    logits, combine = combining(rows, weight)
    sent = merge(kept, taken, kept_grad, taken_grad, peers)
    got = lax.all_to_all(sent, torus, split_axis=0, concat_axis=0, tiled=True)
    told = expert(got, w_in, w_out)
    told = lax.all_to_all(told, torus, split_axis=0, concat_axis=0, tiled=True)
    pair = lax.ppermute(told, "core", swap)
    return tuple(closing(told, pair, rows, cot, combine, logits, weight))


def solution(mesh):
    exp = mesh.devices.shape[1]
    finer = Mesh(mesh.devices.reshape(4, 4, 2, exp), ("x", "z", "core", "exp"))
    every = ("x", "z", "core", "exp")
    rows = P(every, None)
    experts = P(every, None, None)
    return jax.shard_map(
        shards,
        mesh=finer,
        in_specs=(P(("x", "z", "core"), None), P(), experts, experts, rows),
        out_specs=(rows, rows),
        check_vma=False,
    )
```

```python
import functools

import jax
import jax.numpy as jnp
from jax import lax
from jax.experimental import pallas as pl
from jax.experimental.pallas import tpu as pltpu
from jax.sharding import Mesh
from jax.sharding import PartitionSpec as P

LOW = jnp.bfloat16
WIDE = jnp.float32
EXTRA = 128
LIMIT = 20 * 1024 * 1024


def product(left, right, left_dim, right_dim):
    return lax.dot_general(
        left, right, (((left_dim,), (right_dim,)), ((), ())), preferred_element_type=WIDE
    )


def split3(value):
    high = value.astype(LOW).astype(WIDE)
    rest = value - high
    mid = rest.astype(LOW).astype(WIDE)
    return [high, mid, rest - mid]


def place(pieces, shape, axis):
    index = lax.broadcasted_iota(jnp.int32, shape, axis)
    total = jnp.zeros(shape, WIDE)
    for at, piece in enumerate(pieces):
        total = jnp.where(index == at, piece, total)
    return total


def lanes(block, first):
    index = lax.broadcasted_iota(jnp.int32, block.shape, 1)
    inside = (index >= first) & (index < first + 3)
    return jnp.sum(jnp.where(inside, block, 0.0), axis=1, keepdims=True)


IN_SMEM = pl.BlockSpec(memory_space=pltpu.SMEM)
IN_VMEM = pl.BlockSpec(memory_space=pltpu.VMEM)
IN_HBM = pl.BlockSpec(memory_space=pltpu.HBM)


def stay(array):
    return pltpu.with_memory_space_constraint(array, pltpu.HBM)


SPAN = pl.CostEstimate(flops=9_000_000_000, bytes_accessed=20_000_000, transcendentals=0)


def call(kernel, name, args, specs, out_specs, out_shape, scratch=(), cost=None):
    return pl.pallas_call(
        kernel,
        in_specs=specs,
        out_specs=out_specs,
        out_shape=out_shape,
        scratch_shapes=scratch,
        compiler_params=pltpu.CompilerParams(vmem_limit_bytes=LIMIT),
        cost_estimate=cost,
        name=name,
    )(*args)


def ordering(core, slots):
    to = lax.broadcasted_iota(jnp.int32, (slots, 1), 0)
    source = lax.broadcasted_iota(jnp.int32, (slots, slots), 1)
    half = slots // 2
    within = to % half
    other = jnp.where(to // half == 0, core, 1 - core)
    wanted = (within // 8) * 16 + other * 8 + within % 8
    return (source == wanted).astype(WIDE).astype(LOW)


def halves(value, outs, columns):
    half = outs[0].shape[0]
    for at, out in enumerate(outs):
        out[:, columns] = value[at * half : (at + 1) * half].astype(LOW)


def opening_kernel(
    at_ref, tok_hbm, weight_hbm, cot_hbm,
    kept_ref, given_ref, logit_ref, order_ref, rows_ref, cot_ref,
    weight_ref, sems,
):
    slots = weight_ref.shape[1]
    count, width = rows_ref.shape
    start = pl.multiple_of(at_ref[0] * count, count)
    loads = [
        pltpu.make_async_copy(source, target, sems.at[at])
        for at, (source, target) in enumerate(
            (
                (weight_hbm, weight_ref),
                (tok_hbm.at[pl.ds(start, count)], rows_ref),
                (cot_hbm, cot_ref),
            )
        )
    ]
    loads[0].start()
    loads[1].start()
    order = ordering(at_ref[1], slots)
    loads[0].wait()
    weight = product(order, weight_ref[...], 1, 1).astype(LOW)
    order_ref[...] = weight
    loads[1].wait()
    loads[2].start()
    rows = rows_ref[...]
    logits = product(weight, rows, 1, 1)
    logit_ref[...] = logits
    slot_max = jnp.max(logits, axis=1, keepdims=True)
    shifted = jnp.exp(logits - slot_max)
    slot_sum = jnp.sum(shifted, axis=1, keepdims=True)
    outs = (kept_ref, given_ref)
    halves(product(shifted.astype(LOW), rows, 1, 0), outs, slice(0, width))
    pieces = place(split3(slot_max) + split3(slot_sum), (slots, EXTRA), 1)
    halves(pieces, outs, slice(width, width + EXTRA))
    loads[2].wait()


def opening(at, tokens, slot_weight, cotangent):
    rows, width = cotangent.shape
    slots = slot_weight.shape[1]
    shapes = [((slots // 2, width + EXTRA), LOW)] * 2 + [((slots, rows), WIDE)]
    shapes += [((slots, width), LOW)] + [((rows, width), LOW)] * 2
    return call(
        opening_kernel,
        "opening",
        (at, stay(tokens), stay(slot_weight), stay(cotangent)),
        [IN_SMEM] + [IN_HBM] * 3,
        [IN_VMEM] * len(shapes),
        [jax.ShapeDtypeStruct(*shape) for shape in shapes],
        [pltpu.VMEM((width, slots), LOW), pltpu.SemaphoreType.DMA((3,))],
    )


def grads_kernel(logit_ref, cot_ref, kept_ref, given_ref):
    logits = logit_ref[...]
    raised = jnp.exp(logits - jnp.max(logits, axis=0, keepdims=True))
    combine = raised * (1.0 / jnp.sum(raised, axis=0, keepdims=True))
    grad_part = product(combine.astype(LOW), cot_ref[...], 1, 0)
    halves(grad_part, (kept_ref, given_ref), slice(0, grad_part.shape[1]))


SIDE = pl.CostEstimate(flops=1_000_000_000, bytes_accessed=4_000_000, transcendentals=131_072)


def grads_of(logits, cotangent):
    shape = jax.ShapeDtypeStruct((logits.shape[0] // 2, cotangent.shape[1]), LOW)
    args = (logits, cotangent)
    return call(grads_kernel, "grads", args, [IN_VMEM] * 2, [IN_VMEM] * 2, [shape] * 2, (), SIDE)


def combine_kernel(rows_ref, order_ref, logit_ref, comb_ref):
    logits = product(rows_ref[...], order_ref[...], 1, 1)
    logit_ref[...] = logits
    raised = jnp.exp(logits - jnp.max(logits, axis=1, keepdims=True))
    comb_ref[...] = raised * (1.0 / jnp.sum(raised, axis=1, keepdims=True))


def combining(rows, order):
    shape = jax.ShapeDtypeStruct((rows.shape[0], order.shape[0]), WIDE)
    args = (rows, order)
    return call(
        combine_kernel, "combining", args, [IN_VMEM] * 2, [IN_VMEM] * 2, [shape] * 2, (), SIDE
    )


def merge_kernel(kept_ref, taken_ref, kept_grad_ref, taken_grad_ref, out_ref):
    width = kept_grad_ref.shape[1]
    kept, taken = kept_ref[:, width:].astype(WIDE), taken_ref[:, width:].astype(WIDE)
    kept_max, taken_max = lanes(kept, 0), lanes(taken, 0)
    top = jnp.maximum(kept_max, taken_max)
    kept_scale, taken_scale = jnp.exp(kept_max - top), jnp.exp(taken_max - top)
    total = kept_scale * lanes(kept, 3) + taken_scale * lanes(taken, 3)
    slots = kept_scale * kept_ref[:, :width].astype(WIDE) + taken_scale * taken_ref[
        :, :width
    ].astype(WIDE)
    grads = kept_grad_ref[...].astype(WIDE) + taken_grad_ref[...].astype(WIDE)
    pieces = place(split3(top) + split3(total), kept.shape, 1)
    peers, own = out_ref.shape[:2]
    out_ref[:, :, :width] = slots.astype(LOW).reshape(peers, own, width)
    out_ref[:, :, width : 2 * width] = grads.astype(LOW).reshape(peers, own, width)
    out_ref[:, :, 2 * width :] = pieces.astype(LOW).reshape(peers, own, EXTRA)


def merge(kept, taken, kept_grad, taken_grad, peers):
    wide = kept.shape[1] + kept_grad.shape[1]
    shape = jax.ShapeDtypeStruct((peers, kept.shape[0] // peers, wide), LOW)
    args = (kept, taken, kept_grad, taken_grad)
    return call(merge_kernel, "merge", args, [IN_VMEM] * 4, IN_VMEM, shape, (), SPAN)


PART = 256
FEW = 32


def two_rows(left, right_ref, first):
    columns = [[], []]
    for at in range(first, first + PART, FEW):
        right = right_ref[0, at : at + FEW, :].astype(WIDE)
        for row in range(2):
            columns[row].append(jnp.sum(left[row] * right, axis=1, keepdims=True))
    columns = [jnp.concatenate(column, axis=0) for column in columns]
    return place(columns, (PART, EXTRA), 1).T[:8]


def expert_kernel(got_ref, in_ref, out_ref, told_ref):
    peers, own, wide = got_ref.shape
    count, width = peers * own, in_ref.shape[1]
    got = got_ref[...].reshape(count, wide)
    pieces = got[:, 2 * width :].astype(WIDE)
    block_max, block_sum = lanes(pieces, 0), lanes(pieces, 3)
    odd = lax.broadcasted_iota(jnp.int32, (count, 1), 0) % 2 == 1
    lowest = jnp.full((count, 1), -jnp.inf, WIDE)
    top = [
        jnp.max(jnp.where(odd, lowest, block_max), axis=0, keepdims=True),
        jnp.max(jnp.where(odd, block_max, lowest), axis=0, keepdims=True),
    ]
    scale = jnp.exp(block_max - jnp.where(odd, top[1], top[0]))
    scaled_sum = scale * block_sum
    totals = [
        jnp.sum(jnp.where(odd, 0.0, scaled_sum), axis=0, keepdims=True),
        jnp.sum(jnp.where(odd, scaled_sum, 0.0), axis=0, keepdims=True),
    ]
    high = scale.astype(LOW).astype(WIDE)
    rest, ones = scale - high, jnp.ones_like(scale)
    columns = []
    for column in (high, rest, ones):
        columns += [jnp.where(odd, 0.0, column), jnp.where(odd, column, 0.0)]
    picks = place(columns, (count, EXTRA), 1).T[:8].astype(LOW)
    sums = product(picks, got[:, : 2 * width], 1, 0)
    sums_of = lambda row, part: sums[row : row + 1, part]
    front, back = slice(0, width), slice(width, 2 * width)
    exact = [(sums_of(row, front) + sums_of(row + 2, front)) / totals[row] for row in range(2)]
    exact = place(exact, (8, width), 0)
    out_grad = [sums_of(4, back).astype(LOW).astype(WIDE), sums_of(5, back).astype(LOW).astype(WIDE)]
    slot_low = exact.astype(LOW)
    rate = 0.7978845608028654
    slot_out = jnp.zeros((8, width), WIDE)
    in_grad = jnp.zeros((8, width), WIDE)
    for first in range(0, in_ref.shape[2], PART):
        part = slice(first, first + PART)
        preact = product(slot_low, in_ref[0, :, part], 1, 0)
        hid_grad = two_rows(out_grad, out_ref, first)
        square = preact * preact
        curve = jnp.tanh(rate * (preact + 0.044715 * square * preact))
        low_hidden = (0.5 * preact * (1.0 + curve)).astype(LOW)
        slope = 0.5 * (1.0 + curve) + 0.5 * preact * (1.0 - curve * curve) * rate * (
            1.0 + 3.0 * 0.044715 * square
        )
        slot_out += product(low_hidden, out_ref[0, part, :], 1, 0)
        in_grad += product((slope * hid_grad).astype(LOW), in_ref[0, :, part], 1, 1)
    slot_product = jnp.sum(exact * in_grad, axis=1, keepdims=True)
    top = place(top, (8, 1), 0)
    totals = place(totals, (8, 1), 0)
    scalars = place(split3(slot_product) + split3(top) + split3(totals), (8, EXTRA), 1)
    spread = lambda block: jnp.broadcast_to(
        block[:own].astype(LOW)[None], (peers, own, block.shape[1])
    )
    told_ref[:, :, :width] = spread(slot_out)
    told_ref[:, :, width : 2 * width] = spread(in_grad)
    told_ref[:, :, 2 * width :] = spread(scalars)


def expert(got, w_in, w_out):
    shape = jax.ShapeDtypeStruct(got.shape, LOW)
    return call(expert_kernel, "expert", (got, w_in, w_out), [IN_VMEM] * 3, IN_VMEM, shape)


STEPS = 2


def closing_kernel(
    mine_ref, pair_ref, tok_ref, cot_ref, comb_ref, logit_ref, order_ref,
    mixed_hbm, grad_hbm,
    all_out, in_low, rows_ref, mixed_ref, grad_ref, out_sems,
):
    count, width = cot_ref.shape
    half = mine_ref.shape[0] * mine_ref.shape[1]
    block = count // STEPS
    for at, ref in enumerate((mine_ref, pair_ref)):
        part = slice(at * half, (at + 1) * half)
        all_out[part, :] = ref[:, :, :width].reshape(half, width)
        in_low[part, :] = ref[:, :, width : 2 * width].reshape(half, width)
        pieces = ref[:, :, 2 * width :].reshape(half, EXTRA).astype(WIDE).T
        for row in range(3):
            rows_ref[row : row + 1, part] = jnp.sum(
                pieces[3 * row : 3 * row + 3], axis=0, keepdims=True
            )
    slot_product, highest, scale = rows_ref[0:1], rows_ref[1:2], 1.0 / rows_ref[2:3]
    stores = []
    for step in range(STEPS):
        part = pl.ds(step * block, block)
        stores.append(
            pltpu.make_async_copy(mixed_ref.at[part], mixed_hbm.at[part], out_sems.at[0, step])
        )
        stores.append(
            pltpu.make_async_copy(grad_ref.at[part], grad_hbm.at[part], out_sems.at[1, step])
        )
        combine = comb_ref[part]
        mixed_ref[part, :] = product(combine.astype(LOW), all_out[...], 1, 0).astype(LOW)
        stores[-2].start()
        comb_grad = product(cot_ref[part], all_out[...], 1, 1)
        logit_grad = combine * (comb_grad - jnp.sum(combine * comb_grad, axis=1, keepdims=True))
        dispatch = jnp.exp(logit_ref[part] - highest) * scale
        logit_grad += dispatch * (product(tok_ref[part], in_low[...], 1, 1) - slot_product)
        token_grad = product(logit_grad.astype(LOW), order_ref[...], 1, 0)
        token_grad += product(dispatch.astype(LOW), in_low[...], 1, 0)
        grad_ref[part, :] = token_grad.astype(LOW)
        stores[-1].start()
    for copy in stores:
        copy.wait()


def closing(mine, pair, tokens, cotangent, combine, logits, weight):
    rows, width = cotangent.shape
    slots = weight.shape[0]
    return call(
        closing_kernel,
        "closing",
        (mine, pair, tokens, cotangent, combine, logits, weight),
        [IN_VMEM] * 7,
        [IN_HBM] * 2,
        [jax.ShapeDtypeStruct((rows, width), LOW)] * 2,
        [
            pltpu.VMEM((slots, width), LOW),
            pltpu.VMEM((slots, width), LOW),
            pltpu.VMEM((8, slots), WIDE),
            pltpu.VMEM((rows, width), LOW),
            pltpu.VMEM((rows, width), LOW),
            pltpu.SemaphoreType.DMA((2, STEPS)),
        ],
    )


def shards(tokens, slot_weight, w_in, w_out, cotangent):
    torus = ("x", "z", "exp")
    swap = [(0, 1), (1, 0)]
    at = jnp.stack([lax.axis_index("exp"), lax.axis_index("core")]).astype(jnp.int32)
    peers = lax.axis_size(torus)
    kept, given, columns, weight, rows, cot = opening(at, tokens, slot_weight, cotangent)
    taken = lax.ppermute(given, "core", swap)
    kept_grad, given_grad = grads_of(columns, cot)
    taken_grad = lax.ppermute(given_grad, "core", swap)
    logits, combine = combining(rows, weight)
    sent = merge(kept, taken, kept_grad, taken_grad, peers)
    got = lax.all_to_all(sent, torus, split_axis=0, concat_axis=0, tiled=True)
    told = expert(got, w_in, w_out)
    told = lax.all_to_all(told, torus, split_axis=0, concat_axis=0, tiled=True)
    pair = lax.ppermute(told, "core", swap)
    return tuple(closing(told, pair, rows, cot, combine, logits, weight))


def solution(mesh):
    exp = mesh.devices.shape[1]
    finer = Mesh(mesh.devices.reshape(4, 4, 2, exp), ("x", "z", "core", "exp"))
    every = ("x", "z", "core", "exp")
    rows = P(every, None)
    experts = P(every, None, None)
    return jax.shard_map(
        shards,
        mesh=finer,
        in_specs=(P(("x", "z", "core"), None), P(), experts, experts, rows),
        out_specs=(rows, rows),
        check_vma=False,
    )
```

```python
import functools

import jax
import jax.numpy as jnp
from jax import lax
from jax.experimental import pallas as pl
from jax.experimental.pallas import tpu as pltpu
from jax.sharding import Mesh
from jax.sharding import PartitionSpec as P

LOW = jnp.bfloat16
WIDE = jnp.float32
EXTRA = 128
LIMIT = 20 * 1024 * 1024


def product(left, right, left_dim, right_dim):
    return lax.dot_general(
        left, right, (((left_dim,), (right_dim,)), ((), ())), preferred_element_type=WIDE
    )


def split3(value):
    high = value.astype(LOW).astype(WIDE)
    rest = value - high
    mid = rest.astype(LOW).astype(WIDE)
    return [high, mid, rest - mid]


def place(pieces, shape, axis):
    index = lax.broadcasted_iota(jnp.int32, shape, axis)
    total = jnp.zeros(shape, WIDE)
    for at, piece in enumerate(pieces):
        total = jnp.where(index == at, piece, total)
    return total


def lanes(block, first):
    index = lax.broadcasted_iota(jnp.int32, block.shape, 1)
    inside = (index >= first) & (index < first + 3)
    return jnp.sum(jnp.where(inside, block, 0.0), axis=1, keepdims=True)


IN_SMEM = pl.BlockSpec(memory_space=pltpu.SMEM)
IN_VMEM = pl.BlockSpec(memory_space=pltpu.VMEM)
IN_HBM = pl.BlockSpec(memory_space=pltpu.HBM)


def stay(array):
    return pltpu.with_memory_space_constraint(array, pltpu.HBM)


SPAN = pl.CostEstimate(flops=9_000_000_000, bytes_accessed=20_000_000, transcendentals=0)


def call(kernel, name, args, specs, out_specs, out_shape, scratch=(), cost=None):
    return pl.pallas_call(
        kernel,
        in_specs=specs,
        out_specs=out_specs,
        out_shape=out_shape,
        scratch_shapes=scratch,
        compiler_params=pltpu.CompilerParams(vmem_limit_bytes=LIMIT),
        cost_estimate=cost,
        name=name,
    )(*args)


def ordering(core, slots):
    to = lax.broadcasted_iota(jnp.int32, (slots, 1), 0)
    source = lax.broadcasted_iota(jnp.int32, (slots, slots), 1)
    half = slots // 2
    within = to % half
    other = jnp.where(to // half == 0, core, 1 - core)
    wanted = (within // 8) * 16 + other * 8 + within % 8
    return (source == wanted).astype(WIDE).astype(LOW)


def halves(value, outs, columns):
    half = outs[0].shape[0]
    for at, out in enumerate(outs):
        out[:, columns] = value[at * half : (at + 1) * half].astype(LOW)


def opening_kernel(
    at_ref, tok_hbm, weight_hbm, cot_hbm,
    kept_ref, given_ref, logit_ref, order_ref, rows_ref, cot_ref,
    weight_ref, sems,
):
    slots = weight_ref.shape[1]
    count, width = rows_ref.shape
    start = pl.multiple_of(at_ref[0] * count, count)
    block = width // 2
    parts = [pl.ds(at * block, block) for at in range(2)]
    loads = []
    for part in parts:
        source = tok_hbm.at[pl.ds(start, count), part]
        loads.append(pltpu.make_async_copy(weight_hbm.at[part], weight_ref.at[part], sems.at[len(loads)]))
        loads.append(pltpu.make_async_copy(source, rows_ref.at[:, part], sems.at[len(loads)]))
    loads.append(pltpu.make_async_copy(cot_hbm, cot_ref, sems.at[4]))
    for copy in loads[:4]:
        copy.start()
    order = ordering(at_ref[1], slots)
    logits = 0.0
    for at, part in enumerate(parts):
        loads[2 * at].wait()
        weight = product(order, weight_ref[part, :], 1, 1).astype(LOW)
        order_ref[:, part] = weight
        loads[2 * at + 1].wait()
        logits += product(weight, rows_ref[:, part], 1, 1)
    loads[4].start()
    rows = rows_ref[...]
    logit_ref[...] = logits
    slot_max = jnp.max(logits, axis=1, keepdims=True)
    shifted = jnp.exp(logits - slot_max)
    slot_sum = jnp.sum(shifted, axis=1, keepdims=True)
    outs = (kept_ref, given_ref)
    halves(product(shifted.astype(LOW), rows, 1, 0), outs, slice(0, width))
    pieces = place(split3(slot_max) + split3(slot_sum), (slots, EXTRA), 1)
    halves(pieces, outs, slice(width, width + EXTRA))
    loads[4].wait()


def opening(at, tokens, slot_weight, cotangent):
    rows, width = cotangent.shape
    slots = slot_weight.shape[1]
    shapes = [((slots // 2, width + EXTRA), LOW)] * 2 + [((slots, rows), WIDE)]
    shapes += [((slots, width), LOW)] + [((rows, width), LOW)] * 2
    return call(
        opening_kernel,
        "opening",
        (at, stay(tokens), stay(slot_weight), stay(cotangent)),
        [IN_SMEM] + [IN_HBM] * 3,
        [IN_VMEM] * len(shapes),
        [jax.ShapeDtypeStruct(*shape) for shape in shapes],
        [pltpu.VMEM((width, slots), LOW), pltpu.SemaphoreType.DMA((5,))],
    )


def grads_kernel(logit_ref, cot_ref, kept_ref, given_ref):
    logits = logit_ref[...]
    raised = jnp.exp(logits - jnp.max(logits, axis=0, keepdims=True))
    combine = raised * (1.0 / jnp.sum(raised, axis=0, keepdims=True))
    grad_part = product(combine.astype(LOW), cot_ref[...], 1, 0)
    halves(grad_part, (kept_ref, given_ref), slice(0, grad_part.shape[1]))


SIDE = pl.CostEstimate(flops=1_000_000_000, bytes_accessed=4_000_000, transcendentals=131_072)


def grads_of(logits, cotangent):
    shape = jax.ShapeDtypeStruct((logits.shape[0] // 2, cotangent.shape[1]), LOW)
    args = (logits, cotangent)
    return call(grads_kernel, "grads", args, [IN_VMEM] * 2, [IN_VMEM] * 2, [shape] * 2, (), SIDE)


def combine_kernel(rows_ref, order_ref, logit_ref, comb_ref):
    logits = product(rows_ref[...], order_ref[...], 1, 1)
    logit_ref[...] = logits
    raised = jnp.exp(logits - jnp.max(logits, axis=1, keepdims=True))
    comb_ref[...] = raised * (1.0 / jnp.sum(raised, axis=1, keepdims=True))


def combining(rows, order):
    shape = jax.ShapeDtypeStruct((rows.shape[0], order.shape[0]), WIDE)
    args = (rows, order)
    return call(
        combine_kernel, "combining", args, [IN_VMEM] * 2, [IN_VMEM] * 2, [shape] * 2, (), SIDE
    )


def merge_kernel(kept_ref, taken_ref, kept_grad_ref, taken_grad_ref, out_ref):
    width = kept_grad_ref.shape[1]
    kept, taken = kept_ref[:, width:].astype(WIDE), taken_ref[:, width:].astype(WIDE)
    kept_max, taken_max = lanes(kept, 0), lanes(taken, 0)
    top = jnp.maximum(kept_max, taken_max)
    kept_scale, taken_scale = jnp.exp(kept_max - top), jnp.exp(taken_max - top)
    total = kept_scale * lanes(kept, 3) + taken_scale * lanes(taken, 3)
    slots = kept_scale * kept_ref[:, :width].astype(WIDE) + taken_scale * taken_ref[
        :, :width
    ].astype(WIDE)
    grads = kept_grad_ref[...].astype(WIDE) + taken_grad_ref[...].astype(WIDE)
    pieces = place(split3(top) + split3(total), kept.shape, 1)
    peers, own = out_ref.shape[:2]
    out_ref[:, :, :width] = slots.astype(LOW).reshape(peers, own, width)
    out_ref[:, :, width : 2 * width] = grads.astype(LOW).reshape(peers, own, width)
    out_ref[:, :, 2 * width :] = pieces.astype(LOW).reshape(peers, own, EXTRA)


def merge(kept, taken, kept_grad, taken_grad, peers):
    wide = kept.shape[1] + kept_grad.shape[1]
    shape = jax.ShapeDtypeStruct((peers, kept.shape[0] // peers, wide), LOW)
    args = (kept, taken, kept_grad, taken_grad)
    return call(merge_kernel, "merge", args, [IN_VMEM] * 4, IN_VMEM, shape, (), SPAN)


def expert_kernel(got_ref, in_ref, out_ref, told_ref):
    w_in, w_out = in_ref[0], out_ref[0]
    peers, own, wide = got_ref.shape
    count, width = peers * own, w_in.shape[0]
    spread = lambda block: jnp.broadcast_to(
        block[:own].astype(LOW)[None], (peers, own, block.shape[1])
    )
    index = lambda axis: lax.broadcasted_iota(jnp.int32, (8, count), axis)
    picks = (index(1) % 2 == index(0)).astype(WIDE).astype(LOW)
    grads = got_ref[:, :, width : 2 * width].reshape(count, width)
    out_grad = product(picks, grads, 1, 0).astype(LOW)
    hid_grad = product(out_grad, w_out, 1, 1)
    pieces = got_ref[:, :, 2 * width :].reshape(count, EXTRA).astype(WIDE)
    block_max, block_sum = lanes(pieces, 0), lanes(pieces, 3)
    odd = lax.broadcasted_iota(jnp.int32, (count, 1), 0) % 2 == 1
    lowest = jnp.full((count, 1), -jnp.inf, WIDE)
    top = [
        jnp.max(jnp.where(odd, lowest, block_max), axis=0, keepdims=True),
        jnp.max(jnp.where(odd, block_max, lowest), axis=0, keepdims=True),
    ]
    scale = jnp.exp(block_max - jnp.where(odd, top[1], top[0]))
    scaled_sum = scale * block_sum
    totals = [
        jnp.sum(jnp.where(odd, 0.0, scaled_sum), axis=0, keepdims=True),
        jnp.sum(jnp.where(odd, scaled_sum, 0.0), axis=0, keepdims=True),
    ]
    high = scale.astype(LOW).astype(WIDE)
    columns = []
    for column in (high, scale - high):
        columns += [jnp.where(odd, 0.0, column), jnp.where(odd, column, 0.0)]
    picks = place(columns, (count, EXTRA), 1).T[:8].astype(LOW)
    sums = product(picks, got_ref[:, :, :width].reshape(count, width), 1, 0)
    exact = [(sums[row : row + 1] + sums[row + 2 : row + 3]) / totals[row] for row in range(2)]
    exact = place(exact, (8, width), 0)
    preact = product(exact.astype(LOW), w_in, 1, 0)
    rate = 0.7978845608028654
    square = preact * preact
    curve = jnp.tanh(rate * (preact + 0.044715 * square * preact))
    low_hidden = (0.5 * preact * (1.0 + curve)).astype(LOW)
    slope = 0.5 * (1.0 + curve) + 0.5 * preact * (1.0 - curve * curve) * rate * (
        1.0 + 3.0 * 0.044715 * square
    )
    told_ref[:, :, :width] = spread(product(low_hidden, w_out, 1, 0))
    in_grad = product((slope * hid_grad).astype(LOW), w_in, 1, 1)
    told_ref[:, :, width : 2 * width] = spread(in_grad)
    slot_product = jnp.sum(exact * in_grad, axis=1, keepdims=True)
    top = place(top, (8, 1), 0)
    totals = place(totals, (8, 1), 0)
    scalars = place(split3(slot_product) + split3(top) + split3(totals), (8, EXTRA), 1)
    told_ref[:, :, 2 * width :] = spread(scalars)


def expert(got, w_in, w_out):
    shape = jax.ShapeDtypeStruct(got.shape, LOW)
    return call(expert_kernel, "expert", (got, w_in, w_out), [IN_VMEM] * 3, IN_VMEM, shape)


STEPS = 2


def closing_kernel(
    mine_ref, pair_ref, tok_ref, cot_ref, comb_ref, logit_ref, order_ref,
    mixed_hbm, grad_hbm,
    all_out, in_low, rows_ref, mixed_ref, grad_ref, sems,
):
    count, width = cot_ref.shape
    half = mine_ref.shape[0] * mine_ref.shape[1]
    block = count // STEPS
    parts = [pl.ds(step * block, block) for step in range(STEPS)]
    sides = [(slice(0, half), mine_ref), (slice(half, 2 * half), pair_ref)]
    stores = []

    def store(source, target, where):
        at = len(stores)
        stores.append(pltpu.make_async_copy(source.at[where], target.at[where], sems.at[at]))
        stores[at].start()

    for side, ref in sides:
        all_out[side, :] = ref[:, :, :width].reshape(half, width)
    combs = []
    for part in parts:
        combine = comb_ref[part]
        mixed_ref[part, :] = product(combine.astype(LOW), all_out[...], 1, 0).astype(LOW)
        store(mixed_ref, mixed_hbm, part)
        comb_grad = product(cot_ref[part], all_out[...], 1, 1)
        mean = jnp.sum(combine * comb_grad, axis=1, keepdims=True)
        combs.append(combine * (comb_grad - mean))
    for side, ref in sides:
        in_low[side, :] = ref[:, :, width : 2 * width].reshape(half, width)
        pieces = ref[:, :, 2 * width :].reshape(half, EXTRA).astype(WIDE).T
        for row in range(3):
            rows_ref[row : row + 1, side] = jnp.sum(
                pieces[3 * row : 3 * row + 3], axis=0, keepdims=True
            )
    slot_product, highest, scale = rows_ref[0:1], rows_ref[1:2], 1.0 / rows_ref[2:3]
    for step, part in enumerate(parts):
        dispatch = jnp.exp(logit_ref[part] - highest) * scale
        logit_grad = combs[step] + dispatch * (
            product(tok_ref[part], in_low[...], 1, 1) - slot_product
        )
        logit_grad, dispatch = logit_grad.astype(LOW), dispatch.astype(LOW)
        cuts = [0, width] if step + 1 < STEPS else [0, width - 256, width]
        for first, last in zip(cuts, cuts[1:]):
            columns = slice(first, last)
            token_grad = product(logit_grad, order_ref[:, columns], 1, 0)
            token_grad += product(dispatch, in_low[:, columns], 1, 0)
            grad_ref[part, columns] = token_grad.astype(LOW)
            store(grad_ref, grad_hbm, (part, pl.ds(first, last - first)))
    for copy in stores:
        copy.wait()


def closing(mine, pair, tokens, cotangent, combine, logits, weight):
    rows, width = cotangent.shape
    slots = weight.shape[0]
    return call(
        closing_kernel,
        "closing",
        (mine, pair, tokens, cotangent, combine, logits, weight),
        [IN_VMEM] * 7,
        [IN_HBM] * 2,
        [jax.ShapeDtypeStruct((rows, width), LOW)] * 2,
        [
            pltpu.VMEM((slots, width), LOW),
            pltpu.VMEM((slots, width), LOW),
            pltpu.VMEM((8, slots), WIDE),
            pltpu.VMEM((rows, width), LOW),
            pltpu.VMEM((rows, width), LOW),
            pltpu.SemaphoreType.DMA((2 * STEPS + 1,)),
        ],
    )


def shards(tokens, slot_weight, w_in, w_out, cotangent):
    torus = ("x", "z", "exp")
    swap = [(0, 1), (1, 0)]
    at = jnp.stack([lax.axis_index("exp"), lax.axis_index("core")]).astype(jnp.int32)
    peers = lax.axis_size(torus)
    kept, given, columns, weight, rows, cot = opening(at, tokens, slot_weight, cotangent)
    taken = lax.ppermute(given, "core", swap)
    kept_grad, given_grad = grads_of(columns, cot)
    taken_grad = lax.ppermute(given_grad, "core", swap)
    logits, combine = combining(rows, weight)
    sent = merge(kept, taken, kept_grad, taken_grad, peers)
    got = lax.all_to_all(sent, torus, split_axis=0, concat_axis=0, tiled=True)
    told = expert(got, w_in, w_out)
    told = lax.all_to_all(told, torus, split_axis=0, concat_axis=0, tiled=True)
    pair = lax.ppermute(told, "core", swap)
    return tuple(closing(told, pair, rows, cot, combine, logits, weight))


def solution(mesh):
    exp = mesh.devices.shape[1]
    finer = Mesh(mesh.devices.reshape(4, 4, 2, exp), ("x", "z", "core", "exp"))
    every = ("x", "z", "core", "exp")
    rows = P(every, None)
    experts = P(every, None, None)
    return jax.shard_map(
        shards,
        mesh=finer,
        in_specs=(P(("x", "z", "core"), None), P(), experts, experts, rows),
        out_specs=(rows, rows),
        check_vma=False,
    )
```

```python
import functools

import jax
import jax.numpy as jnp
from jax import lax
from jax.experimental import pallas as pl
from jax.experimental.pallas import tpu as pltpu
from jax.sharding import Mesh
from jax.sharding import PartitionSpec as P

LOW = jnp.bfloat16
WIDE = jnp.float32
EXTRA = 128
LIMIT = 20 * 1024 * 1024


def product(left, right, left_dim, right_dim):
    return lax.dot_general(
        left, right, (((left_dim,), (right_dim,)), ((), ())), preferred_element_type=WIDE
    )


def split3(value):
    high = value.astype(LOW).astype(WIDE)
    rest = value - high
    mid = rest.astype(LOW).astype(WIDE)
    return [high, mid, rest - mid]


def place(pieces, shape, axis):
    index = lax.broadcasted_iota(jnp.int32, shape, axis)
    total = jnp.zeros(shape, WIDE)
    for at, piece in enumerate(pieces):
        total = jnp.where(index == at, piece, total)
    return total


def lanes(block, first):
    index = lax.broadcasted_iota(jnp.int32, block.shape, 1)
    inside = (index >= first) & (index < first + 3)
    return jnp.sum(jnp.where(inside, block, 0.0), axis=1, keepdims=True)


IN_SMEM = pl.BlockSpec(memory_space=pltpu.SMEM)
IN_VMEM = pl.BlockSpec(memory_space=pltpu.VMEM)
IN_HBM = pl.BlockSpec(memory_space=pltpu.HBM)


def stay(array):
    return pltpu.with_memory_space_constraint(array, pltpu.HBM)


SPAN = pl.CostEstimate(flops=9_000_000_000, bytes_accessed=20_000_000, transcendentals=0)


def call(kernel, name, args, specs, out_specs, out_shape, scratch=(), cost=None):
    return pl.pallas_call(
        kernel,
        in_specs=specs,
        out_specs=out_specs,
        out_shape=out_shape,
        scratch_shapes=scratch,
        compiler_params=pltpu.CompilerParams(vmem_limit_bytes=LIMIT),
        cost_estimate=cost,
        name=name,
    )(*args)


def ordering(core, slots):
    to = lax.broadcasted_iota(jnp.int32, (slots, 1), 0)
    source = lax.broadcasted_iota(jnp.int32, (slots, slots), 1)
    half = slots // 2
    within = to % half
    other = jnp.where(to // half == 0, core, 1 - core)
    wanted = (within // 8) * 16 + other * 8 + within % 8
    return (source == wanted).astype(WIDE).astype(LOW)


def halves(value, outs, columns):
    half = outs[0].shape[0]
    for at, out in enumerate(outs):
        out[:, columns] = value[at * half : (at + 1) * half].astype(LOW)


def opening_kernel(
    at_ref, tok_hbm, weight_hbm, cot_hbm,
    kept_ref, given_ref, logit_ref, order_ref, rows_ref, cot_ref,
    weight_ref, sems,
):
    slots = weight_ref.shape[1]
    count, width = rows_ref.shape
    start = pl.multiple_of(at_ref[0] * count, count)
    block = count // 4
    parts = [pl.ds(at * block, block) for at in range(4)]
    loads = [pltpu.make_async_copy(weight_hbm, weight_ref, sems.at[0])]
    for at, part in enumerate(parts):
        source = tok_hbm.at[pl.ds(start + at * block, block)]
        loads.append(pltpu.make_async_copy(source, rows_ref.at[part], sems.at[1 + at]))
    loads.append(pltpu.make_async_copy(cot_hbm, cot_ref, sems.at[5]))
    for copy in loads[:5]:
        copy.start()
    order = ordering(at_ref[1], slots)
    loads[0].wait()
    weight = product(order, weight_ref[...], 1, 1).astype(LOW)
    order_ref[...] = weight
    for copy in loads[1:5]:
        copy.wait()
    loads[5].start()
    rows = rows_ref[...]
    logits = product(weight, rows, 1, 1)
    logit_ref[...] = logits
    slot_max = jnp.max(logits, axis=1, keepdims=True)
    shifted = jnp.exp(logits - slot_max)
    slot_sum = jnp.sum(shifted, axis=1, keepdims=True)
    outs = (kept_ref, given_ref)
    halves(product(shifted.astype(LOW), rows, 1, 0), outs, slice(0, width))
    pieces = place(split3(slot_max) + split3(slot_sum), (slots, EXTRA), 1)
    halves(pieces, outs, slice(width, width + EXTRA))
    loads[5].wait()


def opening(at, tokens, slot_weight, cotangent):
    rows, width = cotangent.shape
    slots = slot_weight.shape[1]
    shapes = [((slots // 2, width + EXTRA), LOW)] * 2 + [((slots, rows), WIDE)]
    shapes += [((slots, width), LOW)] + [((rows, width), LOW)] * 2
    return call(
        opening_kernel,
        "opening",
        (at, stay(tokens), stay(slot_weight), stay(cotangent)),
        [IN_SMEM] + [IN_HBM] * 3,
        [IN_VMEM] * len(shapes),
        [jax.ShapeDtypeStruct(*shape) for shape in shapes],
        [pltpu.VMEM((width, slots), LOW), pltpu.SemaphoreType.DMA((6,))],
    )


def grads_kernel(logit_ref, cot_ref, kept_ref, given_ref):
    logits = logit_ref[...]
    raised = jnp.exp(logits - jnp.max(logits, axis=0, keepdims=True))
    combine = raised * (1.0 / jnp.sum(raised, axis=0, keepdims=True))
    grad_part = product(combine.astype(LOW), cot_ref[...], 1, 0)
    halves(grad_part, (kept_ref, given_ref), slice(0, grad_part.shape[1]))


SIDE = pl.CostEstimate(flops=1_000_000_000, bytes_accessed=4_000_000, transcendentals=131_072)


def grads_of(logits, cotangent):
    shape = jax.ShapeDtypeStruct((logits.shape[0] // 2, cotangent.shape[1]), LOW)
    args = (logits, cotangent)
    return call(grads_kernel, "grads", args, [IN_VMEM] * 2, [IN_VMEM] * 2, [shape] * 2, (), SIDE)


def combine_kernel(rows_ref, order_ref, logit_ref, comb_ref):
    logits = product(rows_ref[...], order_ref[...], 1, 1)
    logit_ref[...] = logits
    raised = jnp.exp(logits - jnp.max(logits, axis=1, keepdims=True))
    comb_ref[...] = raised * (1.0 / jnp.sum(raised, axis=1, keepdims=True))


def combining(rows, order):
    shape = jax.ShapeDtypeStruct((rows.shape[0], order.shape[0]), WIDE)
    args = (rows, order)
    return call(
        combine_kernel, "combining", args, [IN_VMEM] * 2, [IN_VMEM] * 2, [shape] * 2, (), SIDE
    )


def merge_slots_kernel(kept_ref, taken_ref, out_ref):
    peers, own, wide = out_ref.shape
    width = kept_ref.shape[1] - EXTRA
    kept, taken = kept_ref[:, width:].astype(WIDE), taken_ref[:, width:].astype(WIDE)
    kept_max, taken_max = lanes(kept, 0), lanes(taken, 0)
    top = jnp.maximum(kept_max, taken_max)
    kept_scale, taken_scale = jnp.exp(kept_max - top), jnp.exp(taken_max - top)
    total = kept_scale * lanes(kept, 3) + taken_scale * lanes(taken, 3)
    slots = kept_scale * kept_ref[:, :width].astype(WIDE) + taken_scale * taken_ref[
        :, :width
    ].astype(WIDE)
    pieces = place(split3(top) + split3(total), kept.shape, 1)
    out_ref[:, :, :width] = slots.astype(LOW).reshape(peers, own, width)
    out_ref[:, :, wide - EXTRA :] = pieces.astype(LOW).reshape(peers, own, EXTRA)


def merge_grads_kernel(sent_ref, kept_ref, taken_ref, out_ref):
    peers, own = out_ref.shape[:2]
    width = kept_ref.shape[1]
    grads = kept_ref[...].astype(WIDE) + taken_ref[...].astype(WIDE)
    out_ref[:, :, width : 2 * width] = grads.astype(LOW).reshape(peers, own, width)


def merge_slots(kept, taken, width, peers):
    shape = jax.ShapeDtypeStruct((peers, kept.shape[0] // peers, kept.shape[1] + width), LOW)
    args = (kept, taken)
    return call(merge_slots_kernel, "merge_slots", args, [IN_VMEM] * 2, IN_VMEM, shape, (), SIDE)


def merge_grads(sent, kept, taken):
    return pl.pallas_call(
        merge_grads_kernel,
        in_specs=[IN_VMEM] * 3,
        out_specs=IN_VMEM,
        out_shape=jax.ShapeDtypeStruct(sent.shape, LOW),
        input_output_aliases={0: 0},
        compiler_params=pltpu.CompilerParams(vmem_limit_bytes=LIMIT),
        cost_estimate=SPAN,
        name="merge_grads",
    )(sent, kept, taken)


PART = 512


def expert_kernel(got_ref, in_ref, out_ref, told_ref):
    peers, own, wide = got_ref.shape
    count, width = peers * own, in_ref.shape[1]
    got = got_ref[...].reshape(count, wide)
    pieces = got[:, 2 * width :].astype(WIDE)
    block_max, block_sum = lanes(pieces, 0), lanes(pieces, 3)
    odd = lax.broadcasted_iota(jnp.int32, (count, 1), 0) % 2 == 1
    lowest = jnp.full((count, 1), -jnp.inf, WIDE)
    top = [
        jnp.max(jnp.where(odd, lowest, block_max), axis=0, keepdims=True),
        jnp.max(jnp.where(odd, block_max, lowest), axis=0, keepdims=True),
    ]
    scale = jnp.exp(block_max - jnp.where(odd, top[1], top[0]))
    scaled_sum = scale * block_sum
    totals = [
        jnp.sum(jnp.where(odd, 0.0, scaled_sum), axis=0, keepdims=True),
        jnp.sum(jnp.where(odd, scaled_sum, 0.0), axis=0, keepdims=True),
    ]
    high = scale.astype(LOW).astype(WIDE)
    rest, ones = scale - high, jnp.ones_like(scale)
    columns = []
    for column in (high, rest, ones):
        columns += [jnp.where(odd, 0.0, column), jnp.where(odd, column, 0.0)]
    picks = place(columns, (count, EXTRA), 1).T[:8].astype(LOW)
    sums = product(picks, got[:, : 2 * width], 1, 0)
    sums_of = lambda row, part: sums[row : row + 1, part]
    front, back = slice(0, width), slice(width, 2 * width)
    exact = [(sums_of(row, front) + sums_of(row + 2, front)) / totals[row] for row in range(2)]
    exact = place(exact, (8, width), 0)
    out_grad = place([sums_of(4, back), sums_of(5, back)], (8, width), 0).astype(LOW)
    slot_low = exact.astype(LOW)
    rate = 0.7978845608028654
    slot_out = jnp.zeros((8, width), WIDE)
    in_grad = jnp.zeros((8, width), WIDE)
    for first in range(0, in_ref.shape[2], PART):
        part = slice(first, first + PART)
        preact = product(slot_low, in_ref[0, :, part], 1, 0)
        hid_grad = product(out_grad, out_ref[0, part, :], 1, 1)
        square = preact * preact
        curve = jnp.tanh(rate * (preact + 0.044715 * square * preact))
        low_hidden = (0.5 * preact * (1.0 + curve)).astype(LOW)
        slope = 0.5 * (1.0 + curve) + 0.5 * preact * (1.0 - curve * curve) * rate * (
            1.0 + 3.0 * 0.044715 * square
        )
        slot_out += product(low_hidden, out_ref[0, part, :], 1, 0)
        in_grad += product((slope * hid_grad).astype(LOW), in_ref[0, :, part], 1, 1)
    slot_product = jnp.sum(exact * in_grad, axis=1, keepdims=True)
    top = place(top, (8, 1), 0)
    totals = place(totals, (8, 1), 0)
    scalars = place(split3(slot_product) + split3(top) + split3(totals), (8, EXTRA), 1)
    spread = lambda block: jnp.broadcast_to(
        block[:own].astype(LOW)[None], (peers, own, block.shape[1])
    )
    told_ref[:, :, :width] = spread(slot_out)
    told_ref[:, :, width : 2 * width] = spread(in_grad)
    told_ref[:, :, 2 * width :] = spread(scalars)


def expert(got, w_in, w_out):
    shape = jax.ShapeDtypeStruct(got.shape, LOW)
    return call(expert_kernel, "expert", (got, w_in, w_out), [IN_VMEM] * 3, IN_VMEM, shape)


STEPS = 2


def closing_kernel(
    mine_ref, pair_ref, tok_ref, cot_ref, comb_ref, logit_ref, order_ref,
    mixed_hbm, grad_hbm,
    all_out, in_low, rows_ref, mixed_ref, grad_ref, out_sems,
):
    count, width = cot_ref.shape
    half = mine_ref.shape[0] * mine_ref.shape[1]
    block = count // STEPS
    for at, ref in enumerate((mine_ref, pair_ref)):
        part = slice(at * half, (at + 1) * half)
        all_out[part, :] = ref[:, :, :width].reshape(half, width)
        in_low[part, :] = ref[:, :, width : 2 * width].reshape(half, width)
        pieces = ref[:, :, 2 * width :].reshape(half, EXTRA).astype(WIDE).T
        for row in range(3):
            rows_ref[row : row + 1, part] = jnp.sum(
                pieces[3 * row : 3 * row + 3], axis=0, keepdims=True
            )
    slot_product, highest, scale = rows_ref[0:1], rows_ref[1:2], 1.0 / rows_ref[2:3]
    stores = []
    for step in range(STEPS):
        part = pl.ds(step * block, block)
        stores.append(
            pltpu.make_async_copy(mixed_ref.at[part], mixed_hbm.at[part], out_sems.at[0, step])
        )
        stores.append(
            pltpu.make_async_copy(grad_ref.at[part], grad_hbm.at[part], out_sems.at[1, step])
        )
        combine = comb_ref[part]
        mixed_ref[part, :] = product(combine.astype(LOW), all_out[...], 1, 0).astype(LOW)
        stores[-2].start()
        comb_grad = product(cot_ref[part], all_out[...], 1, 1)
        logit_grad = combine * (comb_grad - jnp.sum(combine * comb_grad, axis=1, keepdims=True))
        dispatch = jnp.exp(logit_ref[part] - highest) * scale
        logit_grad += dispatch * (product(tok_ref[part], in_low[...], 1, 1) - slot_product)
        token_grad = product(logit_grad.astype(LOW), order_ref[...], 1, 0)
        token_grad += product(dispatch.astype(LOW), in_low[...], 1, 0)
        grad_ref[part, :] = token_grad.astype(LOW)
        stores[-1].start()
    for copy in stores:
        copy.wait()


def closing(mine, pair, tokens, cotangent, combine, logits, weight):
    rows, width = cotangent.shape
    slots = weight.shape[0]
    return call(
        closing_kernel,
        "closing",
        (mine, pair, tokens, cotangent, combine, logits, weight),
        [IN_VMEM] * 7,
        [IN_HBM] * 2,
        [jax.ShapeDtypeStruct((rows, width), LOW)] * 2,
        [
            pltpu.VMEM((slots, width), LOW),
            pltpu.VMEM((slots, width), LOW),
            pltpu.VMEM((8, slots), WIDE),
            pltpu.VMEM((rows, width), LOW),
            pltpu.VMEM((rows, width), LOW),
            pltpu.SemaphoreType.DMA((2, STEPS)),
        ],
    )


def shards(tokens, slot_weight, w_in, w_out, cotangent):
    torus = ("x", "z", "exp")
    swap = [(0, 1), (1, 0)]
    at = jnp.stack([lax.axis_index("exp"), lax.axis_index("core")]).astype(jnp.int32)
    peers = lax.axis_size(torus)
    kept, given, columns, weight, rows, cot = opening(at, tokens, slot_weight, cotangent)
    taken = lax.ppermute(given, "core", swap)
    kept_grad, given_grad = grads_of(columns, cot)
    taken_grad = lax.ppermute(given_grad, "core", swap)
    logits, combine = combining(rows, weight)
    sent = merge_grads(
        merge_slots(kept, taken, cotangent.shape[1], peers), kept_grad, taken_grad
    )
    got = lax.all_to_all(sent, torus, split_axis=0, concat_axis=0, tiled=True)
    told = expert(got, w_in, w_out)
    told = lax.all_to_all(told, torus, split_axis=0, concat_axis=0, tiled=True)
    pair = lax.ppermute(told, "core", swap)
    return tuple(closing(told, pair, rows, cot, combine, logits, weight))


def solution(mesh):
    exp = mesh.devices.shape[1]
    finer = Mesh(mesh.devices.reshape(4, 4, 2, exp), ("x", "z", "core", "exp"))
    every = ("x", "z", "core", "exp")
    rows = P(every, None)
    experts = P(every, None, None)
    return jax.shard_map(
        shards,
        mesh=finer,
        in_specs=(P(("x", "z", "core"), None), P(), experts, experts, rows),
        out_specs=(rows, rows),
        check_vma=False,
    )
```

```python
import functools

import jax
import jax.numpy as jnp
from jax import lax
from jax.experimental import pallas as pl
from jax.experimental.pallas import tpu as pltpu
from jax.sharding import Mesh
from jax.sharding import PartitionSpec as P

LOW = jnp.bfloat16
WIDE = jnp.float32
EXTRA = 128
LIMIT = 20 * 1024 * 1024


def product(left, right, left_dim, right_dim):
    return lax.dot_general(
        left, right, (((left_dim,), (right_dim,)), ((), ())), preferred_element_type=WIDE
    )


def split3(value):
    high = value.astype(LOW).astype(WIDE)
    rest = value - high
    mid = rest.astype(LOW).astype(WIDE)
    return [high, mid, rest - mid]


def place(pieces, shape, axis):
    index = lax.broadcasted_iota(jnp.int32, shape, axis)
    total = jnp.zeros(shape, WIDE)
    for at, piece in enumerate(pieces):
        total = jnp.where(index == at, piece, total)
    return total


def lanes(block, first):
    index = lax.broadcasted_iota(jnp.int32, block.shape, 1)
    inside = (index >= first) & (index < first + 3)
    return jnp.sum(jnp.where(inside, block, 0.0), axis=1, keepdims=True)


IN_SMEM = pl.BlockSpec(memory_space=pltpu.SMEM)
IN_VMEM = pl.BlockSpec(memory_space=pltpu.VMEM)
IN_HBM = pl.BlockSpec(memory_space=pltpu.HBM)


def stay(array):
    return pltpu.with_memory_space_constraint(array, pltpu.HBM)


SPAN = pl.CostEstimate(flops=9_000_000_000, bytes_accessed=20_000_000, transcendentals=0)


def call(kernel, name, args, specs, out_specs, out_shape, scratch=(), cost=None):
    return pl.pallas_call(
        kernel,
        in_specs=specs,
        out_specs=out_specs,
        out_shape=out_shape,
        scratch_shapes=scratch,
        compiler_params=pltpu.CompilerParams(vmem_limit_bytes=LIMIT),
        cost_estimate=cost,
        name=name,
    )(*args)


def ordering(core, slots):
    to = lax.broadcasted_iota(jnp.int32, (slots, 1), 0)
    source = lax.broadcasted_iota(jnp.int32, (slots, slots), 1)
    half = slots // 2
    within = to % half
    other = jnp.where(to // half == 0, core, 1 - core)
    wanted = (within // 8) * 16 + other * 8 + within % 8
    return (source == wanted).astype(WIDE).astype(LOW)


def halves(value, outs, columns):
    half = outs[0].shape[0]
    for at, out in enumerate(outs):
        out[:, columns] = value[at * half : (at + 1) * half].astype(LOW)


def opening_kernel(
    at_ref, tok_hbm, weight_hbm, cot_hbm,
    kept_ref, given_ref, logit_ref, order_ref, rows_ref, cot_ref,
    weight_ref, sems,
):
    slots = weight_ref.shape[1]
    count, width = rows_ref.shape
    start = pl.multiple_of(at_ref[0] * count, count)
    block = count // 4
    parts = [pl.ds(at * block, block) for at in range(4)]
    loads = [pltpu.make_async_copy(weight_hbm, weight_ref, sems.at[0])]
    for at, part in enumerate(parts):
        source = tok_hbm.at[pl.ds(start + at * block, block)]
        loads.append(pltpu.make_async_copy(source, rows_ref.at[part], sems.at[1 + at]))
    loads.append(pltpu.make_async_copy(cot_hbm, cot_ref, sems.at[5]))
    for copy in loads[:5]:
        copy.start()
    order = ordering(at_ref[1], slots)
    loads[0].wait()
    weight = product(order, weight_ref[...], 1, 1).astype(LOW)
    order_ref[...] = weight
    for copy in loads[1:5]:
        copy.wait()
    loads[5].start()
    rows = rows_ref[...]
    logits = product(weight, rows, 1, 1)
    logit_ref[...] = logits
    slot_max = jnp.max(logits, axis=1, keepdims=True)
    shifted = jnp.exp(logits - slot_max)
    slot_sum = jnp.sum(shifted, axis=1, keepdims=True)
    outs = (kept_ref, given_ref)
    halves(product(shifted.astype(LOW), rows, 1, 0), outs, slice(0, width))
    pieces = place(split3(slot_max) + split3(slot_sum), (slots, EXTRA), 1)
    halves(pieces, outs, slice(width, width + EXTRA))
    loads[5].wait()


def opening(at, tokens, slot_weight, cotangent):
    rows, width = cotangent.shape
    slots = slot_weight.shape[1]
    shapes = [((slots // 2, width + EXTRA), LOW)] * 2 + [((slots, rows), WIDE)]
    shapes += [((slots, width), LOW)] + [((rows, width), LOW)] * 2
    return call(
        opening_kernel,
        "opening",
        (at, stay(tokens), stay(slot_weight), stay(cotangent)),
        [IN_SMEM] + [IN_HBM] * 3,
        [IN_VMEM] * len(shapes),
        [jax.ShapeDtypeStruct(*shape) for shape in shapes],
        [pltpu.VMEM((width, slots), LOW), pltpu.SemaphoreType.DMA((6,))],
    )


def grads_kernel(logit_ref, cot_ref, kept_ref, given_ref):
    logits = logit_ref[...]
    raised = jnp.exp(logits - jnp.max(logits, axis=0, keepdims=True))
    combine = raised * (1.0 / jnp.sum(raised, axis=0, keepdims=True))
    grad_part = product(combine.astype(LOW), cot_ref[...], 1, 0)
    halves(grad_part, (kept_ref, given_ref), slice(0, grad_part.shape[1]))


SIDE = pl.CostEstimate(flops=1_000_000_000, bytes_accessed=4_000_000, transcendentals=131_072)


def grads_of(logits, cotangent):
    shape = jax.ShapeDtypeStruct((logits.shape[0] // 2, cotangent.shape[1]), LOW)
    args = (logits, cotangent)
    return call(grads_kernel, "grads", args, [IN_VMEM] * 2, [IN_VMEM] * 2, [shape] * 2, (), SIDE)


def combine_kernel(rows_ref, order_ref, logit_ref, comb_ref):
    logits = product(rows_ref[...], order_ref[...], 1, 1)
    logit_ref[...] = logits
    raised = jnp.exp(logits - jnp.max(logits, axis=1, keepdims=True))
    comb_ref[...] = raised * (1.0 / jnp.sum(raised, axis=1, keepdims=True))


def combining(rows, order):
    shape = jax.ShapeDtypeStruct((rows.shape[0], order.shape[0]), WIDE)
    args = (rows, order)
    return call(
        combine_kernel, "combining", args, [IN_VMEM] * 2, [IN_VMEM] * 2, [shape] * 2, (), SIDE
    )


def merge_slots_kernel(kept_ref, taken_ref, out_ref):
    peers, own, wide = out_ref.shape
    width = kept_ref.shape[1] - EXTRA
    kept, taken = kept_ref[:, width:].astype(WIDE), taken_ref[:, width:].astype(WIDE)
    kept_max, taken_max = lanes(kept, 0), lanes(taken, 0)
    top = jnp.maximum(kept_max, taken_max)
    kept_scale, taken_scale = jnp.exp(kept_max - top), jnp.exp(taken_max - top)
    total = kept_scale * lanes(kept, 3) + taken_scale * lanes(taken, 3)
    slots = kept_scale * kept_ref[:, :width].astype(WIDE) + taken_scale * taken_ref[
        :, :width
    ].astype(WIDE)
    pieces = place(split3(top) + split3(total), kept.shape, 1)
    out_ref[:, :, :width] = slots.astype(LOW).reshape(peers, own, width)
    out_ref[:, :, wide - EXTRA :] = pieces.astype(LOW).reshape(peers, own, EXTRA)


def merge_grads_kernel(sent_ref, kept_ref, taken_ref, out_ref):
    peers, own = out_ref.shape[:2]
    width = kept_ref.shape[1]
    grads = kept_ref[...].astype(WIDE) + taken_ref[...].astype(WIDE)
    out_ref[:, :, width : 2 * width] = grads.astype(LOW).reshape(peers, own, width)


def merge_slots(kept, taken, width, peers):
    shape = jax.ShapeDtypeStruct((peers, kept.shape[0] // peers, kept.shape[1] + width), LOW)
    args = (kept, taken)
    return call(merge_slots_kernel, "merge_slots", args, [IN_VMEM] * 2, IN_VMEM, shape, (), SIDE)


def merge_grads(sent, kept, taken):
    return pl.pallas_call(
        merge_grads_kernel,
        in_specs=[IN_VMEM] * 3,
        out_specs=IN_VMEM,
        out_shape=jax.ShapeDtypeStruct(sent.shape, LOW),
        input_output_aliases={0: 0},
        compiler_params=pltpu.CompilerParams(vmem_limit_bytes=LIMIT),
        cost_estimate=SPAN,
        name="merge_grads",
    )(sent, kept, taken)


PART = 512


def expert_kernel(got_ref, in_ref, out_ref, told_ref):
    peers, own, wide = got_ref.shape
    count, width = peers * own, in_ref.shape[1]
    got = got_ref[...].reshape(count, wide)
    pieces = got[:, 2 * width :].astype(WIDE)
    block_max, block_sum = lanes(pieces, 0), lanes(pieces, 3)
    odd = lax.broadcasted_iota(jnp.int32, (count, 1), 0) % 2 == 1
    lowest = jnp.full((count, 1), -jnp.inf, WIDE)
    top = [
        jnp.max(jnp.where(odd, lowest, block_max), axis=0, keepdims=True),
        jnp.max(jnp.where(odd, block_max, lowest), axis=0, keepdims=True),
    ]
    scale = jnp.exp(block_max - jnp.where(odd, top[1], top[0]))
    scaled_sum = scale * block_sum
    totals = [
        jnp.sum(jnp.where(odd, 0.0, scaled_sum), axis=0, keepdims=True),
        jnp.sum(jnp.where(odd, scaled_sum, 0.0), axis=0, keepdims=True),
    ]
    high = scale.astype(LOW).astype(WIDE)
    rest, ones = scale - high, jnp.ones_like(scale)
    columns = []
    for column in (high, rest, ones):
        columns += [jnp.where(odd, 0.0, column), jnp.where(odd, column, 0.0)]
    picks = place(columns, (count, EXTRA), 1).T[:8].astype(LOW)
    sums = product(picks, got[:, : 2 * width], 1, 0)
    sums_of = lambda row, part: sums[row : row + 1, part]
    front, back = slice(0, width), slice(width, 2 * width)
    exact = [(sums_of(row, front) + sums_of(row + 2, front)) / totals[row] for row in range(2)]
    exact = place(exact, (8, width), 0)
    out_grad = place([sums_of(4, back), sums_of(5, back)], (8, width), 0).astype(LOW)
    slot_low = exact.astype(LOW)
    rate = 0.7978845608028654
    slot_out = jnp.zeros((8, width), WIDE)
    in_grad = jnp.zeros((8, width), WIDE)
    for first in range(0, in_ref.shape[2], PART):
        part = slice(first, first + PART)
        preact = product(slot_low, in_ref[0, :, part], 1, 0)
        hid_grad = product(out_grad, out_ref[0, part, :], 1, 1)
        square = preact * preact
        curve = jnp.tanh(rate * (preact + 0.044715 * square * preact))
        low_hidden = (0.5 * preact * (1.0 + curve)).astype(LOW)
        slope = 0.5 * (1.0 + curve) + 0.5 * preact * (1.0 - curve * curve) * rate * (
            1.0 + 3.0 * 0.044715 * square
        )
        slot_out += product(low_hidden, out_ref[0, part, :], 1, 0)
        in_grad += product((slope * hid_grad).astype(LOW), in_ref[0, :, part], 1, 1)
    slot_product = jnp.sum(exact * in_grad, axis=1, keepdims=True)
    top = place(top, (8, 1), 0)
    totals = place(totals, (8, 1), 0)
    scalars = place(split3(slot_product) + split3(top) + split3(totals), (8, EXTRA), 1)
    spread = lambda block: jnp.broadcast_to(
        block[:own].astype(LOW)[None], (peers, own, block.shape[1])
    )
    told_ref[:, :, :width] = spread(slot_out)
    told_ref[:, :, width : 2 * width] = spread(in_grad)
    told_ref[:, :, 2 * width :] = spread(scalars)


def expert(got, w_in, w_out):
    shape = jax.ShapeDtypeStruct(got.shape, LOW)
    return call(expert_kernel, "expert", (got, w_in, w_out), [IN_VMEM] * 3, IN_VMEM, shape)


def unpack_kernel(told_ref, out_ref, in_ref):
    half, width = out_ref.shape
    out_ref[...] = told_ref[:, :, :width].reshape(half, width)
    in_ref[...] = told_ref[:, :, width:].reshape(half, width + EXTRA)


def unpack(told, width):
    half = told.shape[0] * told.shape[1]
    shapes = [jax.ShapeDtypeStruct((half, wide), LOW) for wide in (width, width + EXTRA)]
    return call(unpack_kernel, "unpack", (told,), [IN_VMEM], [IN_VMEM] * 2, shapes)


STEPS = 2


def mixing_kernel(mine_ref, pair_ref, cot_ref, comb_ref, mixed_ref, logit_ref, all_out):
    half = mine_ref.shape[0]
    block = cot_ref.shape[0] // STEPS
    all_out[:half, :] = mine_ref[...]
    all_out[half:, :] = pair_ref[...]
    for step in range(STEPS):
        part = pl.ds(step * block, block)
        combine = comb_ref[part]
        mixed_ref[part, :] = product(combine.astype(LOW), all_out[...], 1, 0).astype(LOW)
        comb_grad = product(cot_ref[part], all_out[...], 1, 1)
        mean = jnp.sum(combine * comb_grad, axis=1, keepdims=True)
        logit_ref[part, :] = combine * (comb_grad - mean)


def mixing(mine, pair, cotangent, combine):
    rows, width = cotangent.shape
    slots = combine.shape[1]
    shapes = [jax.ShapeDtypeStruct((rows, width), LOW), jax.ShapeDtypeStruct((rows, slots), WIDE)]
    args = (mine, pair, cotangent, combine)
    scratch = [pltpu.VMEM((slots, width), LOW)]
    return call(
        mixing_kernel, "mixing", args, [IN_VMEM] * 4, [IN_VMEM] * 2, shapes, scratch, SIDE
    )


def closing_kernel(
    mixed_ref, mine_ref, pair_ref, tok_ref, comb_ref, logit_ref, order_ref,
    mixed_hbm, grad_hbm,
    in_low, rows_ref, grad_ref, sems,
):
    count, width = tok_ref.shape
    half = mine_ref.shape[0]
    block = count // STEPS
    stores = [pltpu.make_async_copy(mixed_ref, mixed_hbm, sems.at[STEPS])]
    stores[0].start()
    for at, ref in enumerate((mine_ref, pair_ref)):
        part = slice(at * half, (at + 1) * half)
        in_low[part, :] = ref[:, :width]
        pieces = ref[:, width:].astype(WIDE).T
        for row in range(3):
            rows_ref[row : row + 1, part] = jnp.sum(
                pieces[3 * row : 3 * row + 3], axis=0, keepdims=True
            )
    slot_product, highest, scale = rows_ref[0:1], rows_ref[1:2], 1.0 / rows_ref[2:3]
    for step in range(STEPS):
        part = pl.ds(step * block, block)
        dispatch = jnp.exp(logit_ref[part] - highest) * scale
        logit_grad = dispatch * (product(tok_ref[part], in_low[...], 1, 1) - slot_product)
        logit_grad += comb_ref[part]
        token_grad = product(logit_grad.astype(LOW), order_ref[...], 1, 0)
        token_grad += product(dispatch.astype(LOW), in_low[...], 1, 0)
        grad_ref[part, :] = token_grad.astype(LOW)
        stores.append(pltpu.make_async_copy(grad_ref.at[part], grad_hbm.at[part], sems.at[step]))
        stores[-1].start()
    for copy in stores:
        copy.wait()


def closing(mixed, mine, pair, tokens, logit_comb, logits, weight):
    slots, width = weight.shape
    shape = jax.ShapeDtypeStruct(tokens.shape, LOW)
    return call(
        closing_kernel,
        "closing",
        (mixed, mine, pair, tokens, logit_comb, logits, weight),
        [IN_VMEM] * 7,
        [IN_HBM] * 2,
        [shape] * 2,
        [
            pltpu.VMEM((slots, width), LOW),
            pltpu.VMEM((8, slots), WIDE),
            pltpu.VMEM(tokens.shape, LOW),
            pltpu.SemaphoreType.DMA((STEPS + 1,)),
        ],
    )


def shards(tokens, slot_weight, w_in, w_out, cotangent):
    torus = ("x", "z", "exp")
    swap = [(0, 1), (1, 0)]
    at = jnp.stack([lax.axis_index("exp"), lax.axis_index("core")]).astype(jnp.int32)
    peers = lax.axis_size(torus)
    kept, given, columns, weight, rows, cot = opening(at, tokens, slot_weight, cotangent)
    taken = lax.ppermute(given, "core", swap)
    kept_grad, given_grad = grads_of(columns, cot)
    taken_grad = lax.ppermute(given_grad, "core", swap)
    logits, combine = combining(rows, weight)
    sent = merge_grads(
        merge_slots(kept, taken, cotangent.shape[1], peers), kept_grad, taken_grad
    )
    got = lax.all_to_all(sent, torus, split_axis=0, concat_axis=0, tiled=True)
    told = expert(got, w_in, w_out)
    told = lax.all_to_all(told, torus, split_axis=0, concat_axis=0, tiled=True)
    slot_out, in_grad = unpack(told, cotangent.shape[1])
    pair_out = lax.ppermute(slot_out, "core", swap)
    pair_grad = lax.ppermute(in_grad, "core", swap)
    mixed, logit_comb = mixing(slot_out, pair_out, cot, combine)
    return tuple(closing(mixed, in_grad, pair_grad, rows, logit_comb, logits, weight))


def solution(mesh):
    exp = mesh.devices.shape[1]
    finer = Mesh(mesh.devices.reshape(4, 4, 2, exp), ("x", "z", "core", "exp"))
    every = ("x", "z", "core", "exp")
    rows = P(every, None)
    experts = P(every, None, None)
    return jax.shard_map(
        shards,
        mesh=finer,
        in_specs=(P(("x", "z", "core"), None), P(), experts, experts, rows),
        out_specs=(rows, rows),
        check_vma=False,
    )
```

```python
import functools

import jax
import jax.numpy as jnp
from jax import lax
from jax.experimental import pallas as pl
from jax.experimental.pallas import tpu as pltpu
from jax.sharding import Mesh
from jax.sharding import PartitionSpec as P

LOW = jnp.bfloat16
WIDE = jnp.float32
EXTRA = 128
LIMIT = 20 * 1024 * 1024


def product(left, right, left_dim, right_dim):
    return lax.dot_general(
        left, right, (((left_dim,), (right_dim,)), ((), ())), preferred_element_type=WIDE
    )


def split3(value):
    high = value.astype(LOW).astype(WIDE)
    rest = value - high
    mid = rest.astype(LOW).astype(WIDE)
    return [high, mid, rest - mid]


def place(pieces, shape, axis):
    index = lax.broadcasted_iota(jnp.int32, shape, axis)
    total = jnp.zeros(shape, WIDE)
    for at, piece in enumerate(pieces):
        total = jnp.where(index == at, piece, total)
    return total


def lanes(block, first):
    index = lax.broadcasted_iota(jnp.int32, block.shape, 1)
    inside = (index >= first) & (index < first + 3)
    return jnp.sum(jnp.where(inside, block, 0.0), axis=1, keepdims=True)


IN_SMEM = pl.BlockSpec(memory_space=pltpu.SMEM)
IN_VMEM = pl.BlockSpec(memory_space=pltpu.VMEM)
IN_HBM = pl.BlockSpec(memory_space=pltpu.HBM)


def stay(array):
    return pltpu.with_memory_space_constraint(array, pltpu.HBM)


SPAN = pl.CostEstimate(flops=9_000_000_000, bytes_accessed=20_000_000, transcendentals=0)


def call(kernel, name, args, specs, out_specs, out_shape, scratch=(), cost=None):
    return pl.pallas_call(
        kernel,
        in_specs=specs,
        out_specs=out_specs,
        out_shape=out_shape,
        scratch_shapes=scratch,
        compiler_params=pltpu.CompilerParams(vmem_limit_bytes=LIMIT),
        cost_estimate=cost,
        name=name,
    )(*args)


def ordering(group, slots):
    to = lax.broadcasted_iota(jnp.int32, (slots, 1), 0)
    source = lax.broadcasted_iota(jnp.int32, (slots, slots), 1)
    half = slots // 2
    within = to % half
    chip, y = within // 8, (within // 2) % 4
    core = (group + to // half + chip // 4 + chip % 4 + y) % 2
    wanted = chip * 16 + core * 8 + within % 8
    return (source == wanted).astype(WIDE).astype(LOW)


def halves(value, outs, columns):
    half = outs[0].shape[0]
    for at, out in enumerate(outs):
        out[:, columns] = value[at * half : (at + 1) * half].astype(LOW)


def opening_kernel(
    at_ref, tok_hbm, weight_hbm, cot_hbm,
    kept_ref, given_ref, logit_ref, order_ref, rows_ref, cot_ref,
    weight_ref, sems,
):
    slots = weight_ref.shape[1]
    count, width = rows_ref.shape
    start = pl.multiple_of(at_ref[0] * count, count)
    block = count // 4
    parts = [pl.ds(at * block, block) for at in range(4)]
    loads = [pltpu.make_async_copy(weight_hbm, weight_ref, sems.at[0])]
    for at, part in enumerate(parts):
        source = tok_hbm.at[pl.ds(start + at * block, block)]
        loads.append(pltpu.make_async_copy(source, rows_ref.at[part], sems.at[1 + at]))
    loads.append(pltpu.make_async_copy(cot_hbm, cot_ref, sems.at[5]))
    for copy in loads[:5]:
        copy.start()
    order = ordering(at_ref[1], slots)
    loads[0].wait()
    weight = product(order, weight_ref[...], 1, 1).astype(LOW)
    order_ref[...] = weight
    for copy in loads[1:5]:
        copy.wait()
    loads[5].start()
    rows = rows_ref[...]
    logits = product(weight, rows, 1, 1)
    logit_ref[...] = logits
    slot_max = jnp.max(logits, axis=1, keepdims=True)
    shifted = jnp.exp(logits - slot_max)
    slot_sum = jnp.sum(shifted, axis=1, keepdims=True)
    outs = (kept_ref, given_ref)
    halves(product(shifted.astype(LOW), rows, 1, 0), outs, slice(0, width))
    pieces = place(split3(slot_max) + split3(slot_sum), (slots, EXTRA), 1)
    halves(pieces, outs, slice(width, width + EXTRA))
    loads[5].wait()


def opening(at, tokens, slot_weight, cotangent):
    rows, width = cotangent.shape
    slots = slot_weight.shape[1]
    shapes = [((slots // 2, width + EXTRA), LOW)] * 2 + [((slots, rows), WIDE)]
    shapes += [((slots, width), LOW)] + [((rows, width), LOW)] * 2
    return call(
        opening_kernel,
        "opening",
        (at, stay(tokens), stay(slot_weight), stay(cotangent)),
        [IN_SMEM] + [IN_HBM] * 3,
        [IN_VMEM] * len(shapes),
        [jax.ShapeDtypeStruct(*shape) for shape in shapes],
        [pltpu.VMEM((width, slots), LOW), pltpu.SemaphoreType.DMA((6,))],
    )


def grads_kernel(logit_ref, cot_ref, kept_ref, given_ref):
    logits = logit_ref[...]
    raised = jnp.exp(logits - jnp.max(logits, axis=0, keepdims=True))
    combine = raised * (1.0 / jnp.sum(raised, axis=0, keepdims=True))
    grad_part = product(combine.astype(LOW), cot_ref[...], 1, 0)
    halves(grad_part, (kept_ref, given_ref), slice(0, grad_part.shape[1]))


SIDE = pl.CostEstimate(flops=1_000_000_000, bytes_accessed=4_000_000, transcendentals=131_072)


def grads_of(logits, cotangent):
    shape = jax.ShapeDtypeStruct((logits.shape[0] // 2, cotangent.shape[1]), LOW)
    args = (logits, cotangent)
    return call(grads_kernel, "grads", args, [IN_VMEM] * 2, [IN_VMEM] * 2, [shape] * 2, (), SIDE)


def combine_kernel(rows_ref, order_ref, logit_ref, comb_ref):
    logits = product(rows_ref[...], order_ref[...], 1, 1)
    logit_ref[...] = logits
    raised = jnp.exp(logits - jnp.max(logits, axis=1, keepdims=True))
    comb_ref[...] = raised * (1.0 / jnp.sum(raised, axis=1, keepdims=True))


def combining(rows, order):
    shape = jax.ShapeDtypeStruct((rows.shape[0], order.shape[0]), WIDE)
    args = (rows, order)
    return call(
        combine_kernel, "combining", args, [IN_VMEM] * 2, [IN_VMEM] * 2, [shape] * 2, (), SIDE
    )


def merge_slots_kernel(kept_ref, taken_ref, out_ref):
    peers, own, wide = out_ref.shape
    width = kept_ref.shape[1] - EXTRA
    kept, taken = kept_ref[:, width:].astype(WIDE), taken_ref[:, width:].astype(WIDE)
    kept_max, taken_max = lanes(kept, 0), lanes(taken, 0)
    top = jnp.maximum(kept_max, taken_max)
    kept_scale, taken_scale = jnp.exp(kept_max - top), jnp.exp(taken_max - top)
    total = kept_scale * lanes(kept, 3) + taken_scale * lanes(taken, 3)
    slots = kept_scale * kept_ref[:, :width].astype(WIDE) + taken_scale * taken_ref[
        :, :width
    ].astype(WIDE)
    pieces = place(split3(top) + split3(total), kept.shape, 1)
    out_ref[:, :, :width] = slots.astype(LOW).reshape(peers, own, width)
    out_ref[:, :, wide - EXTRA :] = pieces.astype(LOW).reshape(peers, own, EXTRA)


def merge_grads_kernel(sent_ref, kept_ref, taken_ref, out_ref):
    peers, own = out_ref.shape[:2]
    width = kept_ref.shape[1]
    grads = kept_ref[...].astype(WIDE) + taken_ref[...].astype(WIDE)
    out_ref[:, :, width : 2 * width] = grads.astype(LOW).reshape(peers, own, width)


def merge_slots(kept, taken, width, peers):
    shape = jax.ShapeDtypeStruct((peers, kept.shape[0] // peers, kept.shape[1] + width), LOW)
    args = (kept, taken)
    return call(merge_slots_kernel, "merge_slots", args, [IN_VMEM] * 2, IN_VMEM, shape, (), SIDE)


def merge_grads(sent, kept, taken):
    return pl.pallas_call(
        merge_grads_kernel,
        in_specs=[IN_VMEM] * 3,
        out_specs=IN_VMEM,
        out_shape=jax.ShapeDtypeStruct(sent.shape, LOW),
        input_output_aliases={0: 0},
        compiler_params=pltpu.CompilerParams(vmem_limit_bytes=LIMIT),
        cost_estimate=SPAN,
        name="merge_grads",
    )(sent, kept, taken)


PART = 512


def expert_kernel(got_ref, in_ref, out_ref, told_ref):
    peers, own, wide = got_ref.shape
    count, width = peers * own, in_ref.shape[1]
    got = got_ref[...].reshape(count, wide)
    pieces = got[:, 2 * width :].astype(WIDE)
    block_max, block_sum = lanes(pieces, 0), lanes(pieces, 3)
    odd = lax.broadcasted_iota(jnp.int32, (count, 1), 0) % 2 == 1
    lowest = jnp.full((count, 1), -jnp.inf, WIDE)
    top = [
        jnp.max(jnp.where(odd, lowest, block_max), axis=0, keepdims=True),
        jnp.max(jnp.where(odd, block_max, lowest), axis=0, keepdims=True),
    ]
    scale = jnp.exp(block_max - jnp.where(odd, top[1], top[0]))
    scaled_sum = scale * block_sum
    totals = [
        jnp.sum(jnp.where(odd, 0.0, scaled_sum), axis=0, keepdims=True),
        jnp.sum(jnp.where(odd, scaled_sum, 0.0), axis=0, keepdims=True),
    ]
    high = scale.astype(LOW).astype(WIDE)
    rest, ones = scale - high, jnp.ones_like(scale)
    columns = []
    for column in (high, rest, ones):
        columns += [jnp.where(odd, 0.0, column), jnp.where(odd, column, 0.0)]
    picks = place(columns, (count, EXTRA), 1).T[:8].astype(LOW)
    sums = product(picks, got[:, : 2 * width], 1, 0)
    sums_of = lambda row, part: sums[row : row + 1, part]
    front, back = slice(0, width), slice(width, 2 * width)
    exact = [(sums_of(row, front) + sums_of(row + 2, front)) / totals[row] for row in range(2)]
    exact = place(exact, (8, width), 0)
    out_grad = place([sums_of(4, back), sums_of(5, back)], (8, width), 0).astype(LOW)
    slot_low = exact.astype(LOW)
    rate = 0.7978845608028654
    slot_out = jnp.zeros((8, width), WIDE)
    in_grad = jnp.zeros((8, width), WIDE)
    for first in range(0, in_ref.shape[2], PART):
        part = slice(first, first + PART)
        preact = product(slot_low, in_ref[0, :, part], 1, 0)
        hid_grad = product(out_grad, out_ref[0, part, :], 1, 1)
        square = preact * preact
        curve = jnp.tanh(rate * (preact + 0.044715 * square * preact))
        low_hidden = (0.5 * preact * (1.0 + curve)).astype(LOW)
        slope = 0.5 * (1.0 + curve) + 0.5 * preact * (1.0 - curve * curve) * rate * (
            1.0 + 3.0 * 0.044715 * square
        )
        slot_out += product(low_hidden, out_ref[0, part, :], 1, 0)
        in_grad += product((slope * hid_grad).astype(LOW), in_ref[0, :, part], 1, 1)
    slot_product = jnp.sum(exact * in_grad, axis=1, keepdims=True)
    top = place(top, (8, 1), 0)
    totals = place(totals, (8, 1), 0)
    scalars = place(split3(slot_product) + split3(top) + split3(totals), (8, EXTRA), 1)
    spread = lambda block: jnp.broadcast_to(
        block[:own].astype(LOW)[None], (peers, own, block.shape[1])
    )
    told_ref[:, :, :width] = spread(slot_out)
    told_ref[:, :, width : 2 * width] = spread(in_grad)
    told_ref[:, :, 2 * width :] = spread(scalars)


def expert(got, w_in, w_out):
    shape = jax.ShapeDtypeStruct(got.shape, LOW)
    return call(expert_kernel, "expert", (got, w_in, w_out), [IN_VMEM] * 3, IN_VMEM, shape)


STEPS = 2


def closing_kernel(
    mine_ref, pair_ref, tok_ref, cot_ref, comb_ref, logit_ref, order_ref,
    mixed_hbm, grad_hbm,
    all_out, in_low, rows_ref, mixed_ref, grad_ref, out_sems,
):
    count, width = cot_ref.shape
    half = mine_ref.shape[0] * mine_ref.shape[1]
    block = count // STEPS
    for at, ref in enumerate((mine_ref, pair_ref)):
        part = slice(at * half, (at + 1) * half)
        all_out[part, :] = ref[:, :, :width].reshape(half, width)
        in_low[part, :] = ref[:, :, width : 2 * width].reshape(half, width)
        pieces = ref[:, :, 2 * width :].reshape(half, EXTRA).astype(WIDE).T
        for row in range(3):
            rows_ref[row : row + 1, part] = jnp.sum(
                pieces[3 * row : 3 * row + 3], axis=0, keepdims=True
            )
    slot_product, highest, scale = rows_ref[0:1], rows_ref[1:2], 1.0 / rows_ref[2:3]
    stores = []
    for step in range(STEPS):
        part = pl.ds(step * block, block)
        stores.append(
            pltpu.make_async_copy(mixed_ref.at[part], mixed_hbm.at[part], out_sems.at[0, step])
        )
        stores.append(
            pltpu.make_async_copy(grad_ref.at[part], grad_hbm.at[part], out_sems.at[1, step])
        )
        combine = comb_ref[part]
        mixed_ref[part, :] = product(combine.astype(LOW), all_out[...], 1, 0).astype(LOW)
        stores[-2].start()
        comb_grad = product(cot_ref[part], all_out[...], 1, 1)
        logit_grad = combine * (comb_grad - jnp.sum(combine * comb_grad, axis=1, keepdims=True))
        dispatch = jnp.exp(logit_ref[part] - highest) * scale
        logit_grad += dispatch * (product(tok_ref[part], in_low[...], 1, 1) - slot_product)
        token_grad = product(logit_grad.astype(LOW), order_ref[...], 1, 0)
        token_grad += product(dispatch.astype(LOW), in_low[...], 1, 0)
        grad_ref[part, :] = token_grad.astype(LOW)
        stores[-1].start()
    for copy in stores:
        copy.wait()


def closing(mine, pair, tokens, cotangent, combine, logits, weight):
    rows, width = cotangent.shape
    slots = weight.shape[0]
    return call(
        closing_kernel,
        "closing",
        (mine, pair, tokens, cotangent, combine, logits, weight),
        [IN_VMEM] * 7,
        [IN_HBM] * 2,
        [jax.ShapeDtypeStruct((rows, width), LOW)] * 2,
        [
            pltpu.VMEM((slots, width), LOW),
            pltpu.VMEM((slots, width), LOW),
            pltpu.VMEM((8, slots), WIDE),
            pltpu.VMEM((rows, width), LOW),
            pltpu.VMEM((rows, width), LOW),
            pltpu.SemaphoreType.DMA((2, STEPS)),
        ],
    )


def place_of(x, z, core, y):
    return ((x * 4 + z) * 2 + core) * 4 + y


def groups_of():
    chips = [(x, z, y) for x in range(4) for z in range(4) for y in range(4)]
    return [
        [place_of(x, z, (group + x + z + y) % 2, y) for x, z, y in chips] for group in range(2)
    ]


def shards(tokens, slot_weight, w_in, w_out, cotangent):
    every = ("x", "z", "core", "exp")
    x, z, core, y = (lax.axis_index(axis) for axis in every)
    at = jnp.stack([y, (core + x + z + y) % 2]).astype(jnp.int32)
    peers = lax.axis_size(every) // 2
    swap = lambda array: lax.ppermute(array, "core", [(0, 1), (1, 0)])
    trade = lambda array: lax.all_to_all(
        array, every, 0, 0, axis_index_groups=groups_of(), tiled=True
    )
    kept, given, columns, weight, rows, cot = opening(at, tokens, slot_weight, cotangent)
    taken = swap(given)
    kept_grad, given_grad = grads_of(columns, cot)
    taken_grad = swap(given_grad)
    logits, combine = combining(rows, weight)
    sent = merge_grads(
        merge_slots(kept, taken, cotangent.shape[1], peers), kept_grad, taken_grad
    )
    got = trade(sent)
    told = expert(got, w_in, w_out)
    told = trade(told)
    pair = swap(told)
    return tuple(closing(told, pair, rows, cot, combine, logits, weight))


def solution(mesh):
    exp = mesh.devices.shape[1]
    finer = Mesh(mesh.devices.reshape(4, 4, 2, exp), ("x", "z", "core", "exp"))
    every = ("x", "z", "core", "exp")
    rows = P(every, None)
    experts = P(every, None, None)
    return jax.shard_map(
        shards,
        mesh=finer,
        in_specs=(P(("x", "z", "core"), None), P(), experts, experts, rows),
        out_specs=(rows, rows),
        check_vma=False,
    )
```

```python
import functools

import jax
import jax.numpy as jnp
from jax import lax
from jax.experimental import pallas as pl
from jax.experimental.pallas import tpu as pltpu
from jax.sharding import Mesh
from jax.sharding import PartitionSpec as P

LOW = jnp.bfloat16
WIDE = jnp.float32
EXTRA = 128
LIMIT = 20 * 1024 * 1024


def product(left, right, left_dim, right_dim):
    return lax.dot_general(
        left, right, (((left_dim,), (right_dim,)), ((), ())), preferred_element_type=WIDE
    )


def split3(value):
    high = value.astype(LOW).astype(WIDE)
    rest = value - high
    mid = rest.astype(LOW).astype(WIDE)
    return [high, mid, rest - mid]


def place(pieces, shape, axis):
    index = lax.broadcasted_iota(jnp.int32, shape, axis)
    total = jnp.zeros(shape, WIDE)
    for at, piece in enumerate(pieces):
        total = jnp.where(index == at, piece, total)
    return total


def lanes(block, first):
    index = lax.broadcasted_iota(jnp.int32, block.shape, 1)
    inside = (index >= first) & (index < first + 3)
    return jnp.sum(jnp.where(inside, block, 0.0), axis=1, keepdims=True)


IN_SMEM = pl.BlockSpec(memory_space=pltpu.SMEM)
IN_VMEM = pl.BlockSpec(memory_space=pltpu.VMEM)
IN_HBM = pl.BlockSpec(memory_space=pltpu.HBM)


def stay(array):
    return pltpu.with_memory_space_constraint(array, pltpu.HBM)


SPAN = pl.CostEstimate(flops=9_000_000_000, bytes_accessed=20_000_000, transcendentals=0)


def call(kernel, name, args, specs, out_specs, out_shape, scratch=(), cost=None):
    return pl.pallas_call(
        kernel,
        in_specs=specs,
        out_specs=out_specs,
        out_shape=out_shape,
        scratch_shapes=scratch,
        compiler_params=pltpu.CompilerParams(vmem_limit_bytes=LIMIT),
        cost_estimate=cost,
        name=name,
    )(*args)


def ordering(core, slots):
    to = lax.broadcasted_iota(jnp.int32, (slots, 1), 0)
    source = lax.broadcasted_iota(jnp.int32, (slots, slots), 1)
    half = slots // 2
    within = to % half
    other = jnp.where(to // half == 0, core, 1 - core)
    wanted = (within // 8) * 16 + other * 8 + within % 8
    return (source == wanted).astype(WIDE).astype(LOW)


def opening_kernel(
    at_ref, tok_hbm, weight_hbm, cot_hbm,
    given_ref, shift_ref, piece_ref, logit_ref, order_ref, rows_ref, cot_ref,
    weight_ref, sems,
):
    slots = weight_ref.shape[1]
    count, width = rows_ref.shape
    start = pl.multiple_of(at_ref[0] * count, count)
    block = count // 4
    parts = [pl.ds(at * block, block) for at in range(4)]
    loads = [pltpu.make_async_copy(weight_hbm, weight_ref, sems.at[0])]
    for at, part in enumerate(parts):
        source = tok_hbm.at[pl.ds(start + at * block, block)]
        loads.append(pltpu.make_async_copy(source, rows_ref.at[part], sems.at[1 + at]))
    loads.append(pltpu.make_async_copy(cot_hbm, cot_ref, sems.at[5]))
    for copy in loads:
        copy.start()
    order = ordering(at_ref[1], slots)
    loads[0].wait()
    weight = product(order, weight_ref[...], 1, 1).astype(LOW)
    order_ref[...] = weight
    for copy in loads[1:5]:
        copy.wait()
    rows = rows_ref[...]
    logits = product(weight, rows, 1, 1)
    logit_ref[...] = logits
    slot_max = jnp.max(logits, axis=1, keepdims=True)
    shifted = jnp.exp(logits - slot_max)
    slot_sum = jnp.sum(shifted, axis=1, keepdims=True)
    half = slots // 2
    shifted = shifted.astype(LOW)
    given_ref[:, :width] = product(shifted[half:], rows, 1, 0).astype(LOW)
    shift_ref[...] = shifted[:half]
    pieces = place(split3(slot_max) + split3(slot_sum), (slots, EXTRA), 1)
    given_ref[:, width:] = pieces[half:].astype(LOW)
    piece_ref[...] = pieces[:half]
    loads[5].wait()


def opening(at, tokens, slot_weight, cotangent):
    rows, width = cotangent.shape
    slots = slot_weight.shape[1]
    half = slots // 2
    shapes = [((half, width + EXTRA), LOW), ((half, rows), LOW), ((half, EXTRA), WIDE)]
    shapes += [((slots, rows), WIDE), ((slots, width), LOW)] + [((rows, width), LOW)] * 2
    return call(
        opening_kernel,
        "opening",
        (at, stay(tokens), stay(slot_weight), stay(cotangent)),
        [IN_SMEM] + [IN_HBM] * 3,
        [IN_VMEM] * len(shapes),
        [jax.ShapeDtypeStruct(*shape) for shape in shapes],
        [pltpu.VMEM((width, slots), LOW), pltpu.SemaphoreType.DMA((6,))],
    )


def grads_kernel(logit_ref, cot_ref, given_ref, comb_ref):
    logits = logit_ref[...]
    raised = jnp.exp(logits - jnp.max(logits, axis=0, keepdims=True))
    combine = (raised * (1.0 / jnp.sum(raised, axis=0, keepdims=True))).astype(LOW)
    half = given_ref.shape[0]
    given_ref[...] = product(combine[half:], cot_ref[...], 1, 0).astype(LOW)
    comb_ref[...] = combine[:half]


SIDE = pl.CostEstimate(flops=1_000_000_000, bytes_accessed=4_000_000, transcendentals=131_072)


def grads_of(logits, cotangent):
    half, rows = logits.shape[0] // 2, logits.shape[1]
    shapes = [jax.ShapeDtypeStruct((half, wide), LOW) for wide in (cotangent.shape[1], rows)]
    args = (logits, cotangent)
    return call(grads_kernel, "grads", args, [IN_VMEM] * 2, [IN_VMEM] * 2, shapes, (), SIDE)


def combine_kernel(rows_ref, order_ref, logit_ref, comb_ref):
    logits = product(rows_ref[...], order_ref[...], 1, 1)
    logit_ref[...] = logits
    raised = jnp.exp(logits - jnp.max(logits, axis=1, keepdims=True))
    comb_ref[...] = raised * (1.0 / jnp.sum(raised, axis=1, keepdims=True))


def combining(rows, order):
    shape = jax.ShapeDtypeStruct((rows.shape[0], order.shape[0]), WIDE)
    args = (rows, order)
    return call(
        combine_kernel, "combining", args, [IN_VMEM] * 2, [IN_VMEM] * 2, [shape] * 2, (), SIDE
    )


def merge_slots_kernel(
    shift_ref, piece_ref, comb_ref, rows_ref, cot_ref, taken_ref, out_ref, grad_ref
):
    peers, own, wide = out_ref.shape
    width = rows_ref.shape[1]
    kept, taken = piece_ref[...], taken_ref[:, width:].astype(WIDE)
    kept_max, taken_max = lanes(kept, 0), lanes(taken, 0)
    top = jnp.maximum(kept_max, taken_max)
    kept_scale, taken_scale = jnp.exp(kept_max - top), jnp.exp(taken_max - top)
    total = kept_scale * lanes(kept, 3) + taken_scale * lanes(taken, 3)
    slots = kept_scale * product(shift_ref[...], rows_ref[...], 1, 0)
    slots += taken_scale * taken_ref[:, :width].astype(WIDE)
    pieces = place(split3(top) + split3(total), kept.shape, 1)
    out_ref[:, :, :width] = slots.astype(LOW).reshape(peers, own, width)
    out_ref[:, :, wide - EXTRA :] = pieces.astype(LOW).reshape(peers, own, EXTRA)
    grad_ref[...] = product(comb_ref[...], cot_ref[...], 1, 0)


def merge_grads_kernel(sent_ref, kept_ref, taken_ref, out_ref):
    peers, own = out_ref.shape[:2]
    width = kept_ref.shape[1]
    grads = kept_ref[...] + taken_ref[...].astype(WIDE)
    out_ref[:, :, width : 2 * width] = grads.astype(LOW).reshape(peers, own, width)


def merge_slots(shifted, pieces, combine, rows, cotangent, taken, peers):
    half, width = shifted.shape[0], rows.shape[1]
    args = (shifted, pieces, combine, rows, cotangent, taken)
    shapes = [
        jax.ShapeDtypeStruct((peers, half // peers, taken.shape[1] + width), LOW),
        jax.ShapeDtypeStruct((half, width), WIDE),
    ]
    return call(
        merge_slots_kernel, "merge_slots", args, [IN_VMEM] * 6, [IN_VMEM] * 2, shapes, (), SIDE
    )


def merge_grads(sent, kept, taken):
    return pl.pallas_call(
        merge_grads_kernel,
        in_specs=[IN_VMEM] * 3,
        out_specs=IN_VMEM,
        out_shape=jax.ShapeDtypeStruct(sent.shape, LOW),
        input_output_aliases={0: 0},
        compiler_params=pltpu.CompilerParams(vmem_limit_bytes=LIMIT),
        cost_estimate=SPAN,
        name="merge_grads",
    )(sent, kept, taken)


PART = 512


def expert_kernel(got_ref, in_ref, out_ref, told_ref):
    peers, own, wide = got_ref.shape
    count, width = peers * own, in_ref.shape[1]
    got = got_ref[...].reshape(count, wide)
    pieces = got[:, 2 * width :].astype(WIDE)
    block_max, block_sum = lanes(pieces, 0), lanes(pieces, 3)
    odd = lax.broadcasted_iota(jnp.int32, (count, 1), 0) % 2 == 1
    lowest = jnp.full((count, 1), -jnp.inf, WIDE)
    top = [
        jnp.max(jnp.where(odd, lowest, block_max), axis=0, keepdims=True),
        jnp.max(jnp.where(odd, block_max, lowest), axis=0, keepdims=True),
    ]
    scale = jnp.exp(block_max - jnp.where(odd, top[1], top[0]))
    scaled_sum = scale * block_sum
    totals = [
        jnp.sum(jnp.where(odd, 0.0, scaled_sum), axis=0, keepdims=True),
        jnp.sum(jnp.where(odd, scaled_sum, 0.0), axis=0, keepdims=True),
    ]
    high = scale.astype(LOW).astype(WIDE)
    rest, ones = scale - high, jnp.ones_like(scale)
    columns = []
    for column in (high, rest, ones):
        columns += [jnp.where(odd, 0.0, column), jnp.where(odd, column, 0.0)]
    picks = place(columns, (count, EXTRA), 1).T[:8].astype(LOW)
    sums = product(picks, got[:, : 2 * width], 1, 0)
    sums_of = lambda row, part: sums[row : row + 1, part]
    front, back = slice(0, width), slice(width, 2 * width)
    exact = [(sums_of(row, front) + sums_of(row + 2, front)) / totals[row] for row in range(2)]
    exact = place(exact, (8, width), 0)
    out_grad = place([sums_of(4, back), sums_of(5, back)], (8, width), 0).astype(LOW)
    slot_low = exact.astype(LOW)
    rate = 0.7978845608028654
    slot_out = jnp.zeros((8, width), WIDE)
    in_grad = jnp.zeros((8, width), WIDE)
    for first in range(0, in_ref.shape[2], PART):
        part = slice(first, first + PART)
        preact = product(slot_low, in_ref[0, :, part], 1, 0)
        hid_grad = product(out_grad, out_ref[0, part, :], 1, 1)
        square = preact * preact
        curve = jnp.tanh(rate * (preact + 0.044715 * square * preact))
        low_hidden = (0.5 * preact * (1.0 + curve)).astype(LOW)
        slope = 0.5 * (1.0 + curve) + 0.5 * preact * (1.0 - curve * curve) * rate * (
            1.0 + 3.0 * 0.044715 * square
        )
        slot_out += product(low_hidden, out_ref[0, part, :], 1, 0)
        in_grad += product((slope * hid_grad).astype(LOW), in_ref[0, :, part], 1, 1)
    slot_product = jnp.sum(exact * in_grad, axis=1, keepdims=True)
    top = place(top, (8, 1), 0)
    totals = place(totals, (8, 1), 0)
    scalars = place(split3(slot_product) + split3(top) + split3(totals), (8, EXTRA), 1)
    spread = lambda block: jnp.broadcast_to(
        block[:own].astype(LOW)[None], (peers, own, block.shape[1])
    )
    told_ref[:, :, :width] = spread(slot_out)
    told_ref[:, :, width : 2 * width] = spread(in_grad)
    told_ref[:, :, 2 * width :] = spread(scalars)


def expert(got, w_in, w_out):
    shape = jax.ShapeDtypeStruct(got.shape, LOW)
    return call(expert_kernel, "expert", (got, w_in, w_out), [IN_VMEM] * 3, IN_VMEM, shape)


STEPS = 2


def closing_kernel(
    mine_ref, pair_ref, tok_ref, cot_ref, comb_ref, logit_ref, order_ref,
    mixed_hbm, grad_hbm,
    all_out, in_low, rows_ref, mixed_ref, grad_ref, out_sems,
):
    count, width = cot_ref.shape
    half = mine_ref.shape[0] * mine_ref.shape[1]
    block = count // STEPS
    for at, ref in enumerate((mine_ref, pair_ref)):
        part = slice(at * half, (at + 1) * half)
        all_out[part, :] = ref[:, :, :width].reshape(half, width)
        in_low[part, :] = ref[:, :, width : 2 * width].reshape(half, width)
        pieces = ref[:, :, 2 * width :].reshape(half, EXTRA).astype(WIDE).T
        for row in range(3):
            rows_ref[row : row + 1, part] = jnp.sum(
                pieces[3 * row : 3 * row + 3], axis=0, keepdims=True
            )
    slot_product, highest, scale = rows_ref[0:1], rows_ref[1:2], 1.0 / rows_ref[2:3]
    stores = []
    for step in range(STEPS):
        part = pl.ds(step * block, block)
        stores.append(
            pltpu.make_async_copy(mixed_ref.at[part], mixed_hbm.at[part], out_sems.at[0, step])
        )
        stores.append(
            pltpu.make_async_copy(grad_ref.at[part], grad_hbm.at[part], out_sems.at[1, step])
        )
        combine = comb_ref[part]
        mixed_ref[part, :] = product(combine.astype(LOW), all_out[...], 1, 0).astype(LOW)
        stores[-2].start()
        comb_grad = product(cot_ref[part], all_out[...], 1, 1)
        logit_grad = combine * (comb_grad - jnp.sum(combine * comb_grad, axis=1, keepdims=True))
        dispatch = jnp.exp(logit_ref[part] - highest) * scale
        logit_grad += dispatch * (product(tok_ref[part], in_low[...], 1, 1) - slot_product)
        token_grad = product(logit_grad.astype(LOW), order_ref[...], 1, 0)
        token_grad += product(dispatch.astype(LOW), in_low[...], 1, 0)
        grad_ref[part, :] = token_grad.astype(LOW)
        stores[-1].start()
    for copy in stores:
        copy.wait()


def closing(mine, pair, tokens, cotangent, combine, logits, weight):
    rows, width = cotangent.shape
    slots = weight.shape[0]
    return call(
        closing_kernel,
        "closing",
        (mine, pair, tokens, cotangent, combine, logits, weight),
        [IN_VMEM] * 7,
        [IN_HBM] * 2,
        [jax.ShapeDtypeStruct((rows, width), LOW)] * 2,
        [
            pltpu.VMEM((slots, width), LOW),
            pltpu.VMEM((slots, width), LOW),
            pltpu.VMEM((8, slots), WIDE),
            pltpu.VMEM((rows, width), LOW),
            pltpu.VMEM((rows, width), LOW),
            pltpu.SemaphoreType.DMA((2, STEPS)),
        ],
    )


def shards(tokens, slot_weight, w_in, w_out, cotangent):
    torus = ("x", "z", "exp")
    swap = [(0, 1), (1, 0)]
    at = jnp.stack([lax.axis_index("exp"), lax.axis_index("core")]).astype(jnp.int32)
    peers = lax.axis_size(torus)
    given, shifted, pieces, columns, weight, rows, cot = opening(
        at, tokens, slot_weight, cotangent
    )
    taken = lax.ppermute(given, "core", swap)
    given_grad, kept_combine = grads_of(columns, cot)
    taken_grad = lax.ppermute(given_grad, "core", swap)
    logits, combine = combining(rows, weight)
    sent, kept_grad = merge_slots(shifted, pieces, kept_combine, rows, cot, taken, peers)
    sent = merge_grads(sent, kept_grad, taken_grad)
    got = lax.all_to_all(sent, torus, split_axis=0, concat_axis=0, tiled=True)
    told = expert(got, w_in, w_out)
    told = lax.all_to_all(told, torus, split_axis=0, concat_axis=0, tiled=True)
    pair = lax.ppermute(told, "core", swap)
    return tuple(closing(told, pair, rows, cot, combine, logits, weight))


def solution(mesh):
    exp = mesh.devices.shape[1]
    finer = Mesh(mesh.devices.reshape(4, 4, 2, exp), ("x", "z", "core", "exp"))
    every = ("x", "z", "core", "exp")
    rows = P(every, None)
    experts = P(every, None, None)
    return jax.shard_map(
        shards,
        mesh=finer,
        in_specs=(P(("x", "z", "core"), None), P(), experts, experts, rows),
        out_specs=(rows, rows),
        check_vma=False,
    )
```

```python
import functools

import jax
import jax.numpy as jnp
from jax import lax
from jax.experimental import pallas as pl
from jax.experimental.pallas import tpu as pltpu
from jax.sharding import Mesh
from jax.sharding import PartitionSpec as P

LOW = jnp.bfloat16
WIDE = jnp.float32
EXTRA = 128
LIMIT = 20 * 1024 * 1024


def product(left, right, left_dim, right_dim):
    return lax.dot_general(
        left, right, (((left_dim,), (right_dim,)), ((), ())), preferred_element_type=WIDE
    )


def split3(value):
    high = value.astype(LOW).astype(WIDE)
    rest = value - high
    mid = rest.astype(LOW).astype(WIDE)
    return [high, mid, rest - mid]


def place(pieces, shape, axis):
    index = lax.broadcasted_iota(jnp.int32, shape, axis)
    total = jnp.zeros(shape, WIDE)
    for at, piece in enumerate(pieces):
        total = jnp.where(index == at, piece, total)
    return total


def lanes(block, first):
    index = lax.broadcasted_iota(jnp.int32, block.shape, 1)
    inside = (index >= first) & (index < first + 3)
    return jnp.sum(jnp.where(inside, block, 0.0), axis=1, keepdims=True)


IN_SMEM = pl.BlockSpec(memory_space=pltpu.SMEM)
IN_VMEM = pl.BlockSpec(memory_space=pltpu.VMEM)
IN_HBM = pl.BlockSpec(memory_space=pltpu.HBM)


def stay(array):
    return pltpu.with_memory_space_constraint(array, pltpu.HBM)


SPAN = pl.CostEstimate(flops=9_000_000_000, bytes_accessed=20_000_000, transcendentals=0)


def call(kernel, name, args, specs, out_specs, out_shape, scratch=(), cost=None):
    return pl.pallas_call(
        kernel,
        in_specs=specs,
        out_specs=out_specs,
        out_shape=out_shape,
        scratch_shapes=scratch,
        compiler_params=pltpu.CompilerParams(vmem_limit_bytes=LIMIT),
        cost_estimate=cost,
        name=name,
    )(*args)


def ordering(core, slots):
    to = lax.broadcasted_iota(jnp.int32, (slots, 1), 0)
    source = lax.broadcasted_iota(jnp.int32, (slots, slots), 1)
    half = slots // 2
    within = to % half
    other = jnp.where(to // half == 0, core, 1 - core)
    wanted = (within // 8) * 16 + other * 8 + within % 8
    return (source == wanted).astype(WIDE).astype(LOW)


def opening_kernel(
    at_ref, tok_hbm, weight_hbm, cot_hbm,
    given_ref, shift_ref, piece_ref, logit_ref, order_ref, rows_ref, cot_ref,
    weight_ref, sems,
):
    slots = weight_ref.shape[1]
    count, width = rows_ref.shape
    start = pl.multiple_of(at_ref[0] * count, count)
    block = count // 4
    parts = [pl.ds(at * block, block) for at in range(4)]
    loads = [pltpu.make_async_copy(weight_hbm, weight_ref, sems.at[0])]
    for at, part in enumerate(parts):
        source = tok_hbm.at[pl.ds(start + at * block, block)]
        loads.append(pltpu.make_async_copy(source, rows_ref.at[part], sems.at[1 + at]))
    loads.append(pltpu.make_async_copy(cot_hbm, cot_ref, sems.at[5]))
    for copy in loads[:5]:
        copy.start()
    order = ordering(at_ref[1], slots)
    loads[0].wait()
    loads[5].start()
    weight = product(order, weight_ref[...], 1, 1).astype(LOW)
    order_ref[...] = weight
    for copy in loads[1:5]:
        copy.wait()
    rows = rows_ref[...]
    logits = product(weight, rows, 1, 1)
    logit_ref[...] = logits
    slot_max = jnp.max(logits, axis=1, keepdims=True)
    shifted = jnp.exp(logits - slot_max)
    slot_sum = jnp.sum(shifted, axis=1, keepdims=True)
    half = slots // 2
    shifted = shifted.astype(LOW)
    given_ref[:, :width] = product(shifted[half:], rows, 1, 0).astype(LOW)
    shift_ref[...] = shifted[:half]
    pieces = place(split3(slot_max) + split3(slot_sum), (slots, EXTRA), 1)
    given_ref[:, width:] = pieces[half:].astype(LOW)
    piece_ref[...] = pieces[:half]
    loads[5].wait()


def opening(at, tokens, slot_weight, cotangent):
    rows, width = cotangent.shape
    slots = slot_weight.shape[1]
    half = slots // 2
    shapes = [((half, width + EXTRA), LOW), ((half, rows), LOW), ((half, EXTRA), WIDE)]
    shapes += [((slots, rows), WIDE), ((slots, width), LOW)] + [((rows, width), LOW)] * 2
    return call(
        opening_kernel,
        "opening",
        (at, stay(tokens), stay(slot_weight), stay(cotangent)),
        [IN_SMEM] + [IN_HBM] * 3,
        [IN_VMEM] * len(shapes),
        [jax.ShapeDtypeStruct(*shape) for shape in shapes],
        [pltpu.VMEM((width, slots), LOW), pltpu.SemaphoreType.DMA((6,))],
    )


def grads_kernel(logit_ref, cot_ref, given_ref, comb_ref):
    logits = logit_ref[...]
    raised = jnp.exp(logits - jnp.max(logits, axis=0, keepdims=True))
    combine = (raised * (1.0 / jnp.sum(raised, axis=0, keepdims=True))).astype(LOW)
    half = given_ref.shape[0]
    given_ref[...] = product(combine[half:], cot_ref[...], 1, 0).astype(LOW)
    comb_ref[...] = combine[:half]


SIDE = pl.CostEstimate(flops=1_000_000_000, bytes_accessed=4_000_000, transcendentals=131_072)


def grads_of(logits, cotangent):
    half, rows = logits.shape[0] // 2, logits.shape[1]
    shapes = [jax.ShapeDtypeStruct((half, wide), LOW) for wide in (cotangent.shape[1], rows)]
    args = (logits, cotangent)
    return call(grads_kernel, "grads", args, [IN_VMEM] * 2, [IN_VMEM] * 2, shapes, (), SIDE)


def combine_kernel(rows_ref, order_ref, logit_ref, comb_ref):
    logits = product(rows_ref[...], order_ref[...], 1, 1)
    logit_ref[...] = logits
    raised = jnp.exp(logits - jnp.max(logits, axis=1, keepdims=True))
    comb_ref[...] = raised * (1.0 / jnp.sum(raised, axis=1, keepdims=True))


def combining(rows, order):
    shape = jax.ShapeDtypeStruct((rows.shape[0], order.shape[0]), WIDE)
    args = (rows, order)
    return call(
        combine_kernel, "combining", args, [IN_VMEM] * 2, [IN_VMEM] * 2, [shape] * 2, (), SIDE
    )


def merge_slots_kernel(
    shift_ref, piece_ref, comb_ref, rows_ref, cot_ref, taken_ref, out_ref, grad_ref
):
    peers, own, wide = out_ref.shape
    width = rows_ref.shape[1]
    kept, taken = piece_ref[...], taken_ref[:, width:].astype(WIDE)
    kept_max, taken_max = lanes(kept, 0), lanes(taken, 0)
    top = jnp.maximum(kept_max, taken_max)
    kept_scale, taken_scale = jnp.exp(kept_max - top), jnp.exp(taken_max - top)
    total = kept_scale * lanes(kept, 3) + taken_scale * lanes(taken, 3)
    slots = kept_scale * product(shift_ref[...], rows_ref[...], 1, 0)
    slots += taken_scale * taken_ref[:, :width].astype(WIDE)
    pieces = place(split3(top) + split3(total), kept.shape, 1)
    out_ref[:, :, :width] = slots.astype(LOW).reshape(peers, own, width)
    out_ref[:, :, wide - EXTRA :] = pieces.astype(LOW).reshape(peers, own, EXTRA)
    grad_ref[...] = product(comb_ref[...], cot_ref[...], 1, 0)


def merge_grads_kernel(sent_ref, kept_ref, taken_ref, out_ref):
    peers, own = out_ref.shape[:2]
    width = kept_ref.shape[1]
    grads = kept_ref[...] + taken_ref[...].astype(WIDE)
    out_ref[:, :, width : 2 * width] = grads.astype(LOW).reshape(peers, own, width)


def merge_slots(shifted, pieces, combine, rows, cotangent, taken, peers):
    half, width = shifted.shape[0], rows.shape[1]
    args = (shifted, pieces, combine, rows, cotangent, taken)
    shapes = [
        jax.ShapeDtypeStruct((peers, half // peers, taken.shape[1] + width), LOW),
        jax.ShapeDtypeStruct((half, width), WIDE),
    ]
    return call(
        merge_slots_kernel, "merge_slots", args, [IN_VMEM] * 6, [IN_VMEM] * 2, shapes, (), SIDE
    )


def merge_grads(sent, kept, taken):
    return pl.pallas_call(
        merge_grads_kernel,
        in_specs=[IN_VMEM] * 3,
        out_specs=IN_VMEM,
        out_shape=jax.ShapeDtypeStruct(sent.shape, LOW),
        input_output_aliases={0: 0},
        compiler_params=pltpu.CompilerParams(vmem_limit_bytes=LIMIT),
        cost_estimate=SPAN,
        name="merge_grads",
    )(sent, kept, taken)


PART = 512


def expert_kernel(got_ref, in_ref, out_ref, told_ref):
    peers, own, wide = got_ref.shape
    count, width = peers * own, in_ref.shape[1]
    got = got_ref[...].reshape(count, wide)
    pieces = got[:, 2 * width :].astype(WIDE)
    block_max, block_sum = lanes(pieces, 0), lanes(pieces, 3)
    odd = lax.broadcasted_iota(jnp.int32, (count, 1), 0) % 2 == 1
    lowest = jnp.full((count, 1), -jnp.inf, WIDE)
    top = [
        jnp.max(jnp.where(odd, lowest, block_max), axis=0, keepdims=True),
        jnp.max(jnp.where(odd, block_max, lowest), axis=0, keepdims=True),
    ]
    scale = jnp.exp(block_max - jnp.where(odd, top[1], top[0]))
    scaled_sum = scale * block_sum
    totals = [
        jnp.sum(jnp.where(odd, 0.0, scaled_sum), axis=0, keepdims=True),
        jnp.sum(jnp.where(odd, scaled_sum, 0.0), axis=0, keepdims=True),
    ]
    high = scale.astype(LOW).astype(WIDE)
    rest, ones = scale - high, jnp.ones_like(scale)
    columns = []
    for column in (high, rest, ones):
        columns += [jnp.where(odd, 0.0, column), jnp.where(odd, column, 0.0)]
    picks = place(columns, (count, EXTRA), 1).T[:8].astype(LOW)
    sums = product(picks, got[:, : 2 * width], 1, 0)
    sums_of = lambda row, part: sums[row : row + 1, part]
    front, back = slice(0, width), slice(width, 2 * width)
    exact = [(sums_of(row, front) + sums_of(row + 2, front)) / totals[row] for row in range(2)]
    exact = place(exact, (8, width), 0)
    out_grad = place([sums_of(4, back), sums_of(5, back)], (8, width), 0).astype(LOW)
    slot_low = exact.astype(LOW)
    rate = 0.7978845608028654
    slot_out = jnp.zeros((8, width), WIDE)
    in_grad = jnp.zeros((8, width), WIDE)
    for first in range(0, in_ref.shape[2], PART):
        part = slice(first, first + PART)
        preact = product(slot_low, in_ref[0, :, part], 1, 0)
        hid_grad = product(out_grad, out_ref[0, part, :], 1, 1)
        square = preact * preact
        curve = jnp.tanh(rate * (preact + 0.044715 * square * preact))
        low_hidden = (0.5 * preact * (1.0 + curve)).astype(LOW)
        slope = 0.5 * (1.0 + curve) + 0.5 * preact * (1.0 - curve * curve) * rate * (
            1.0 + 3.0 * 0.044715 * square
        )
        slot_out += product(low_hidden, out_ref[0, part, :], 1, 0)
        in_grad += product((slope * hid_grad).astype(LOW), in_ref[0, :, part], 1, 1)
    slot_product = jnp.sum(exact * in_grad, axis=1, keepdims=True)
    top = place(top, (8, 1), 0)
    totals = place(totals, (8, 1), 0)
    scalars = place(split3(slot_product) + split3(top) + split3(totals), (8, EXTRA), 1)
    spread = lambda block: jnp.broadcast_to(
        block[:own].astype(LOW)[None], (peers, own, block.shape[1])
    )
    told_ref[:, :, :width] = spread(slot_out)
    told_ref[:, :, width : 2 * width] = spread(in_grad)
    told_ref[:, :, 2 * width :] = spread(scalars)


def expert(got, w_in, w_out):
    shape = jax.ShapeDtypeStruct(got.shape, LOW)
    return call(expert_kernel, "expert", (got, w_in, w_out), [IN_VMEM] * 3, IN_VMEM, shape)


STEPS = 2


def closing_kernel(
    mine_ref, pair_ref, tok_ref, cot_ref, comb_ref, logit_ref, order_ref,
    mixed_hbm, grad_hbm,
    all_out, in_low, rows_ref, mixed_ref, grad_ref, out_sems,
):
    count, width = cot_ref.shape
    half = mine_ref.shape[0] * mine_ref.shape[1]
    block = count // STEPS
    for at, ref in enumerate((mine_ref, pair_ref)):
        part = slice(at * half, (at + 1) * half)
        all_out[part, :] = ref[:, :, :width].reshape(half, width)
        in_low[part, :] = ref[:, :, width : 2 * width].reshape(half, width)
        pieces = ref[:, :, 2 * width :].reshape(half, EXTRA).astype(WIDE).T
        for row in range(3):
            rows_ref[row : row + 1, part] = jnp.sum(
                pieces[3 * row : 3 * row + 3], axis=0, keepdims=True
            )
    slot_product, highest, scale = rows_ref[0:1], rows_ref[1:2], 1.0 / rows_ref[2:3]
    stores = []
    for step in range(STEPS):
        part = pl.ds(step * block, block)
        stores.append(
            pltpu.make_async_copy(mixed_ref.at[part], mixed_hbm.at[part], out_sems.at[0, step])
        )
        stores.append(
            pltpu.make_async_copy(grad_ref.at[part], grad_hbm.at[part], out_sems.at[1, step])
        )
        combine = comb_ref[part]
        mixed_ref[part, :] = product(combine.astype(LOW), all_out[...], 1, 0).astype(LOW)
        stores[-2].start()
        comb_grad = product(cot_ref[part], all_out[...], 1, 1)
        logit_grad = combine * (comb_grad - jnp.sum(combine * comb_grad, axis=1, keepdims=True))
        dispatch = jnp.exp(logit_ref[part] - highest) * scale
        logit_grad += dispatch * (product(tok_ref[part], in_low[...], 1, 1) - slot_product)
        token_grad = product(logit_grad.astype(LOW), order_ref[...], 1, 0)
        token_grad += product(dispatch.astype(LOW), in_low[...], 1, 0)
        grad_ref[part, :] = token_grad.astype(LOW)
        stores[-1].start()
    for copy in stores:
        copy.wait()


def closing(mine, pair, tokens, cotangent, combine, logits, weight):
    rows, width = cotangent.shape
    slots = weight.shape[0]
    return call(
        closing_kernel,
        "closing",
        (mine, pair, tokens, cotangent, combine, logits, weight),
        [IN_VMEM] * 7,
        [IN_HBM] * 2,
        [jax.ShapeDtypeStruct((rows, width), LOW)] * 2,
        [
            pltpu.VMEM((slots, width), LOW),
            pltpu.VMEM((slots, width), LOW),
            pltpu.VMEM((8, slots), WIDE),
            pltpu.VMEM((rows, width), LOW),
            pltpu.VMEM((rows, width), LOW),
            pltpu.SemaphoreType.DMA((2, STEPS)),
        ],
    )


def shards(tokens, slot_weight, w_in, w_out, cotangent):
    torus = ("x", "z", "exp")
    swap = [(0, 1), (1, 0)]
    at = jnp.stack([lax.axis_index("exp"), lax.axis_index("core")]).astype(jnp.int32)
    peers = lax.axis_size(torus)
    given, shifted, pieces, columns, weight, rows, cot = opening(
        at, tokens, slot_weight, cotangent
    )
    taken = lax.ppermute(given, "core", swap)
    given_grad, kept_combine = grads_of(columns, cot)
    taken_grad = lax.ppermute(given_grad, "core", swap)
    logits, combine = combining(rows, weight)
    sent, kept_grad = merge_slots(shifted, pieces, kept_combine, rows, cot, taken, peers)
    sent = merge_grads(sent, kept_grad, taken_grad)
    got = lax.all_to_all(sent, torus, split_axis=0, concat_axis=0, tiled=True)
    told = expert(got, w_in, w_out)
    told = lax.all_to_all(told, torus, split_axis=0, concat_axis=0, tiled=True)
    pair = lax.ppermute(told, "core", swap)
    return tuple(closing(told, pair, rows, cot, combine, logits, weight))


def solution(mesh):
    exp = mesh.devices.shape[1]
    finer = Mesh(mesh.devices.reshape(4, 4, 2, exp), ("x", "z", "core", "exp"))
    every = ("x", "z", "core", "exp")
    rows = P(every, None)
    experts = P(every, None, None)
    return jax.shard_map(
        shards,
        mesh=finer,
        in_specs=(P(("x", "z", "core"), None), P(), experts, experts, rows),
        out_specs=(rows, rows),
        check_vma=False,
    )
```

```python
import functools

import jax
import jax.numpy as jnp
from jax import lax
from jax.experimental import pallas as pl
from jax.experimental.pallas import tpu as pltpu
from jax.sharding import Mesh
from jax.sharding import PartitionSpec as P

LOW = jnp.bfloat16
WIDE = jnp.float32
EXTRA = 128
LIMIT = 20 * 1024 * 1024


def product(left, right, left_dim, right_dim):
    return lax.dot_general(
        left, right, (((left_dim,), (right_dim,)), ((), ())), preferred_element_type=WIDE
    )


def split3(value):
    high = value.astype(LOW).astype(WIDE)
    rest = value - high
    mid = rest.astype(LOW).astype(WIDE)
    return [high, mid, rest - mid]


def place(pieces, shape, axis):
    index = lax.broadcasted_iota(jnp.int32, shape, axis)
    total = jnp.zeros(shape, WIDE)
    for at, piece in enumerate(pieces):
        total = jnp.where(index == at, piece, total)
    return total


def lanes(block, first):
    index = lax.broadcasted_iota(jnp.int32, block.shape, 1)
    inside = (index >= first) & (index < first + 3)
    return jnp.sum(jnp.where(inside, block, 0.0), axis=1, keepdims=True)


IN_SMEM = pl.BlockSpec(memory_space=pltpu.SMEM)
IN_VMEM = pl.BlockSpec(memory_space=pltpu.VMEM)
IN_HBM = pl.BlockSpec(memory_space=pltpu.HBM)


def stay(array):
    return pltpu.with_memory_space_constraint(array, pltpu.HBM)


SPAN = pl.CostEstimate(flops=9_000_000_000, bytes_accessed=20_000_000, transcendentals=0)


def call(kernel, name, args, specs, out_specs, out_shape, scratch=(), cost=None):
    return pl.pallas_call(
        kernel,
        in_specs=specs,
        out_specs=out_specs,
        out_shape=out_shape,
        scratch_shapes=scratch,
        compiler_params=pltpu.CompilerParams(vmem_limit_bytes=LIMIT),
        cost_estimate=cost,
        name=name,
    )(*args)


def ordering(core, slots):
    to = lax.broadcasted_iota(jnp.int32, (slots, 1), 0)
    source = lax.broadcasted_iota(jnp.int32, (slots, slots), 1)
    half = slots // 2
    within = to % half
    other = jnp.where(to // half == 0, core, 1 - core)
    wanted = (within // 8) * 16 + other * 8 + within % 8
    return (source == wanted).astype(WIDE).astype(LOW)


def opening_kernel(
    at_ref, tok_hbm, weight_hbm, cot_hbm,
    given_ref, shift_ref, piece_ref, logit_ref, order_ref, rows_ref, cot_ref,
    weight_ref, sems,
):
    slots = weight_ref.shape[1]
    count, width = rows_ref.shape
    start = pl.multiple_of(at_ref[0] * count, count)
    block = count // 4
    parts = [pl.ds(at * block, block) for at in range(4)]
    loads = [pltpu.make_async_copy(weight_hbm, weight_ref, sems.at[0])]
    for at, part in enumerate(parts):
        source = tok_hbm.at[pl.ds(start + at * block, block)]
        loads.append(pltpu.make_async_copy(source, rows_ref.at[part], sems.at[1 + at]))
    loads.append(pltpu.make_async_copy(cot_hbm, cot_ref, sems.at[5]))
    for copy in loads[:5]:
        copy.start()
    order = ordering(at_ref[1], slots)
    loads[0].wait()
    loads[5].start()
    weight = product(order, weight_ref[...], 1, 1).astype(LOW)
    order_ref[...] = weight
    for copy in loads[1:5]:
        copy.wait()
    rows = rows_ref[...]
    logits = product(weight, rows, 1, 1)
    logit_ref[...] = logits
    slot_max = jnp.max(logits, axis=1, keepdims=True)
    shifted = jnp.exp(logits - slot_max)
    slot_sum = jnp.sum(shifted, axis=1, keepdims=True)
    half = slots // 2
    shifted = shifted.astype(LOW)
    given_ref[:, :width] = product(shifted[half:], rows, 1, 0).astype(LOW)
    shift_ref[...] = shifted[:half]
    pieces = place(split3(slot_max) + split3(slot_sum), (slots, EXTRA), 1)
    given_ref[:, width:] = pieces[half:].astype(LOW)
    piece_ref[...] = pieces[:half]
    loads[5].wait()


def opening(at, tokens, slot_weight, cotangent):
    rows, width = cotangent.shape
    slots = slot_weight.shape[1]
    half = slots // 2
    shapes = [((half, width + EXTRA), LOW), ((half, rows), LOW), ((half, EXTRA), WIDE)]
    shapes += [((slots, rows), WIDE), ((slots, width), LOW)] + [((rows, width), LOW)] * 2
    return call(
        opening_kernel,
        "opening",
        (at, stay(tokens), stay(slot_weight), stay(cotangent)),
        [IN_SMEM] + [IN_HBM] * 3,
        [IN_VMEM] * len(shapes),
        [jax.ShapeDtypeStruct(*shape) for shape in shapes],
        [pltpu.VMEM((width, slots), LOW), pltpu.SemaphoreType.DMA((6,))],
    )


def grads_kernel(logit_ref, cot_ref, given_ref, comb_ref):
    logits = logit_ref[...]
    raised = jnp.exp(logits - jnp.max(logits, axis=0, keepdims=True))
    combine = (raised * (1.0 / jnp.sum(raised, axis=0, keepdims=True))).astype(LOW)
    half = given_ref.shape[0]
    given_ref[...] = product(combine[half:], cot_ref[...], 1, 0).astype(LOW)
    comb_ref[...] = combine[:half]


SIDE = pl.CostEstimate(flops=1_000_000_000, bytes_accessed=4_000_000, transcendentals=131_072)


def grads_of(logits, cotangent):
    half, rows = logits.shape[0] // 2, logits.shape[1]
    shapes = [jax.ShapeDtypeStruct((half, wide), LOW) for wide in (cotangent.shape[1], rows)]
    args = (logits, cotangent)
    return call(grads_kernel, "grads", args, [IN_VMEM] * 2, [IN_VMEM] * 2, shapes, (), SIDE)


def combine_kernel(rows_ref, order_ref, logit_ref, comb_ref):
    logits = product(rows_ref[...], order_ref[...], 1, 1)
    logit_ref[...] = logits
    raised = jnp.exp(logits - jnp.max(logits, axis=1, keepdims=True))
    comb_ref[...] = raised * (1.0 / jnp.sum(raised, axis=1, keepdims=True))


def combining(rows, order):
    shape = jax.ShapeDtypeStruct((rows.shape[0], order.shape[0]), WIDE)
    args = (rows, order)
    return call(
        combine_kernel, "combining", args, [IN_VMEM] * 2, [IN_VMEM] * 2, [shape] * 2, (), SIDE
    )


def kept_kernel(shift_ref, comb_ref, rows_ref, cot_ref, slot_ref, grad_ref):
    slot_ref[...] = product(shift_ref[...], rows_ref[...], 1, 0)
    grad_ref[...] = product(comb_ref[...], cot_ref[...], 1, 0)


def kept_sums(shifted, combine, rows, cotangent):
    shape = jax.ShapeDtypeStruct((shifted.shape[0], rows.shape[1]), WIDE)
    args = (shifted, combine, rows, cotangent)
    return call(kept_kernel, "kept", args, [IN_VMEM] * 4, [IN_VMEM] * 2, [shape] * 2, (), SIDE)


def merge_slots_kernel(kept_ref, piece_ref, taken_ref, out_ref):
    peers, own, wide = out_ref.shape
    width = kept_ref.shape[1]
    kept, taken = piece_ref[...], taken_ref[:, width:].astype(WIDE)
    kept_max, taken_max = lanes(kept, 0), lanes(taken, 0)
    top = jnp.maximum(kept_max, taken_max)
    kept_scale, taken_scale = jnp.exp(kept_max - top), jnp.exp(taken_max - top)
    total = kept_scale * lanes(kept, 3) + taken_scale * lanes(taken, 3)
    slots = kept_scale * kept_ref[...] + taken_scale * taken_ref[:, :width].astype(WIDE)
    pieces = place(split3(top) + split3(total), kept.shape, 1)
    out_ref[:, :, :width] = slots.astype(LOW).reshape(peers, own, width)
    out_ref[:, :, wide - EXTRA :] = pieces.astype(LOW).reshape(peers, own, EXTRA)


def merge_grads_kernel(sent_ref, kept_ref, taken_ref, out_ref):
    peers, own = out_ref.shape[:2]
    width = kept_ref.shape[1]
    grads = kept_ref[...] + taken_ref[...].astype(WIDE)
    out_ref[:, :, width : 2 * width] = grads.astype(LOW).reshape(peers, own, width)


def merge_slots(kept, pieces, taken, peers):
    half, width = kept.shape
    shape = jax.ShapeDtypeStruct((peers, half // peers, taken.shape[1] + width), LOW)
    args = (kept, pieces, taken)
    return call(merge_slots_kernel, "merge_slots", args, [IN_VMEM] * 3, IN_VMEM, shape, (), SIDE)


def merge_grads(sent, kept, taken):
    return pl.pallas_call(
        merge_grads_kernel,
        in_specs=[IN_VMEM] * 3,
        out_specs=IN_VMEM,
        out_shape=jax.ShapeDtypeStruct(sent.shape, LOW),
        input_output_aliases={0: 0},
        compiler_params=pltpu.CompilerParams(vmem_limit_bytes=LIMIT),
        cost_estimate=SPAN,
        name="merge_grads",
    )(sent, kept, taken)


PART = 512


def expert_kernel(got_ref, in_ref, out_ref, told_ref):
    peers, own, wide = got_ref.shape
    count, width = peers * own, in_ref.shape[1]
    got = got_ref[...].reshape(count, wide)
    pieces = got[:, 2 * width :].astype(WIDE)
    block_max, block_sum = lanes(pieces, 0), lanes(pieces, 3)
    odd = lax.broadcasted_iota(jnp.int32, (count, 1), 0) % 2 == 1
    lowest = jnp.full((count, 1), -jnp.inf, WIDE)
    top = [
        jnp.max(jnp.where(odd, lowest, block_max), axis=0, keepdims=True),
        jnp.max(jnp.where(odd, block_max, lowest), axis=0, keepdims=True),
    ]
    scale = jnp.exp(block_max - jnp.where(odd, top[1], top[0]))
    scaled_sum = scale * block_sum
    totals = [
        jnp.sum(jnp.where(odd, 0.0, scaled_sum), axis=0, keepdims=True),
        jnp.sum(jnp.where(odd, scaled_sum, 0.0), axis=0, keepdims=True),
    ]
    high = scale.astype(LOW).astype(WIDE)
    rest, ones = scale - high, jnp.ones_like(scale)
    columns = []
    for column in (high, rest, ones):
        columns += [jnp.where(odd, 0.0, column), jnp.where(odd, column, 0.0)]
    picks = place(columns, (count, EXTRA), 1).T[:8].astype(LOW)
    sums = product(picks, got[:, : 2 * width], 1, 0)
    sums_of = lambda row, part: sums[row : row + 1, part]
    front, back = slice(0, width), slice(width, 2 * width)
    exact = [(sums_of(row, front) + sums_of(row + 2, front)) / totals[row] for row in range(2)]
    exact = place(exact, (8, width), 0)
    out_grad = place([sums_of(4, back), sums_of(5, back)], (8, width), 0).astype(LOW)
    slot_low = exact.astype(LOW)
    rate = 0.7978845608028654
    slot_out = jnp.zeros((8, width), WIDE)
    in_grad = jnp.zeros((8, width), WIDE)
    for first in range(0, in_ref.shape[2], PART):
        part = slice(first, first + PART)
        preact = product(slot_low, in_ref[0, :, part], 1, 0)
        hid_grad = product(out_grad, out_ref[0, part, :], 1, 1)
        square = preact * preact
        curve = jnp.tanh(rate * (preact + 0.044715 * square * preact))
        low_hidden = (0.5 * preact * (1.0 + curve)).astype(LOW)
        slope = 0.5 * (1.0 + curve) + 0.5 * preact * (1.0 - curve * curve) * rate * (
            1.0 + 3.0 * 0.044715 * square
        )
        slot_out += product(low_hidden, out_ref[0, part, :], 1, 0)
        in_grad += product((slope * hid_grad).astype(LOW), in_ref[0, :, part], 1, 1)
    slot_product = jnp.sum(exact * in_grad, axis=1, keepdims=True)
    top = place(top, (8, 1), 0)
    totals = place(totals, (8, 1), 0)
    scalars = place(split3(slot_product) + split3(top) + split3(totals), (8, EXTRA), 1)
    spread = lambda block: jnp.broadcast_to(
        block[:own].astype(LOW)[None], (peers, own, block.shape[1])
    )
    told_ref[:, :, :width] = spread(slot_out)
    told_ref[:, :, width : 2 * width] = spread(in_grad)
    told_ref[:, :, 2 * width :] = spread(scalars)


def expert(got, w_in, w_out):
    shape = jax.ShapeDtypeStruct(got.shape, LOW)
    return call(expert_kernel, "expert", (got, w_in, w_out), [IN_VMEM] * 3, IN_VMEM, shape)


STEPS = 2


def closing_kernel(
    mine_ref, pair_ref, tok_ref, cot_ref, comb_ref, logit_ref, order_ref,
    mixed_hbm, grad_hbm,
    all_out, in_low, rows_ref, mixed_ref, grad_ref, out_sems,
):
    count, width = cot_ref.shape
    half = mine_ref.shape[0] * mine_ref.shape[1]
    block = count // STEPS
    for at, ref in enumerate((mine_ref, pair_ref)):
        part = slice(at * half, (at + 1) * half)
        all_out[part, :] = ref[:, :, :width].reshape(half, width)
        in_low[part, :] = ref[:, :, width : 2 * width].reshape(half, width)
        pieces = ref[:, :, 2 * width :].reshape(half, EXTRA).astype(WIDE).T
        for row in range(3):
            rows_ref[row : row + 1, part] = jnp.sum(
                pieces[3 * row : 3 * row + 3], axis=0, keepdims=True
            )
    slot_product, highest, scale = rows_ref[0:1], rows_ref[1:2], 1.0 / rows_ref[2:3]
    stores = []
    for step in range(STEPS):
        part = pl.ds(step * block, block)
        stores.append(
            pltpu.make_async_copy(mixed_ref.at[part], mixed_hbm.at[part], out_sems.at[0, step])
        )
        stores.append(
            pltpu.make_async_copy(grad_ref.at[part], grad_hbm.at[part], out_sems.at[1, step])
        )
        combine = comb_ref[part]
        mixed_ref[part, :] = product(combine.astype(LOW), all_out[...], 1, 0).astype(LOW)
        stores[-2].start()
        comb_grad = product(cot_ref[part], all_out[...], 1, 1)
        logit_grad = combine * (comb_grad - jnp.sum(combine * comb_grad, axis=1, keepdims=True))
        dispatch = jnp.exp(logit_ref[part] - highest) * scale
        logit_grad += dispatch * (product(tok_ref[part], in_low[...], 1, 1) - slot_product)
        token_grad = product(logit_grad.astype(LOW), order_ref[...], 1, 0)
        token_grad += product(dispatch.astype(LOW), in_low[...], 1, 0)
        grad_ref[part, :] = token_grad.astype(LOW)
        stores[-1].start()
    for copy in stores:
        copy.wait()


def closing(mine, pair, tokens, cotangent, combine, logits, weight):
    rows, width = cotangent.shape
    slots = weight.shape[0]
    return call(
        closing_kernel,
        "closing",
        (mine, pair, tokens, cotangent, combine, logits, weight),
        [IN_VMEM] * 7,
        [IN_HBM] * 2,
        [jax.ShapeDtypeStruct((rows, width), LOW)] * 2,
        [
            pltpu.VMEM((slots, width), LOW),
            pltpu.VMEM((slots, width), LOW),
            pltpu.VMEM((8, slots), WIDE),
            pltpu.VMEM((rows, width), LOW),
            pltpu.VMEM((rows, width), LOW),
            pltpu.SemaphoreType.DMA((2, STEPS)),
        ],
    )


def shards(tokens, slot_weight, w_in, w_out, cotangent):
    torus = ("x", "z", "exp")
    swap = [(0, 1), (1, 0)]
    at = jnp.stack([lax.axis_index("exp"), lax.axis_index("core")]).astype(jnp.int32)
    peers = lax.axis_size(torus)
    given, shifted, pieces, columns, weight, rows, cot = opening(
        at, tokens, slot_weight, cotangent
    )
    taken = lax.ppermute(given, "core", swap)
    given_grad, kept_combine = grads_of(columns, cot)
    taken_grad = lax.ppermute(given_grad, "core", swap)
    logits, combine = combining(rows, weight)
    kept, kept_grad = kept_sums(shifted, kept_combine, rows, cot)
    sent = merge_grads(merge_slots(kept, pieces, taken, peers), kept_grad, taken_grad)
    got = lax.all_to_all(sent, torus, split_axis=0, concat_axis=0, tiled=True)
    told = expert(got, w_in, w_out)
    told = lax.all_to_all(told, torus, split_axis=0, concat_axis=0, tiled=True)
    pair = lax.ppermute(told, "core", swap)
    return tuple(closing(told, pair, rows, cot, combine, logits, weight))


def solution(mesh):
    exp = mesh.devices.shape[1]
    finer = Mesh(mesh.devices.reshape(4, 4, 2, exp), ("x", "z", "core", "exp"))
    every = ("x", "z", "core", "exp")
    rows = P(every, None)
    experts = P(every, None, None)
    return jax.shard_map(
        shards,
        mesh=finer,
        in_specs=(P(("x", "z", "core"), None), P(), experts, experts, rows),
        out_specs=(rows, rows),
        check_vma=False,
    )
```
